32 devices in a mesh: rep: 4 (over y, x), exp: 8 (over z, core).
Axes of the slice: x: 2, y: 2, z: 4, core: 2. Of those that a mesh axis runs over, the one named last changes fastest.
Arguments:
- tokens: bfloat16 [8, 1024, 1024], P('exp', 'rep'), may hold values from -6 to 6
- doc_ids: int32 [8, 1024], P('exp'), may hold values from 0 to 3, as said below
- routes: int32 [8, 1024, 1], P('exp', 'rep'), may hold values from 0 to 3; in each aligned block of 256 rows (0 to 255, 256 to 511, ..., all dimensions but the last counted through in order) at most 80 rows name the same one
- norm_gains: bfloat16 [1024, 2], P(('rep', 'exp')), may hold values from 0.5 to 1.5
- norm_biases: bfloat16 [1024, 2], P(('rep', 'exp')), may hold values from -1 to 1
- w_qkv: bfloat16 [1024, 3072], P(('rep', 'exp')), may hold values from -0.1875 to 0.1875
- w_proj: bfloat16 [1024, 1024], P(('rep', 'exp')), may hold values from -1 to 1
- centroids: bfloat16 [1024, 4], P(('rep', 'exp')), may hold values from -0.1875 to 0.1875
- w_in: bfloat16 [8, 2, 1024, 2048], P('exp', None, None, 'rep'), may hold values from -0.1875 to 0.1875
- w_out: bfloat16 [8, 2, 1024, 2048], P('exp', None, None, 'rep'), may hold values from -0.09375 to 0.09375
- grad_out: bfloat16 [8, 1024, 1024], P('exp', 'rep'), may hold values from -6 to 6
Outputs:
- block_out: bfloat16 [8, 1024, 1024], P('exp', 'rep')
- grad_tokens: bfloat16 [8, 1024, 1024], P('exp', 'rep')
- grad_gains: float32 [1024, 2], P(('rep', 'exp'))
- grad_biases: float32 [1024, 2], P(('rep', 'exp'))
- grad_qkv: float32 [1024, 3072], P(('rep', 'exp'))
- grad_proj: float32 [1024, 1024], P(('rep', 'exp'))
- grad_centroids: float32 [1024, 4], P(('rep', 'exp'))
- grad_w_in: float32 [8, 2, 1024, 2048], P('exp', None, None, 'rep')
- grad_w_out: float32 [8, 2, 1024, 2048], P('exp', None, None, 'rep')
The draws below stay inside these ranges and needn't reach their ends.
Inputs may be any that keep to these rules, and one draw needn't show every extreme that they name: `routes`: each token names one expert. In the rows of one device no expert is named by more than 80 rows, and in some device's rows one expert by exactly 80. `doc_ids`: within a sequence document numbers start at 0, never fall and rise by one at each boundary; every sequence has one document that starts within its first 128 positions and ends within its last 128.
All inputs are finite; a program needn't handle non-finite values.
Results may differ from the reference program's by a relative error of at most 0.015.
Values may be sent and summed in bfloat16 or wider, within the bound.
No kernel may reach another device: no remote copies, remote signals or barrier semaphores. Data moves between devices by JAX's collectives and lax.ppermute only.
A program may use at most 256 MiB of HBM per device.

```python
import math
import jax
import jax.numpy as jnp
import numpy as np
from jax import lax

D = 1024
HEAD_DIM = 64
FF = 4096
TOK_DEV = 256
LEN = 1024
SEQS = 8
TOKENS = 8192
EXPERTS = 4
CAP = 80
N_REP = 4
N_EXP = 8


def draw_doc_ids(key, part):
    key = jax.random.fold_in(key, 7)
    key_start, key_early, key_finish = jax.random.split(key, 3)
    start_pos = jax.random.randint(key_start, (SEQS, 1), 2, LEN // 8 + 1)
    early_pos = jax.random.randint(key_early, (SEQS, 1), 1, start_pos)
    finish_pos = jax.random.randint(key_finish, (SEQS, 1), LEN - LEN // 8, LEN)
    position = jnp.arange(LEN, dtype=jnp.int32)[None, :]
    marks = (position >= early_pos).astype(jnp.int32) + (position >= start_pos).astype(jnp.int32)
    return (marks + (position >= finish_pos).astype(jnp.int32)).astype(jnp.int32)


def with_spikes(values, key, source, target, parts, factor):
    def block_of(dim):
        return (jnp.arange(values.shape[dim]) // (values.shape[dim] // parts)).reshape((-1,) + (1,) * (values.ndim - 1 - dim))

    near = jax.random.permutation(key, parts)[block_of(target)]
    far = (block_of(target) + parts // 2) % parts
    return jnp.where((block_of(source) == near) | (block_of(source) == far), factor * values, values)


def levels(stream_key, shape, pieces, smallest, largest):
    factor_of = 1.0
    for dim, blocks in pieces:
        heights = jax.random.uniform(jax.random.fold_in(jax.random.fold_in(stream_key, 6), dim), (blocks,), jnp.float32, smallest / len(pieces), largest / len(pieces))
        factor_of = factor_of * jnp.repeat(jnp.exp(heights), shape[dim] // blocks).reshape((-1,) + (1,) * (len(shape) - 1 - dim))
    return factor_of


def assign_block(own_key, own, number, rows, amount, top, reach, slope):
    order = jax.random.permutation(own_key, amount)
    crowded, common = load_shares(amount, rows * top, reach, slope, True), load_shares(amount, rows * top, reach, slope, False)
    places = jnp.arange(amount)

    def named(sizes, turn):
        used = int((sizes > 0).sum())
        fixed = max(1, used // 4)
        passed = fixed + (places - fixed + turn * (used - fixed)) % max(1, amount - fixed)
        return jnp.zeros((amount,), jnp.int32).at[order[jnp.where(places < fixed, places, passed)]].set(jnp.asarray(sizes, jnp.int32))

    sizes = jnp.where(number % 4 == 0, named(crowded, number // 4), named(common, number - number // 4 - 1))
    mixed = jax.random.permutation(jax.random.fold_in(own, 3), amount)
    donor, receiver = mixed[0:amount // 2 * 2:2], mixed[1:amount // 2 * 2:2]
    room = jnp.minimum(sizes[donor] - 1, reach - sizes[receiver]) // 2
    room = jnp.where((donor == order[0]) | (receiver == order[0]) | (sizes[receiver] == 0), 0, jnp.maximum(room, 0))
    passed = jax.random.randint(jax.random.fold_in(own, 4), (amount // 2,), 0, 1 << 20) % (room + 1)
    sizes = sizes.at[donor].add(-passed).at[receiver].add(passed)
    members = jnp.searchsorted(jnp.cumsum(sizes), jnp.arange(rows * top), side="right").astype(jnp.int32)
    listing = members.reshape(top, rows).T
    listing = listing[jax.random.permutation(jax.random.fold_in(own, 1), rows)]
    turn = jax.random.randint(jax.random.fold_in(own, 2), (rows, 1), 0, top)
    return jnp.take_along_axis(listing, (jnp.arange(top)[None, :] + turn) % top, axis=1)


def load_shares(number_of, total, most, lean, full):
    loads = [(1 << 20) // math.isqrt(standing ** lean) + 1 for standing in range(1, number_of + 1)]
    largest = most if full else min(most, max(-(-total // number_of), total * loads[0] // sum(loads)))
    least = 1 if total - largest >= number_of - 1 else 0
    given, surplus = [largest] + [least] * (number_of - 1), total - largest - least * (number_of - 1)
    while surplus > 0:
        movable = [i for i in range(1, number_of) if given[i] < largest] or [i for i in range(1, number_of) if given[i] < most]
        mass, remaining = sum([loads[i] for i in movable]), surplus
        for i in movable:
            more = min(most - given[i], max(1, remaining * loads[i] // mass), surplus)
            given[i] = given[i] + more
            surplus = surplus - more
    return np.array(given)


def bell_draw(rng, shape, deviation, bound, pieces=(), held_as=jnp.bfloat16):
    loudness = levels(rng, shape, pieces, -0.22, 0.18) if pieces else 1.0
    values = jax.random.normal(rng, shape, jnp.float32) * deviation * loudness
    return jnp.minimum(jnp.maximum(values, -bound), bound).astype(held_as)


def bell_draw_with(key, shape, spread, bound, cuts, heavy, held_as=jnp.bfloat16):
    values = spread * jax.random.normal(key, shape, jnp.float32)
    if cuts:
        values = values * levels(key, shape, cuts, -0.22, 0.18)
    return jnp.clip(with_spikes(values, jax.random.fold_in(key, 3), *heavy), -bound, bound).astype(held_as)


def setup_inputs(seed: int = 0) -> dict:
    key_list = jax.random.split(jax.random.key(seed), 12)
    tokens = bell_draw_with(key_list[0], (SEQS, LEN, D), 1.0, 6.0, ((0, 8), (1, 4)), (0, 2, 8, 2.0))
    doc_ids = draw_doc_ids(jax.random.fold_in(key_list[11], 71), 0)
    routes_keys = jax.random.split(jax.random.fold_in(key_list[2], 1), SEQS * LEN // TOK_DEV)
    routes_turns = jax.random.permutation(jax.random.fold_in(key_list[2], 3), SEQS * LEN // TOK_DEV)
    routes = jax.vmap(lambda own, number: assign_block(jax.random.fold_in(key_list[2], 2), own, number, TOK_DEV, EXPERTS, 1, CAP, 1))(routes_keys, routes_turns).reshape((SEQS, LEN, 1))
    norm_gains = jnp.clip(1.0 + 0.1 * jax.random.normal(key_list[3], (D, 2), jnp.float32), 0.5, 1.5).astype(jnp.bfloat16)
    norm_biases = bell_draw(key_list[4], (D, 2), 0.2, 1.0, ((0, 32),))
    w_qkv = bell_draw(key_list[5], (D, 3 * D), D ** -0.5, 0.1875, ((0, 32),))
    w_proj = bell_draw(key_list[6], (D, D), (D // 32) ** -0.5, 1.0, ((0, 32),))
    centroids = bell_draw(key_list[7], (D, EXPERTS), D ** -0.5, 0.1875, ((0, 32),))
    w_in = bell_draw(key_list[8], (2 * EXPERTS, 2, D, FF // 2), D ** -0.5, 0.1875, ((0, 8), (3, 4)))
    w_out = bell_draw(key_list[9], (2 * EXPERTS, 2, D, FF // 2), FF ** -0.5, 0.09375, ((0, 8), (3, 4)))
    grad_out = bell_draw_with(key_list[10], (SEQS, LEN, D), 1.0, 6.0, ((0, 8), (1, 4)), (0, 2, 8, 2.0))
    return dict(tokens=tokens, doc_ids=doc_ids, routes=routes, norm_gains=norm_gains, norm_biases=norm_biases, w_qkv=w_qkv, w_proj=w_proj, centroids=centroids, w_in=w_in, w_out=w_out, grad_out=grad_out)


eps = 1e-05
neg_fill = -1e+30
highest = lax.Precision.HIGHEST

@jax.custom_vjp
def low(v):
    return lax.optimization_barrier(v.astype(jnp.bfloat16)).astype(jnp.float32)

@jax.custom_vjp
def low_back(v):
    return v

def low_keep(v):
    return (low(v), None)

def low_pass(kept, grad):
    return (grad,)

def back_keep(v):
    return (v, None)

def back_low(kept, grad):
    return (low(grad),)
low.defvjp(low_keep, low_pass)
low_back.defvjp(back_keep, back_low)

def layer_norm(values, gain_vec, shift):
    average = lax.optimization_barrier(jnp.mean(values, axis=-1, keepdims=True))
    centred = values - average
    inverse = lax.rsqrt(lax.optimization_barrier(jnp.mean(centred * centred, axis=-1, keepdims=True)) + eps)
    return centred * inverse * gain_vec + shift

def attend_one(sequence, doc_row, gain_vec, shift, w_qkv, w_proj):
    tok_rows, model_width = sequence.shape
    head_count = model_width // HEAD_DIM
    normed = layer_norm(sequence, gain_vec, shift)
    projected = low_back(low(jnp.dot(low(normed), w_qkv, precision=highest)))
    query = projected[:, :model_width].reshape(tok_rows, head_count, HEAD_DIM)
    keys = projected[:, model_width:2 * model_width].reshape(tok_rows, head_count, HEAD_DIM)
    values = projected[:, 2 * model_width:].reshape(tok_rows, head_count, HEAD_DIM)
    raw = low_back(jnp.einsum('qhd,khd->hqk', query, keys, precision=highest) * HEAD_DIM ** (-0.5))
    position = jnp.arange(tok_rows)
    allowed = (position[None, :] <= position[:, None]) & (doc_row[None, :] == doc_row[:, None])
    probs = jax.nn.softmax(jnp.where(allowed[None], raw, neg_fill), axis=-1)
    mixed = jnp.einsum('hqk,khd->qhd', low(probs), values, precision=highest).reshape(tok_rows, model_width)
    mixed = low_back(low(mixed))
    return sequence + low_back(jnp.dot(mixed, w_proj, precision=highest))

def slot_tables(routes):
    devices = N_REP * N_EXP
    expert = routes.reshape(devices, TOK_DEV)
    onehot = (expert[:, :, None] == jnp.arange(EXPERTS, dtype=jnp.int32)[None, None, :]).astype(jnp.int32)
    slot_rank = lax.optimization_barrier(jnp.sum((jnp.cumsum(onehot, axis=1) - onehot) * onehot, axis=2))
    device = jnp.arange(devices, dtype=jnp.int32)[:, None]
    slot_of = (expert * (devices * CAP) + device * CAP + slot_rank).reshape(-1).astype(jnp.int32)
    slot_owner = jnp.full((EXPERTS * devices * CAP,), TOKENS, jnp.int32)
    slot_owner = slot_owner.at[slot_of].set(jnp.arange(TOKENS, dtype=jnp.int32))
    return (slot_of, slot_owner)

def whole_experts(halves):
    joined = halves.reshape(EXPERTS, 2, 2, D, FF // 2).transpose(0, 2, 3, 1, 4)
    return joined.reshape(EXPERTS, 2, D, FF)

def one_expert(bundle):
    inputs, centroid, expert_in, expert_out = bundle
    stream = inputs
    for sublayer in range(2):
        pre_act = low_back(jnp.dot(low(stream), expert_in[sublayer], precision=highest))
        active = low(jax.nn.gelu(pre_act))
        stream = stream + low_back(jnp.dot(active, expert_out[sublayer].T, precision=highest))
    gating = jax.nn.sigmoid(jnp.dot(inputs, centroid, precision=highest))
    return low(gating[:, None] * stream)

def reference(tokens, doc_ids, routes, norm_gains, norm_biases, w_qkv, w_proj, centroids, w_in, w_out, grad_out):
    slot_of, slot_owner = slot_tables(routes)
    group = min(SEQS, max(1, 2048 // LEN))
    devices = N_REP * N_EXP

    def forward(tokens32, gains, biases, qkv_weight, proj_weight, cents, in_halves, out_halves):
        seq_blocks = tokens32.reshape(SEQS // group, group, LEN, D)
        doc_blocks = doc_ids.reshape(SEQS // group, group, LEN)

        def single(sequence, doc_row):
            return attend_one(sequence, doc_row, gains[:, 0], biases[:, 0], qkv_weight, proj_weight)

        def block_fn(bundle):
            return jax.vmap(single)(bundle[0], bundle[1])
        hidden = lax.map(jax.checkpoint(block_fn), (seq_blocks, doc_blocks)).reshape(TOKENS, D)
        normed_mid = low_back(low(layer_norm(hidden, gains[:, 1], biases[:, 1])))
        padded = jnp.concatenate([normed_mid, jnp.zeros((1, D), jnp.float32)], axis=0)
        grouped = padded[slot_owner].reshape(EXPERTS, devices * CAP, D)
        expert_in = whole_experts(in_halves)
        expert_out = whole_experts(out_halves)
        answers = lax.map(jax.checkpoint(one_expert), (grouped, cents.T, expert_in, expert_out))
        combined = answers.reshape(-1, D)[slot_of]
        return (hidden + combined).reshape(SEQS, LEN, D)
    primal = (tokens.astype(jnp.float32), norm_gains.astype(jnp.float32), norm_biases.astype(jnp.float32), w_qkv.astype(jnp.float32), w_proj.astype(jnp.float32), centroids.astype(jnp.float32), w_in.astype(jnp.float32), w_out.astype(jnp.float32))
    result, pullback = jax.vjp(forward, *primal)
    grads = pullback(grad_out.astype(jnp.float32))
    return (result.astype(jnp.bfloat16), grads[0].astype(jnp.bfloat16), grads[1], grads[2], grads[3], grads[4], grads[5], grads[6], grads[7])
```

```python
import jax
import jax.numpy as jnp
from jax import lax
from jax.sharding import PartitionSpec as P

HEAD_DIM = 64
REPS = 4
eps = 1e-05
neg_fill = -1e30
bf16 = jnp.bfloat16
f32 = jnp.float32


def flip(value, axis, mask):
    pairs = [(source, source ^ mask) for source in range(lax.axis_size(axis))]
    return lax.ppermute(value, axis, pairs)


def over_x(value):
    return flip(value, "rep", 1)


def over_y(value):
    return flip(value, "rep", 2)


def over_diag(value):
    return flip(value, "rep", 3)


def over_core(value):
    return flip(value, "exp", 1)


def shift_z(value, step):
    size = lax.axis_size("exp")
    if step % (size // 2) == 0:
        return value
    pairs = [(source, (source + 2 * step) % size) for source in range(size)]
    return lax.ppermute(value, "exp", pairs)


def gather_plane(first, second):
    first_x, second_y = over_x(first), over_y(second)
    first_y, second_x = over_y(first), over_x(second)
    return (
        [first, first_x, first_y, over_y(first_x)],
        [second, second_x, second_y, over_x(second_y)],
    )


def scatter_plane_x(blocks):
    low = [block.astype(bf16) for block in blocks]
    kept = blocks[0].astype(f32) + over_x(low[1]).astype(f32)
    passed = blocks[2].astype(f32) + over_x(low[3]).astype(f32)
    return kept + over_y(passed.astype(bf16)).astype(f32)


def scatter_plane_y(blocks):
    low = [block.astype(bf16) for block in blocks]
    kept = blocks[0].astype(f32) + over_y(low[2]).astype(f32)
    passed = blocks[1].astype(f32) + over_y(low[3]).astype(f32)
    return kept + over_x(passed.astype(bf16)).astype(f32)


def pick(stacked, index, axis=0):
    return lax.dynamic_index_in_dim(stacked, index, axis=axis, keepdims=False)


def gather_z(block):
    n_z = lax.axis_size("exp") // 2
    own_z = lax.axis_index("exp") // 2
    out = jnp.zeros((n_z,) + block.shape, block.dtype)
    for step in range(n_z):
        out = lax.dynamic_update_index_in_dim(out, shift_z(block, step), (own_z - step) % n_z, 0)
    return out


def scatter_z(blocks):
    n_z = lax.axis_size("exp") // 2
    own_z = lax.axis_index("exp") // 2
    total = pick(blocks, own_z)
    for step in range(1, n_z):
        sent = pick(blocks, (own_z + step) % n_z).astype(bf16)
        total = total + shift_z(sent, step).astype(f32)
    return total


def both_cores(value, parity, axis):
    other = over_core(value)
    return jnp.stack(
        [jnp.where(parity == 0, value, other), jnp.where(parity == 0, other, value)], axis=axis
    )


def layer_norm(values, gain_vec, shift):
    average = jnp.mean(values, axis=-1, keepdims=True)
    centred = values - average
    inverse = lax.rsqrt(jnp.mean(centred * centred, axis=-1, keepdims=True) + eps)
    normed = centred * inverse
    return (normed * gain_vec + shift, normed, inverse)


def norm_back(gradient, normed, inverse, gain_vec):
    scaled = gradient * gain_vec
    bracket = (
        scaled
        - jnp.mean(scaled, axis=-1, keepdims=True)
        - normed * jnp.mean(scaled * normed, axis=-1, keepdims=True)
    )
    return inverse * bracket


def contract_rows(former, latter):
    return lax.dot_general(former, latter, (((0,), (0,)), ((), ())), preferred_element_type=f32)


def contract_last(former, latter):
    return lax.dot_general(former, latter, (((1,), (1,)), ((), ())), preferred_element_type=f32)


def product(former, latter):
    return jnp.dot(former, latter, preferred_element_type=f32)


def local(
    tokens,
    doc_ids,
    routes,
    norm_gains,
    norm_biases,
    w_qkv,
    w_proj,
    centroids,
    w_in,
    w_out,
    grad_out,
):
    rep = lax.axis_index("rep")
    parity = lax.axis_index("exp") % 2
    own_z = lax.axis_index("exp") // 2
    n_z = lax.axis_size("exp") // 2
    tok_rows = tokens.shape[1]
    width = tokens.shape[2]
    experts = centroids.shape[1]
    capacity = 2 * (5 * tok_rows // (8 * experts))
    group = width // REPS
    heads = group // HEAD_DIM
    shard = w_qkv.shape[0]
    score_scale = HEAD_DIM ** (-0.5)

    half = tok_rows // 2
    own_tokens = tokens[0]
    tok_a, tok_b = gather_plane(own_tokens[:half], own_tokens[half:])
    seq = jnp.concatenate([part for pair in zip(tok_a, tok_b) for part in pair], axis=0)

    extra = 4 + experts
    pad = -extra % 128
    small = jnp.concatenate(
        [norm_gains, norm_biases, centroids, jnp.zeros((shard, pad), bf16)], axis=1
    )
    by_rep = w_qkv.reshape(shard, 3, REPS, group)
    sends = [
        jnp.concatenate([pick(by_rep, rep ^ k, 2).reshape(shard, 3 * group), small], axis=1)
        for k in range(REPS)
    ]
    got = jnp.stack([sends[0], over_x(sends[1]), over_y(sends[2]), over_diag(sends[3])])
    got = jnp.stack([pick(got, rep ^ k) for k in range(REPS)])
    along = gather_z(got)
    whole = both_cores(along, parity, 1)
    whole = whole.transpose(2, 0, 1, 3, 4).reshape(width, 3 * group + extra + pad)
    qkv_w = whole[:, : 3 * group]
    params = whole[:, 3 * group : 3 * group + extra].T.astype(f32)
    centroid = pick(whole[:, 3 * group + 4 : 3 * group + extra], own_z, 1)

    expert = routes[0, :, 0]
    onehot = (expert[:, None] == jnp.arange(experts, dtype=jnp.int32)[None, :]).astype(jnp.int32)
    before = jnp.cumsum(onehot, axis=0) - onehot
    rank = jnp.sum(before * onehot, axis=1)
    slot = ((expert - own_z) % n_z) * capacity + rank
    table = (jnp.arange(n_z * capacity, dtype=jnp.int32)[:, None] == slot[None, :]).astype(bf16)

    def dispatch(values):
        packed = product(table, values).astype(bf16).reshape(n_z, capacity, width)
        mine = jnp.concatenate([shift_z(packed[step], step) for step in range(n_z)], axis=0)
        return jnp.concatenate([mine, over_core(mine)], axis=0)

    def recall(rows):
        rows = rows.reshape(n_z, capacity, width)
        back = jnp.concatenate([shift_z(rows[step], -step) for step in range(n_z)], axis=0)
        return contract_rows(table, back)

    own_grad = grad_out[0]
    grad_rows = dispatch(own_grad).astype(f32)

    proj_core = gather_z(w_proj)
    proj_half = n_z // 2
    proj_a, proj_b = gather_plane(proj_core[:proj_half], proj_core[proj_half:])
    proj_w = [
        both_cores(jnp.concatenate(pair, axis=0), parity, 1).reshape(group, width)
        for pair in zip(proj_a, proj_b)
    ]

    layers = [gather_plane(w_in[0, sub], w_out[0, sub]) for sub in range(2)]

    seq32 = seq.astype(f32)
    normed, unit_in, inverse_in = layer_norm(seq32, params[0], params[2])
    attn_in = normed.astype(bf16)
    qkv = product(attn_in, qkv_w).astype(bf16)
    seq_len = qkv.shape[0]
    query, keys, values = [
        qkv[:, part * group : (part + 1) * group].reshape(seq_len, heads, HEAD_DIM)
        for part in range(3)
    ]
    docs = doc_ids[0].reshape(REPS, tok_rows)
    doc_rel = jnp.concatenate([pick(docs, rep ^ k) for k in range(REPS)])
    pos = jnp.concatenate([(rep ^ k) * tok_rows + jnp.arange(tok_rows) for k in range(REPS)])
    allowed = (pos[None, :] <= pos[:, None]) & (doc_rel[None, :] == doc_rel[:, None])
    raw = jnp.einsum("qhd,khd->hqk", query, keys, preferred_element_type=f32) * score_scale
    scores = jnp.where(allowed[None], raw, neg_fill)
    probs = jax.nn.softmax(scores, axis=-1)
    probs_b = probs.astype(bf16)
    mixed = jnp.einsum("hqk,khd->qhd", probs_b, values, preferred_element_type=f32)
    mixed = mixed.astype(bf16).reshape(REPS, tok_rows, group)
    mixed = [mixed[0], over_x(mixed[1]), over_y(mixed[2]), over_diag(mixed[3])]
    tokens32 = own_tokens.astype(f32)
    hidden = tokens32 + sum(product(mixed[k], proj_w[k]) for k in range(REPS))
    normed_mid, unit_mid, inverse_mid = layer_norm(hidden, params[1], params[3])
    expert_inputs = normed_mid.astype(bf16)

    own_slots = n_z * capacity
    rows = dispatch(expert_inputs)

    def swap(partial_sum):
        low = partial_sum.astype(bf16)
        return jnp.concatenate([over_core(low[own_slots:]), over_core(low[:own_slots])], axis=0)

    def own_total(partial_sum):
        sent = partial_sum[own_slots:].astype(bf16)
        return partial_sum[:own_slots] + over_core(sent).astype(f32)

    gating = jax.nn.sigmoid(product(rows, centroid))
    stream = rows.astype(f32)
    stored = []
    for sub in range(2):
        ins, outs = layers[sub]
        stream_b = stream.astype(bf16)
        pre = [product(stream_b, w) for w in ins]
        active = [jax.nn.gelu(u).astype(bf16) for u in pre]
        partial_sum = sum(contract_last(g, w) for g, w in zip(active, outs))
        stored.append((stream_b, pre, active))
        if sub == 0:
            stream = stream + partial_sum + swap(partial_sum).astype(f32)
        else:
            final = stream[:own_slots] + own_total(partial_sum)
    own_gate = gating[:own_slots]
    answer = (own_gate[:, None] * final).astype(bf16)
    combined = recall(answer)
    block_out = (hidden + combined).astype(bf16)

    own_rows32 = rows[:own_slots].astype(f32)
    grad_score = jnp.sum(grad_rows[:own_slots] * final, axis=-1) * own_gate * (1.0 - own_gate)
    grad_centroid = jnp.sum(grad_score[:, None] * own_rows32, axis=0)
    grad_stream = gating[:, None] * grad_rows
    grads_in, grads_out = [None, None], [None, None]
    for sub in (1, 0):
        ins, outs = layers[sub]
        stream_b, pre, active = stored[sub]
        branch = grad_stream.astype(bf16)
        grad_pre = []
        for u, w in zip(pre, outs):
            unused, gelu_back = jax.vjp(jax.nn.gelu, u)
            grad_pre.append(gelu_back(product(branch, w))[0].astype(bf16))
        partial_sum = sum(contract_last(du, w) for du, w in zip(grad_pre, ins))
        grads_in[sub] = scatter_plane_x([contract_rows(stream_b, du) for du in grad_pre])
        grads_out[sub] = scatter_plane_y([contract_rows(branch, g) for g in active])
        if sub == 1:
            grad_stream = grad_stream + partial_sum + swap(partial_sum).astype(f32)
        else:
            grad_first_rows = grad_stream[:own_slots] + own_total(partial_sum)
    grad_w_in = jnp.stack(grads_in)[None]
    grad_w_out = jnp.stack(grads_out)[None]
    grad_inputs = grad_first_rows + grad_score[:, None] * centroid.astype(f32)
    grad_mid = recall(grad_inputs.astype(bf16))

    grad_gain_mid = jnp.sum(grad_mid * unit_mid, axis=0)
    grad_bias_mid = jnp.sum(grad_mid, axis=0)
    grad_hidden = own_grad.astype(f32) + norm_back(grad_mid, unit_mid, inverse_mid, params[1])
    grad_hidden_b = grad_hidden.astype(bf16)
    grad_mixed = [contract_last(grad_hidden_b, w).astype(bf16) for w in proj_w]
    grad_mixed = [
        grad_mixed[0],
        over_x(grad_mixed[1]),
        over_y(grad_mixed[2]),
        over_diag(grad_mixed[3]),
    ]
    grad_mixed = jnp.concatenate(grad_mixed, axis=0).reshape(seq_len, heads, HEAD_DIM)

    def own_parity(blocks):
        axis = blocks.ndim - 3
        sent = pick(blocks, 1 - parity, axis).astype(bf16)
        return pick(blocks, parity, axis) + over_core(sent).astype(f32)

    proj_parts = [
        own_parity(contract_rows(o, grad_hidden_b).reshape(n_z, 2, shard, width)) for o in mixed
    ]
    proj_plane = jnp.concatenate(
        [
            scatter_plane_x([part[:proj_half] for part in proj_parts]),
            scatter_plane_y([part[proj_half:] for part in proj_parts]),
        ],
        axis=0,
    )
    grad_proj = scatter_z(proj_plane)

    grad_values = jnp.einsum("hqk,qhd->khd", probs_b, grad_mixed, preferred_element_type=f32)
    grad_probs = jnp.einsum("qhd,khd->hqk", grad_mixed, values, preferred_element_type=f32)
    grad_scores = (
        probs * (grad_probs - jnp.sum(grad_probs * probs, axis=-1, keepdims=True))
    ).astype(bf16)
    grad_query = score_scale * jnp.einsum(
        "hqk,khd->qhd", grad_scores, keys, preferred_element_type=f32
    )
    grad_keys = score_scale * jnp.einsum(
        "hqk,qhd->khd", grad_scores, query, preferred_element_type=f32
    )
    grad_qkv_b = jnp.concatenate(
        [g.reshape(seq_len, group).astype(bf16) for g in (grad_query, grad_keys, grad_values)],
        axis=1,
    )
    grad_attn = contract_last(grad_qkv_b, qkv_w)
    blocks = grad_attn.reshape(REPS, 2, half, width)
    grad_attn_own = jnp.concatenate(
        [
            scatter_plane_x([blocks[k, 0] for k in range(REPS)]),
            scatter_plane_y([blocks[k, 1] for k in range(REPS)]),
        ],
        axis=0,
    )
    grad_first = norm_back(grad_attn_own, unit_in[:tok_rows], inverse_in[:tok_rows], params[0])
    grad_tokens = (grad_hidden + grad_first).astype(bf16)

    column_mask = (jnp.arange(experts) == own_z).astype(f32)
    small_grads = jnp.concatenate(
        [
            jnp.stack(
                [
                    jnp.sum(grad_attn * unit_in, axis=0),
                    grad_gain_mid,
                    jnp.sum(grad_attn, axis=0),
                    grad_bias_mid,
                ],
                axis=1,
            ),
            grad_centroid[:, None] * column_mask[None, :],
            jnp.zeros((width, pad), f32),
        ],
        axis=1,
    )
    qkv_part = jnp.concatenate([contract_rows(attn_in, grad_qkv_b), small_grads], axis=1)
    columns = qkv_part.shape[1]
    qkv_part = own_parity(qkv_part.reshape(REPS, n_z, 2, shard, columns))
    qkv_part = scatter_z(qkv_part.transpose(1, 0, 2, 3)).astype(bf16)
    sends = [pick(qkv_part, rep ^ k) for k in range(REPS)]
    got = jnp.stack([sends[0], over_x(sends[1]), over_y(sends[2]), over_diag(sends[3])])
    got = got.astype(f32)
    small_sum = jnp.sum(got[:, :, 3 * group : 3 * group + extra], axis=0)
    big = jnp.stack([pick(got, rep ^ k) for k in range(REPS)])[:, :, : 3 * group]
    grad_qkv = big.reshape(REPS, shard, 3, group).transpose(1, 2, 0, 3).reshape(shard, 3 * width)
    return (
        block_out[None],
        grad_tokens[None],
        small_sum[:, 0:2],
        small_sum[:, 2:4],
        grad_qkv,
        grad_proj,
        small_sum[:, 4:],
        grad_w_in,
        grad_w_out,
    )


def solution(mesh):
    in_specs = (
        P("exp", "rep", None),
        P("exp", None),
        P("exp", "rep", None),
        P(("rep", "exp"), None),
        P(("rep", "exp"), None),
        P(("rep", "exp"), None),
        P(("rep", "exp"), None),
        P(("rep", "exp"), None),
        P("exp", None, None, "rep"),
        P("exp", None, None, "rep"),
        P("exp", "rep", None),
    )
    out_specs = (
        P("exp", "rep", None),
        P("exp", "rep", None),
        P(("rep", "exp"), None),
        P(("rep", "exp"), None),
        P(("rep", "exp"), None),
        P(("rep", "exp"), None),
        P(("rep", "exp"), None),
        P("exp", None, None, "rep"),
        P("exp", None, None, "rep"),
    )
    return jax.shard_map(local, mesh=mesh, in_specs=in_specs, out_specs=out_specs, check_vma=False)
```

```python
import functools

import jax
import jax.numpy as jnp
from jax import lax
from jax.experimental import pallas as pl
from jax.experimental.pallas import tpu as pltpu
from jax.sharding import PartitionSpec as P

HEAD_DIM = 64
REPS = 4
eps = 1e-05
neg_fill = -1e30
bf16 = jnp.bfloat16
f32 = jnp.float32


def flip(value, axis, mask):
    pairs = [(source, source ^ mask) for source in range(lax.axis_size(axis))]
    return lax.ppermute(value, axis, pairs)


def over_x(value):
    return flip(value, "rep", 1)


def over_y(value):
    return flip(value, "rep", 2)


def over_core(value):
    return flip(value, "exp", 1)


def shift_z(value, step):
    size = lax.axis_size("exp")
    if step % (size // 2) == 0:
        return value
    pairs = [(source, (source + 2 * step) % size) for source in range(size)]
    return lax.ppermute(value, "exp", pairs)


def pick(stacked, index, axis=0):
    return lax.dynamic_index_in_dim(stacked, index, axis=axis, keepdims=False)


def gather_z(block):
    n_z = lax.axis_size("exp") // 2
    own_z = lax.axis_index("exp") // 2
    out = jnp.zeros((n_z,) + block.shape, block.dtype)
    for step in range(n_z):
        out = lax.dynamic_update_index_in_dim(out, shift_z(block, step), (own_z - step) % n_z, 0)
    return out


def scatter_z(blocks):
    n_z = lax.axis_size("exp") // 2
    own_z = lax.axis_index("exp") // 2
    total = pick(blocks, own_z)
    for step in range(1, n_z):
        sent = pick(blocks, (own_z + step) % n_z).astype(bf16)
        total = total + shift_z(sent, step).astype(f32)
    return total


def both_cores(value, parity, axis):
    other = over_core(value)
    return jnp.stack(
        [jnp.where(parity == 0, value, other), jnp.where(parity == 0, other, value)], axis=axis
    )


def layer_norm(values, gain_vec, shift):
    average = jnp.mean(values, axis=-1, keepdims=True)
    centred = values - average
    inverse = lax.rsqrt(jnp.mean(centred * centred, axis=-1, keepdims=True) + eps)
    normed = centred * inverse
    return (normed * gain_vec + shift, normed, inverse)


def norm_back(gradient, normed, inverse, gain_vec):
    scaled = gradient * gain_vec
    bracket = (
        scaled
        - jnp.mean(scaled, axis=-1, keepdims=True)
        - normed * jnp.mean(scaled * normed, axis=-1, keepdims=True)
    )
    return inverse * bracket


def product(former, latter):
    return jnp.dot(former, latter, preferred_element_type=f32)


def after(values, *earlier):
    return lax.optimization_barrier((values, earlier))[0]


def exchange(blocks, axis):
    return lax.all_to_all(blocks, axis, split_axis=0, concat_axis=0, tiled=True)


MIB = 1 << 20


def call(
    body, outs, *operands, cost, grid=(), in_specs=None, out_specs=None, scratch=(), limit=32
):
    shapes = [jax.ShapeDtypeStruct(shape, dtype) for shape, dtype in outs]
    if in_specs is None:
        in_specs = [VMEM] * len(operands)
    if out_specs is None:
        out_specs = [VMEM] * len(outs)
    return pl.pallas_call(
        body,
        out_shape=shapes,
        grid=grid,
        in_specs=in_specs,
        out_specs=out_specs,
        scratch_shapes=list(scratch),
        compiler_params=pltpu.CompilerParams(vmem_limit_bytes=limit * MIB),
        cost_estimate=pl.CostEstimate(flops=cost * 1000**3, bytes_accessed=0, transcendentals=0),
    )(*operands)


VMEM = pl.BlockSpec(memory_space=pltpu.VMEM)
SMEM = pl.BlockSpec(memory_space=pltpu.SMEM)
HBM = pl.BlockSpec(memory_space=pl.ANY)


def dot_nn(a, b):
    return lax.dot_general(a, b, (((1,), (0,)), ((), ())), preferred_element_type=f32)


def dot_nt(a, b):
    return lax.dot_general(a, b, (((1,), (1,)), ((), ())), preferred_element_type=f32)


def dot_tn(a, b):
    return lax.dot_general(a, b, (((0,), (0,)), ((), ())), preferred_element_type=f32)


def stats_of(values):
    average = jnp.mean(values, axis=-1, keepdims=True)
    centred = values - average
    inverse = lax.rsqrt(jnp.mean(centred * centred, axis=-1, keepdims=True) + eps)
    return centred * inverse, inverse


def head_lanes(values, head):
    lanes = lax.broadcasted_iota(jnp.int32, values.shape, 1)
    keep = (lanes >= head * HEAD_DIM) & (lanes < (head + 1) * HEAD_DIM)
    return jnp.where(keep, values, jnp.zeros_like(values))


def mask_of(doc_col, doc_row, index, rows):
    reach = (index + 1) * rows
    keys = lax.broadcasted_iota(jnp.int32, (reach, rows), 0)
    queries = lax.broadcasted_iota(jnp.int32, (reach, rows), 1) + index * rows
    same = doc_col[:reach] == doc_row[:, index * rows : reach]
    return jnp.where((keys <= queries) & same, 0.0, neg_fill)


def sequence_parts(refs, rows):
    own, beside, above, diag_a, diag_b = refs
    return [
        (own, 0, 0),
        (beside, 1, 0),
        (above, 2, 0),
        (diag_a, 3, 0),
        (diag_b, 3, rows // 2),
    ]


def sequence_parts(refs, rows):
    own, beside, above, diag_a, diag_b = refs
    return [
        (own, 0, 0),
        (beside, 1, 0),
        (above, 2, 0),
        (diag_a, 3, 0),
        (diag_b, 3, rows // 2),
    ]


def attention_kernel(rows, group, place_ref, *refs):
    toks, refs = refs[:5], refs[5:]
    par_ref, w_ref, col_ref, row_ref, a_ref, qkv_ref, o_ref, lse_ref, vt_ref, ot_ref = refs
    rep = place_ref[0]
    heads = group // HEAD_DIM
    gain, shift = par_ref[0:1], par_ref[2:3]
    for ref, k, first in sequence_parts(toks, rows):
        normed, _ = stats_of(ref[...].astype(f32))
        block = (normed * gain + shift).astype(bf16)
        count = ref.shape[0]
        here = pl.ds(pl.multiple_of((rep ^ k) * rows + first, count), count)
        a_ref[here] = block
        qkv_ref[here] = dot_nn(block, w_ref[:, : 3 * group]).astype(bf16)
    vt_ref[...] = qkv_ref[:, 2 * group :].T
    for index in range(REPS):
        reach = (index + 1) * rows
        here = pl.ds(index * rows, rows)
        bias = mask_of(col_ref[...], row_ref[...], index, rows)

        def one(head, carry):
            query = head_lanes(qkv_ref[here, :group] * jnp.asarray(HEAD_DIM**-0.5, bf16), head)
            score = dot_nt(qkv_ref[:reach, group : 2 * group], query) + bias
            top = jnp.max(score, axis=0, keepdims=True)
            weight = jnp.exp(score - top)
            total = jnp.sum(weight, axis=0, keepdims=True)
            lanes = pl.ds(pl.multiple_of(head * HEAD_DIM, HEAD_DIM), HEAD_DIM)
            ot_ref[lanes] = dot_nn(vt_ref[lanes, :reach], weight.astype(bf16)) / total
            lse_ref[pl.ds(head, 1), here] = top + jnp.log(total)
            return carry

        lax.fori_loop(0, heads, one, 0)
        o_ref[here] = ot_ref[...].T.astype(bf16)


def attention_back_kernel(rows, group, place_ref, *refs):
    toks, refs = refs[:5], refs[5:]
    do_ref, w_ref, col_ref, row_ref, qkv_ref, o_ref, lse_ref, *refs = refs
    grad_ref, sum_ref, own_ref, to_x, to_y, left_y, left_x, *refs = refs
    kt_ref, dq_ref, dk_ref, dv_ref, delta_ref = refs
    rep = place_ref[0]
    heads = group // HEAD_DIM
    half = rows // 2
    kt_ref[...] = qkv_ref[:, group : 2 * group].T
    dk_ref[...] = jnp.zeros_like(dk_ref)
    dv_ref[...] = jnp.zeros_like(dv_ref)
    for index in range(REPS):
        reach = (index + 1) * rows
        here = pl.ds(index * rows, rows)
        bias = mask_of(col_ref[...], row_ref[...], index, rows)
        both = (do_ref[here].astype(f32) * o_ref[here].astype(f32)).T
        for head in range(heads):
            delta_ref[head : head + 1] = jnp.sum(
                both[head * HEAD_DIM : (head + 1) * HEAD_DIM], axis=0, keepdims=True
            )

        def one(head, carry):
            query = head_lanes(qkv_ref[here, :group] * jnp.asarray(HEAD_DIM**-0.5, bf16), head)
            grad = head_lanes(do_ref[here], head)
            score = dot_nt(qkv_ref[:reach, group : 2 * group], query) + bias
            prob = jnp.exp(score - lse_ref[pl.ds(head, 1), here])
            dprob = dot_nt(qkv_ref[:reach, 2 * group :], grad)
            dscore = (prob * (dprob - delta_ref[pl.ds(head, 1)])).astype(bf16)
            dv_ref[:reach] += dot_nn(prob.astype(bf16), grad)
            dk_ref[:reach] += dot_nn(dscore, query)
            lanes = pl.ds(pl.multiple_of(head * HEAD_DIM, HEAD_DIM), HEAD_DIM)
            dq_ref[lanes] = dot_nn(kt_ref[lanes, :reach], dscore)
            return carry

        lax.fori_loop(0, heads, one, 0)
        grad_ref[here, :group] = (dq_ref[...].T * HEAD_DIM**-0.5).astype(bf16)
    grad_ref[:, group : 2 * group] = dk_ref[...].astype(bf16)
    grad_ref[:, 2 * group :] = dv_ref[...].astype(bf16)
    sum_ref[...] = jnp.zeros_like(sum_ref)
    for ref, k, first in sequence_parts(toks, rows):
        count = ref.shape[0]
        here = pl.ds(pl.multiple_of((rep ^ k) * rows + first, count), count)
        back = dot_nt(grad_ref[here], w_ref[:, : 3 * group])
        normed, _ = stats_of(ref[...].astype(f32))
        sum_ref[0:1] += jnp.sum(back * normed, axis=0, keepdims=True)
        sum_ref[1:2] += jnp.sum(back, axis=0, keepdims=True)
        if k == 0:
            own_ref[...] = back
        elif k == 1:
            to_x[half:] = back[:half].astype(bf16)
            left_x[...] = back[half:]
        elif k == 2:
            left_y[...] = back[:half]
            to_y[half:] = back[half:].astype(bf16)
        elif first == 0:
            to_x[:half] = back.astype(bf16)
        else:
            to_y[:half] = back.astype(bf16)


def qkv_grad_kernel(group, extra, own_ref, a_ref, grad_ref, first_ref, mid_ref, cent_ref, out_ref):
    width = a_ref.shape[1]
    pad = out_ref.shape[1] - 3 * group
    row = lax.broadcasted_iota(jnp.int32, (pad, width), 0)
    small = jnp.where(row == 0, first_ref[0:1], 0.0)
    small = jnp.where(row == 1, mid_ref[0:1], small)
    small = jnp.where(row == 2, first_ref[1:2], small)
    small = jnp.where(row == 3, mid_ref[1:2], small)
    small = jnp.where(row == 4 + own_ref[1], cent_ref[0:1], small)
    out_ref[:, 3 * group :] = small.T
    for part in range(width // 256):
        piece = slice(part * 256, (part + 1) * 256)
        out_ref[piece, : 3 * group] = dot_tn(a_ref[:, piece], grad_ref[...])


def project_kernel(part_ref, w_ref, tok_ref, par_ref, table_ref, hidden_ref, packed_ref):
    hidden = tok_ref[...].astype(f32)
    for k in range(REPS):
        hidden = hidden + dot_nn(part_ref[k], w_ref[k])
    hidden_ref[...] = hidden
    normed, _ = stats_of(hidden)
    states = (normed * par_ref[1:2] + par_ref[3:4]).astype(bf16)
    packed_ref[...] = dot_nn(table_ref[...], states).astype(bf16)


def project_back_kernel(back_ref, w_ref, *refs):
    table_ref, hidden_ref, dy_ref, par_ref, dh_ref, dhb_ref, sum_ref, do_ref = refs
    grad = dot_nn(table_ref[...], back_ref[...])
    normed, inverse = stats_of(hidden_ref[...])
    sum_ref[...] = jnp.zeros_like(sum_ref)
    sum_ref[0:1] = jnp.sum(grad * normed, axis=0, keepdims=True)
    sum_ref[1:2] = jnp.sum(grad, axis=0, keepdims=True)
    dh = dy_ref[...].astype(f32) + norm_back(grad, normed, inverse, par_ref[1:2])
    dh_ref[...] = dh
    low = dh.astype(bf16)
    dhb_ref[...] = low
    for k in range(REPS):
        do_ref[k] = dot_nt(low, w_ref[k]).astype(bf16)


def proj_grad_kernel(part_ref, dhb_ref, out_ref):
    for k in range(REPS):
        out_ref[k] = dot_tn(part_ref[k], dhb_ref[...])


def tokens_grad_kernel(*refs):
    own_ref, from_x, from_y, upper, lower, tok_ref, par_ref, dh_ref, out_ref = refs
    half = upper.shape[0]
    parts = ((from_x, upper), (from_y, lower))
    for here, (direct, passed) in zip(halves(2 * half), parts):
        grad = own_ref[here] + direct[half:].astype(f32) + passed[...].astype(f32)
        normed, inverse = stats_of(tok_ref[here].astype(f32))
        back = norm_back(grad, normed, inverse, par_ref[0:1])
        out_ref[here] = (dh_ref[here] + back).astype(bf16)


def gelu_both(u):
    scale = (2.0 / jnp.pi) ** 0.5
    square = u * u
    turn = jnp.tanh(scale * u * (1.0 + 0.044715 * square))
    lift = 0.5 * (1.0 + turn)
    slope = lift + 0.5 * u * (1.0 - turn * turn) * (scale * (1.0 + 0.134145 * square))
    return u * lift, slope


def fetch_slices(sources, in_buf, out_buf, sems):
    step = pl.program_id(0)

    @pl.when(step == 0)
    def _():
        for k, source_in, source_out in sources:
            pltpu.make_async_copy(source_in, in_buf.at[k], sems.at[0, k]).start()
            pltpu.make_async_copy(source_out, out_buf.at[k], sems.at[1, k]).start()

    _, source_in, source_out = sources[-1]
    pltpu.make_async_copy(source_in, in_buf.at[step], sems.at[0, step]).wait()
    pltpu.make_async_copy(source_out, out_buf.at[step], sems.at[1, step]).wait()


def gathered(ref):
    return [(k, ref.at[k, 0], ref.at[k, 1]) for k in range(REPS)]


def plane_slices(refs, rep):
    w_in, w_out, beside, above, diag_in, diag_out = refs
    return [
        (rep, w_in.at[0, 1], w_out.at[0, 1]),
        (rep ^ 1, beside.at[0], beside.at[1]),
        (rep ^ 2, above.at[0], above.at[1]),
        (rep ^ 3, diag_in, diag_out),
    ]


def halves(count):
    half = count // 2
    return [slice(0, half), slice(half, count)]


def expert_first_kernel(place_ref, par_ref, rows_a, rows_b, w_ref, gate_ref, *refs):
    act_ref, slope_ref, total_ref, low_a, low_b, rows_buf, in_buf, out_buf, sems = refs
    step = pl.program_id(0)
    count = rows_buf.shape[0]
    upper, lower = halves(count)

    @pl.when(step == 0)
    def _():
        rows_buf[upper] = rows_a[...]
        rows_buf[lower] = rows_b[...]
        total_ref[...] = jnp.zeros_like(total_ref)
        centroid = par_ref[pl.ds(4 + place_ref[1], 1)]
        weight = jnp.broadcast_to(centroid, (128, centroid.shape[1])).astype(bf16)
        for here in (upper, lower):
            gate_ref[here] = 1.0 / (1.0 + jnp.exp(-dot_nt(rows_buf[here], weight)))

    fetch_slices(gathered(w_ref), in_buf, out_buf, sems)
    tile = count // 2

    def one(index, carry):
        here = pl.ds(pl.multiple_of(index * tile, tile), tile)
        active, slope = gelu_both(dot_nn(rows_buf[here], in_buf[step]))
        active = active.astype(bf16)
        act_ref[0, here] = active
        slope_ref[0, here] = slope
        total_ref[here] += dot_nt(active, out_buf[step])
        return carry

    lax.fori_loop(0, 2, one, 0)

    @pl.when(step == pl.num_programs(0) - 1)
    def _():
        low_a[...] = total_ref[upper].astype(bf16)
        low_b[...] = total_ref[lower].astype(bf16)


def expert_second_kernel(*refs):
    place_ref, rows_a, rows_b, first_ref, rec_a, rec_b, gate_ref, dy_a, dy_b, *refs = refs
    weights, refs = refs[:6], refs[6:]
    act_ref, du_ref, zb_ref, db_ref, own_ref, z2_ref, dz_ref, low_a, low_b, *refs = refs
    z2_acc, in_buf, out_buf, sems = refs
    step = pl.program_id(0)
    count = zb_ref.shape[0]
    upper, lower = halves(count)

    @pl.when(step == 0)
    def _():
        own = rows_a[...].astype(f32) + first_ref[upper] + rec_a[...].astype(f32)
        own_ref[...] = own
        zb_ref[upper] = own.astype(bf16)
        other = rows_b[...].astype(f32) + first_ref[lower] + rec_b[...].astype(f32)
        zb_ref[lower] = other.astype(bf16)
        db_ref[upper] = (gate_ref[upper, 0:1] * dy_a[...].astype(f32)).astype(bf16)
        db_ref[lower] = (gate_ref[lower, 0:1] * dy_b[...].astype(f32)).astype(bf16)
        z2_acc[...] = jnp.zeros_like(z2_acc)
        dz_ref[...] = jnp.zeros_like(dz_ref)

    fetch_slices(plane_slices(weights, place_ref[0]), in_buf, out_buf, sems)
    tile = count // 2

    def one(index, carry):
        here = pl.ds(pl.multiple_of(index * tile, tile), tile)
        active, slope = gelu_both(dot_nn(zb_ref[here], in_buf[step]))
        active = active.astype(bf16)
        act_ref[0, here] = active
        z2_acc[here] += dot_nt(active, out_buf[step])
        du = (slope * dot_nn(db_ref[here], out_buf[step])).astype(bf16)
        du_ref[0, here] = du
        dz_ref[here] += dot_nt(du, in_buf[step])
        return carry

    lax.fori_loop(0, 2, one, 0)

    @pl.when(step == REPS - 1)
    def _():
        own_ref[...] += z2_acc[upper]
        z2_ref[...] = z2_acc[lower].astype(bf16)
        low_a[...] = dz_ref[upper].astype(bf16)
        low_b[...] = dz_ref[lower].astype(bf16)


def expert_last_kernel(*refs):
    gate_ref, dy_a, dy_b, second_ref, rec_a, rec_b, slope_ref, *refs = refs
    w_ref, *refs = refs
    du_ref, db_ref, own_ref, low_ref, acc, in_buf, out_buf, sems = refs
    step = pl.program_id(0)
    count = db_ref.shape[0]
    upper, lower = halves(count)

    @pl.when(step == 0)
    def _():
        own = gate_ref[upper, 0:1] * dy_a[...].astype(f32) + second_ref[upper]
        own = own + rec_a[...].astype(f32)
        own_ref[...] = own
        db_ref[upper] = own.astype(bf16)
        other = gate_ref[lower, 0:1] * dy_b[...].astype(f32) + second_ref[lower]
        db_ref[lower] = (other + rec_b[...].astype(f32)).astype(bf16)
        acc[...] = jnp.zeros_like(acc)

    fetch_slices(gathered(w_ref), in_buf, out_buf, sems)
    tile = count // 2

    def one(index, carry):
        here = pl.ds(pl.multiple_of(index * tile, tile), tile)
        du = (slope_ref[0, here] * dot_nn(db_ref[here], out_buf[step])).astype(bf16)
        du_ref[0, here] = du
        acc[here] += dot_nt(du, in_buf[step])
        return carry

    lax.fori_loop(0, 2, one, 0)

    @pl.when(step == REPS - 1)
    def _():
        own_ref[...] += acc[upper]
        low_ref[...] = acc[lower].astype(bf16)


def weights_kernel(rows_a, rows_b, db_ref, du_ref, act_ref, out_ref):
    rows = jnp.concatenate([rows_a[...], rows_b[...]], axis=0)
    out_ref[0, 0] = dot_tn(rows, du_ref[0]).astype(bf16)
    out_ref[0, 1] = dot_tn(db_ref[...], act_ref[0]).astype(bf16)


def answer_kernel(final_ref, z2_ref, gate_ref, dy_ref, rows_ref, out_ref, score_ref, cent_ref):
    final = final_ref[...] + z2_ref[...].astype(f32)
    gate = gate_ref[...]
    out_ref[...] = (gate[:, 0:1] * final).astype(bf16)
    score = jnp.sum(dy_ref[...].astype(f32) * final, axis=1, keepdims=True)
    score = score * gate * (1.0 - gate)
    score_ref[...] = score
    cent_ref[...] = jnp.zeros_like(cent_ref)
    cent_ref[0:1] = jnp.sum(score[:, 0:1] * rows_ref[...].astype(f32), axis=0, keepdims=True)


def states_grad_kernel(place_ref, own_ref, low_ref, score_ref, par_ref, out_ref):
    centroid = par_ref[pl.ds(4 + place_ref[1], 1)]
    grad = own_ref[...] + low_ref[...].astype(f32) + score_ref[:, 0:1] * centroid
    out_ref[...] = grad.astype(bf16)


def local(
    tokens,
    doc_ids,
    routes,
    norm_gains,
    norm_biases,
    w_qkv,
    w_proj,
    centroids,
    w_in,
    w_out,
    grad_out,
):
    rep = lax.axis_index("rep")
    parity = lax.axis_index("exp") % 2
    own_z = lax.axis_index("exp") // 2
    n_z = lax.axis_size("exp") // 2
    tok_rows = tokens.shape[1]
    width = tokens.shape[2]
    experts = centroids.shape[1]
    capacity = 2 * (5 * tok_rows // (8 * experts))
    group = width // REPS
    shard = w_qkv.shape[0]
    hidden_units = w_in.shape[3]
    seq_len = doc_ids.shape[1]
    half = tok_rows // 2
    place = jnp.stack([rep, own_z]).astype(jnp.int32)

    extra = 4 + experts
    pad = -extra % 128
    columns = 3 * group + extra + pad
    small = jnp.concatenate(
        [norm_gains, norm_biases, centroids, jnp.zeros((shard, pad), bf16)], axis=1
    )
    by_rep = w_qkv.reshape(shard, 3, REPS, group).transpose(2, 0, 1, 3)
    by_rep = by_rep.reshape(REPS, shard, 3 * group)
    small = jnp.concatenate([small, w_proj], axis=1)
    sends = jnp.concatenate(
        [by_rep, jnp.broadcast_to(small[None], (REPS,) + small.shape)], axis=2
    )
    got = exchange(sends, "rep")

    def assembled(blocks):
        blocks = both_cores(blocks, parity, 1).transpose(2, 0, 1, 3, 4)
        return blocks.reshape(width, blocks.shape[-1])

    along = gather_z(got[:, :, :columns])
    whole = assembled(along)
    proj_w = assembled(gather_z(after(got[:, :, columns:], along))).reshape(REPS, group, width)
    params = whole[:, 3 * group :].T.astype(f32)

    own_tokens = tokens[0]
    first_tokens = after(own_tokens, got)
    tok_x, tok_y = over_x(first_tokens), over_y(first_tokens)
    seq = [own_tokens, tok_x, tok_y, over_y(tok_x[:half]), over_x(tok_y[half:])]

    layer0 = lax.all_gather(jnp.stack([w_in[0, 0], w_out[0, 0]]), "rep")
    expert = routes[0, :, 0]
    onehot = (expert[:, None] == jnp.arange(experts, dtype=jnp.int32)[None, :]).astype(jnp.int32)
    before = jnp.cumsum(onehot, axis=0) - onehot
    rank = jnp.sum(before * onehot, axis=1)
    slot = expert * capacity + rank % 2 * (capacity // 2) + rank // 2
    own_slots = experts * capacity
    slots = jnp.arange(own_slots, dtype=jnp.int32)
    table = (slots[:, None] == slot[None, :]).astype(bf16)
    table_t = (slots[None, :] == slot[:, None]).astype(bf16)
    spread = (2 * n_z, capacity // 2, width)

    def travel(rows):
        return exchange(rows.reshape(spread), "exp").reshape(own_slots, width)

    own_grad = grad_out[0]
    packed_grad = product(table, own_grad).astype(bf16)

    docs = doc_ids.reshape(1, seq_len)
    doc_col = doc_ids.reshape(seq_len, 1)
    attn_in, qkv, mixed_own, lse = call(
        functools.partial(attention_kernel, tok_rows, group),
        [
            ((seq_len, width), bf16),
            ((seq_len, 3 * group), bf16),
            ((seq_len, group), bf16),
            ((8, seq_len), f32),
        ],
        place,
        *seq,
        params,
        whole,
        doc_col,
        docs,
        in_specs=[SMEM] + [VMEM] * 9,
        scratch=[pltpu.VMEM((group, seq_len), bf16), pltpu.VMEM((group, tok_rows), f32)],
        cost=14,
    )
    mixed = exchange(mixed_own.reshape(REPS, tok_rows, group), "rep")
    own_second = after(jnp.stack([w_in[0, 1], w_out[0, 1]]), mixed)
    w1_x, w1_y = over_x(own_second), over_y(own_second)
    layer1 = [w_in, w_out, w1_x, w1_y, over_y(w1_x[0]), over_x(w1_y[1])]
    hidden, packed = call(
        project_kernel,
        [((tok_rows, width), f32), ((own_slots, width), bf16)],
        mixed,
        proj_w,
        own_tokens,
        params,
        table,
        cost=2,
    )

    all_slots = 2 * own_slots
    own_rows, all_rows = (own_slots, width), (all_slots, width)
    rows_a = travel(packed)
    rows_b = over_core(rows_a)
    dy_a = travel(after(packed_grad, rows_a))
    dy_b = over_core(dy_a)
    gate_shape = (all_slots, 128)
    by_slice = (REPS, all_slots, hidden_units)
    sliced = pl.BlockSpec((1, all_slots, hidden_units), lambda k: (k, 0, 0))
    slice_buf = pltpu.VMEM((REPS, width, hidden_units), bf16)
    slices = [slice_buf, slice_buf, pltpu.SemaphoreType.DMA((2, REPS))]
    gate, active0, slope0, first, low_a, low_b = call(
        expert_first_kernel,
        [
            (gate_shape, f32),
            (by_slice, bf16),
            (by_slice, f32),
            (all_rows, f32),
            (own_rows, bf16),
            (own_rows, bf16),
        ],
        place,
        params,
        rows_a,
        rows_b,
        layer0,
        grid=(REPS,),
        in_specs=[SMEM] + [VMEM] * 3 + [HBM],
        out_specs=[VMEM, sliced, sliced] + [VMEM] * 3,
        scratch=[pltpu.VMEM(all_rows, bf16)] + slices,
        limit=48,
        cost=14,
    )
    rec_a, rec_b = over_core(low_b), over_core(low_a)
    active1, du1, stream1, branch1, own_final, z2_low, second, low_a, low_b = call(
        expert_second_kernel,
        [
            (by_slice, bf16),
            (by_slice, bf16),
            (all_rows, bf16),
            (all_rows, bf16),
            (own_rows, f32),
            (own_rows, bf16),
            (all_rows, f32),
            (own_rows, bf16),
            (own_rows, bf16),
        ],
        place,
        rows_a,
        rows_b,
        first,
        rec_a,
        rec_b,
        gate,
        dy_a,
        dy_b,
        *layer1,
        grid=(REPS,),
        in_specs=[SMEM] + [VMEM] * 8 + [HBM] * 6,
        out_specs=[sliced, sliced] + [VMEM] * 7,
        scratch=[pltpu.VMEM(all_rows, f32)] + slices,
        limit=56,
        cost=22,
    )
    rec_a, rec_b = over_core(low_b), over_core(low_a)
    answer, score, grad_centroid = call(
        answer_kernel,
        [(own_rows, bf16), ((own_slots, 128), f32), ((8, width), f32)],
        own_final,
        over_core(z2_low),
        gate[:own_slots],
        dy_a,
        rows_a,
        cost=2,
    )
    du0, branch0, own_first_grad, low = call(
        expert_last_kernel,
        [(by_slice, bf16), (all_rows, bf16), (own_rows, f32), (own_rows, bf16)],
        gate,
        dy_a,
        dy_b,
        second,
        rec_a,
        rec_b,
        slope0,
        layer0,
        grid=(REPS,),
        in_specs=[VMEM] * 6 + [sliced, HBM],
        out_specs=[sliced] + [VMEM] * 3,
        scratch=[pltpu.VMEM(all_rows, f32)] + slices,
        limit=56,
        cost=13,
    )
    (grad_inputs,) = call(
        states_grad_kernel,
        [(own_rows, bf16)],
        place,
        own_first_grad,
        over_core(low),
        score,
        params,
        in_specs=[SMEM] + [VMEM] * 4,
        cost=1,
    )
    grad_back = travel(grad_inputs)

    pair = (2, width, hidden_units)

    def weights(a, b, branch, du, active, order):
        (out,) = call(
            weights_kernel,
            [((REPS,) + pair, bf16)],
            a,
            b,
            branch,
            du,
            active,
            grid=(REPS,),
            in_specs=[
                pl.BlockSpec(own_rows, lambda k: (0, 0)),
                pl.BlockSpec(own_rows, lambda k: (0, 0)),
                pl.BlockSpec(all_rows, lambda k: (0, 0)),
                sliced,
                sliced,
            ],
            out_specs=[pl.BlockSpec((1,) + pair, order)],
            limit=48,
            cost=10,
        )
        return out

    def natural(k):
        return (k, 0, 0, 0)

    def swapped(k):
        return (k % 2 * 2 + k // 2, 0, 0, 0)

    weights1 = weights(stream1[:own_slots], stream1[own_slots:], branch1, du1, active1, natural)
    grads1 = lax.psum_scatter(weights1, "rep", scatter_dimension=0).astype(f32)
    streams = after((rows_a, rows_b), grad_inputs)
    weights0 = weights(*streams, branch0, du0, active0, swapped)
    grads0 = lax.psum_scatter(
        weights0, "rep", scatter_dimension=0, axis_index_groups=[[0, 2, 1, 3]]
    ).astype(f32)

    grad_hidden, grad_hidden_b, mid_sums, grad_mixed = call(
        project_back_kernel,
        [
            ((tok_rows, width), f32),
            ((tok_rows, width), bf16),
            ((8, width), f32),
            ((REPS, tok_rows, group), bf16),
        ],
        grad_back,
        proj_w,
        table_t,
        hidden,
        own_grad,
        params,
        cost=3,
    )
    grad_mixed = exchange(grad_mixed, "rep").reshape(seq_len, group)
    (proj_part,) = call(
        proj_grad_kernel, [((REPS, group, width), f32)], mixed, grad_hidden_b, cost=2
    )
    returned = travel(after(answer, grad_mixed))
    block_out = (hidden + product(table_t, returned)).astype(bf16)

    def own_parity(blocks):
        axis = blocks.ndim - 3
        sent = pick(blocks, 1 - parity, axis).astype(bf16)
        return pick(blocks, parity, axis) + over_core(sent).astype(f32)

    proj_part = own_parity(proj_part.reshape(REPS, n_z, 2, shard, width)).astype(bf16)
    proj_part = jnp.sum(exchange(proj_part, "rep").astype(f32), axis=0)
    grad_proj = scatter_z(proj_part)

    grad_qkv_b, first_sums, own_attn, to_x, to_y, left_y, left_x = call(
        functools.partial(attention_back_kernel, tok_rows, group),
        [
            ((seq_len, 3 * group), bf16),
            ((8, width), f32),
            ((tok_rows, width), f32),
            ((tok_rows, width), bf16),
            ((tok_rows, width), bf16),
            ((half, width), f32),
            ((half, width), f32),
        ],
        place,
        *seq,
        grad_mixed,
        whole,
        doc_col,
        docs,
        qkv,
        mixed_own,
        lse,
        in_specs=[SMEM] + [VMEM] * 12,
        scratch=[
            pltpu.VMEM((group, seq_len), bf16),
            pltpu.VMEM((group, tok_rows), f32),
            pltpu.VMEM((seq_len, group), f32),
            pltpu.VMEM((seq_len, group), f32),
            pltpu.VMEM((8, tok_rows), f32),
        ],
        limit=40,
        cost=17,
    )
    from_x, from_y = over_x(to_x), over_y(to_y)
    grad_w_in = jnp.stack([grads0[0], grads1[0]])[None]
    grad_w_out = jnp.stack([grads0[1], grads1[1]])[None]
    upper = over_y((left_y + from_x[:half].astype(f32)).astype(bf16))
    lower = over_x((left_x + from_y[:half].astype(f32)).astype(bf16))
    (grad_tokens,) = call(
        tokens_grad_kernel,
        [((tok_rows, width), bf16)],
        own_attn,
        from_x,
        from_y,
        upper,
        lower,
        own_tokens,
        params,
        grad_hidden,
        cost=2,
    )

    (qkv_part,) = call(
        functools.partial(qkv_grad_kernel, group, extra),
        [((width, columns), f32)],
        place,
        attn_in,
        grad_qkv_b,
        first_sums,
        mid_sums,
        grad_centroid,
        in_specs=[SMEM] + [VMEM] * 5,
        cost=2,
    )
    qkv_part = own_parity(qkv_part.reshape(REPS, n_z, 2, shard, columns))
    qkv_part = scatter_z(qkv_part.transpose(1, 0, 2, 3)).astype(bf16)
    got = exchange(after(qkv_part, proj_part), "rep").astype(f32)
    small_sum = jnp.sum(got[:, :, 3 * group : 3 * group + extra], axis=0)
    big = got[:, :, : 3 * group].reshape(REPS, shard, 3, group)
    grad_qkv = big.transpose(1, 2, 0, 3).reshape(shard, 3 * width)
    return (
        block_out[None],
        grad_tokens[None],
        small_sum[:, 0:2],
        small_sum[:, 2:4],
        grad_qkv,
        grad_proj,
        small_sum[:, 4:],
        grad_w_in,
        grad_w_out,
    )


def solution(mesh):
    in_specs = (
        P("exp", "rep", None),
        P("exp", None),
        P("exp", "rep", None),
        P(("rep", "exp"), None),
        P(("rep", "exp"), None),
        P(("rep", "exp"), None),
        P(("rep", "exp"), None),
        P(("rep", "exp"), None),
        P("exp", None, None, "rep"),
        P("exp", None, None, "rep"),
        P("exp", "rep", None),
    )
    out_specs = (
        P("exp", "rep", None),
        P("exp", "rep", None),
        P(("rep", "exp"), None),
        P(("rep", "exp"), None),
        P(("rep", "exp"), None),
        P(("rep", "exp"), None),
        P(("rep", "exp"), None),
        P("exp", None, None, "rep"),
        P("exp", None, None, "rep"),
    )
    return jax.shard_map(local, mesh=mesh, in_specs=in_specs, out_specs=out_specs, check_vma=False)
```

```python
import functools

import jax
import jax.numpy as jnp
from jax import lax
from jax.experimental import pallas as pl
from jax.experimental.pallas import tpu as pltpu
from jax.sharding import PartitionSpec as P

HEAD_DIM = 64
REPS = 4
eps = 1e-05
neg_fill = -1e30
bf16 = jnp.bfloat16
f32 = jnp.float32


def flip(value, axis, mask):
    pairs = [(source, source ^ mask) for source in range(lax.axis_size(axis))]
    return lax.ppermute(value, axis, pairs)


def over_x(value):
    return flip(value, "rep", 1)


def over_y(value):
    return flip(value, "rep", 2)


def over_core(value):
    return flip(value, "exp", 1)


def shift_z(value, step):
    size = lax.axis_size("exp")
    if step % (size // 2) == 0:
        return value
    pairs = [(source, (source + 2 * step) % size) for source in range(size)]
    return lax.ppermute(value, "exp", pairs)


def pick(stacked, index, axis=0):
    return lax.dynamic_index_in_dim(stacked, index, axis=axis, keepdims=False)


def gather_z(block):
    n_z = lax.axis_size("exp") // 2
    own_z = lax.axis_index("exp") // 2
    out = jnp.zeros((n_z,) + block.shape, block.dtype)
    for step in range(n_z):
        out = lax.dynamic_update_index_in_dim(out, shift_z(block, step), (own_z - step) % n_z, 0)
    return out


def scatter_z(blocks):
    n_z = lax.axis_size("exp") // 2
    own_z = lax.axis_index("exp") // 2
    total = pick(blocks, own_z)
    for step in range(1, n_z):
        sent = pick(blocks, (own_z + step) % n_z).astype(bf16)
        total = total + shift_z(sent, step).astype(f32)
    return total


def both_cores(value, parity, axis):
    other = over_core(value)
    return jnp.stack(
        [jnp.where(parity == 0, value, other), jnp.where(parity == 0, other, value)], axis=axis
    )


def layer_norm(values, gain_vec, shift):
    average = jnp.mean(values, axis=-1, keepdims=True)
    centred = values - average
    inverse = lax.rsqrt(jnp.mean(centred * centred, axis=-1, keepdims=True) + eps)
    normed = centred * inverse
    return (normed * gain_vec + shift, normed, inverse)


def norm_back(gradient, normed, inverse, gain_vec):
    scaled = gradient * gain_vec
    bracket = (
        scaled
        - jnp.mean(scaled, axis=-1, keepdims=True)
        - normed * jnp.mean(scaled * normed, axis=-1, keepdims=True)
    )
    return inverse * bracket


def product(former, latter):
    return jnp.dot(former, latter, preferred_element_type=f32)


def after(values, *earlier):
    return lax.optimization_barrier((values, earlier))[0]


def exchange(blocks, axis):
    return lax.all_to_all(blocks, axis, split_axis=0, concat_axis=0, tiled=True)


MIB = 1 << 20


def whole_block(shape):
    return pl.BlockSpec(shape, lambda *_: (0,) * len(shape), pipeline_mode=pl.Buffered(1))


def call(
    body, outs, *operands, cost, grid=(1,), specs=None, out_specs=None, scratch=(), limit=40, alias=None
):
    shapes = [jax.ShapeDtypeStruct(shape, dtype) for shape, dtype in outs]
    in_specs = [whole_block(operand.shape) for operand in operands]
    for number, spec in (specs or {}).items():
        in_specs[number] = spec
    kinds = [whole_block(shape) for shape, _ in outs]
    for number, spec in (out_specs or {}).items():
        kinds[number] = spec
    return pl.pallas_call(
        body,
        out_shape=shapes,
        grid=grid,
        in_specs=in_specs,
        out_specs=kinds,
        scratch_shapes=list(scratch),
        input_output_aliases=alias or {},
        compiler_params=pltpu.CompilerParams(vmem_limit_bytes=limit * MIB),
        cost_estimate=pl.CostEstimate(flops=cost * 1000**3, bytes_accessed=0, transcendentals=0),
    )(*operands)


SMEM = pl.BlockSpec(memory_space=pltpu.SMEM)
HBM = pl.BlockSpec(memory_space=pl.ANY)


def dot_nn(a, b):
    return lax.dot_general(a, b, (((1,), (0,)), ((), ())), preferred_element_type=f32)


def dot_nt(a, b):
    return lax.dot_general(a, b, (((1,), (1,)), ((), ())), preferred_element_type=f32)


def dot_tn(a, b):
    return lax.dot_general(a, b, (((0,), (0,)), ((), ())), preferred_element_type=f32)


def stats_of(values):
    average = jnp.mean(values, axis=-1, keepdims=True)
    centred = values - average
    inverse = lax.rsqrt(jnp.mean(centred * centred, axis=-1, keepdims=True) + eps)
    return centred * inverse, inverse


def head_lanes(values, head):
    lanes = lax.broadcasted_iota(jnp.int32, values.shape, 1)
    keep = (lanes >= head * HEAD_DIM) & (lanes < (head + 1) * HEAD_DIM)
    return jnp.where(keep, values, jnp.zeros_like(values))


def mask_of(doc_col, doc_row, index, rows):
    reach = (index + 1) * rows
    keys = lax.broadcasted_iota(jnp.int32, (reach, rows), 0)
    queries = lax.broadcasted_iota(jnp.int32, (reach, rows), 1) + index * rows
    same = doc_col[:reach] == doc_row[:, index * rows : reach]
    return jnp.where((keys <= queries) & same, 0.0, neg_fill)


def sequence_parts(refs, rows):
    own, beside, above, diag_a, diag_b = refs
    return [
        (own, 0, 0),
        (beside, 1, 0),
        (above, 2, 0),
        (diag_a, 3, 0),
        (diag_b, 3, rows // 2),
    ]


def sequence_parts(refs, rows):
    own, beside, above, diag_a, diag_b = refs
    return [
        (own, 0, 0),
        (beside, 1, 0),
        (above, 2, 0),
        (diag_a, 3, 0),
        (diag_b, 3, rows // 2),
    ]


def attention_kernel(rows, group, place_ref, *refs):
    toks, refs = refs[:5], refs[5:]
    par_ref, w_ref, col_ref, row_ref, a_ref, qkv_ref, o_ref, lse_ref, vt_ref, ot_ref = refs
    rep = place_ref[0]
    heads = group // HEAD_DIM
    gain, shift = par_ref[0:1], par_ref[2:3]
    for ref, k, first in sequence_parts(toks, rows):
        normed, _ = stats_of(ref[...].astype(f32))
        block = (normed * gain + shift).astype(bf16)
        count = ref.shape[0]
        here = pl.ds(pl.multiple_of((rep ^ k) * rows + first, count), count)
        a_ref[here] = block
        qkv_ref[here] = dot_nn(block, w_ref[:, : 3 * group]).astype(bf16)
    vt_ref[...] = qkv_ref[:, 2 * group :].T
    for index in range(REPS):
        reach = (index + 1) * rows
        here = pl.ds(index * rows, rows)
        bias = mask_of(col_ref[...], row_ref[...], index, rows)

        def one(head, carry):
            query = head_lanes(qkv_ref[here, :group] * jnp.asarray(HEAD_DIM**-0.5, bf16), head)
            score = dot_nt(qkv_ref[:reach, group : 2 * group], query) + bias
            top = jnp.max(score, axis=0, keepdims=True)
            weight = jnp.exp(score - top)
            total = jnp.sum(weight, axis=0, keepdims=True)
            lanes = pl.ds(pl.multiple_of(head * HEAD_DIM, HEAD_DIM), HEAD_DIM)
            ot_ref[lanes] = dot_nn(vt_ref[lanes, :reach], weight.astype(bf16)) / total
            lse_ref[pl.ds(head, 1), here] = top + jnp.log(total)
            return carry

        lax.fori_loop(0, heads, one, 0)
        o_ref[here] = ot_ref[...].T.astype(bf16)


def attention_back_kernel(rows, group, place_ref, *refs):
    toks, refs = refs[:5], refs[5:]
    do_ref, w_ref, col_ref, row_ref, qkv_ref, o_ref, lse_ref, *refs = refs
    grad_ref, sum_ref, own_ref, to_x, to_y, left_y, left_x, *refs = refs
    kt_ref, dq_ref, dk_ref, dv_ref, delta_ref = refs
    rep = place_ref[0]
    heads = group // HEAD_DIM
    half = rows // 2
    kt_ref[...] = qkv_ref[:, group : 2 * group].T
    dk_ref[...] = jnp.zeros_like(dk_ref)
    dv_ref[...] = jnp.zeros_like(dv_ref)
    for index in range(REPS):
        reach = (index + 1) * rows
        here = pl.ds(index * rows, rows)
        bias = mask_of(col_ref[...], row_ref[...], index, rows)
        both = (do_ref[here].astype(f32) * o_ref[here].astype(f32)).T
        for head in range(heads):
            delta_ref[head : head + 1] = jnp.sum(
                both[head * HEAD_DIM : (head + 1) * HEAD_DIM], axis=0, keepdims=True
            )

        def one(head, carry):
            query = head_lanes(qkv_ref[here, :group] * jnp.asarray(HEAD_DIM**-0.5, bf16), head)
            grad = head_lanes(do_ref[here], head)
            score = dot_nt(qkv_ref[:reach, group : 2 * group], query) + bias
            prob = jnp.exp(score - lse_ref[pl.ds(head, 1), here])
            dprob = dot_nt(qkv_ref[:reach, 2 * group :], grad)
            dscore = (prob * (dprob - delta_ref[pl.ds(head, 1)])).astype(bf16)
            dv_ref[:reach] += dot_nn(prob.astype(bf16), grad)
            dk_ref[:reach] += dot_nn(dscore, query)
            lanes = pl.ds(pl.multiple_of(head * HEAD_DIM, HEAD_DIM), HEAD_DIM)
            dq_ref[lanes] = dot_nn(kt_ref[lanes, :reach], dscore)
            return carry

        lax.fori_loop(0, heads, one, 0)
        grad_ref[here, :group] = (dq_ref[...].T * HEAD_DIM**-0.5).astype(bf16)
    grad_ref[:, group : 2 * group] = dk_ref[...].astype(bf16)
    grad_ref[:, 2 * group :] = dv_ref[...].astype(bf16)
    sum_ref[...] = jnp.zeros_like(sum_ref)
    for ref, k, first in sequence_parts(toks, rows):
        count = ref.shape[0]
        here = pl.ds(pl.multiple_of((rep ^ k) * rows + first, count), count)
        back = dot_nt(grad_ref[here], w_ref[:, : 3 * group])
        normed, _ = stats_of(ref[...].astype(f32))
        sum_ref[0:1] += jnp.sum(back * normed, axis=0, keepdims=True)
        sum_ref[1:2] += jnp.sum(back, axis=0, keepdims=True)
        if k == 0:
            own_ref[...] = back
        elif k == 1:
            to_x[half:] = back[:half].astype(bf16)
            left_x[...] = back[half:]
        elif k == 2:
            left_y[...] = back[:half]
            to_y[half:] = back[half:].astype(bf16)
        elif first == 0:
            to_x[:half] = back.astype(bf16)
        else:
            to_y[:half] = back.astype(bf16)


def qkv_grad_kernel(group, extra, own_ref, a_ref, grad_ref, first_ref, mid_ref, cent_ref, out_ref):
    width = a_ref.shape[1]
    pad = out_ref.shape[1] - 3 * group
    row = lax.broadcasted_iota(jnp.int32, (pad, width), 0)
    small = jnp.where(row == 0, first_ref[0:1], 0.0)
    small = jnp.where(row == 1, mid_ref[0:1], small)
    small = jnp.where(row == 2, first_ref[1:2], small)
    small = jnp.where(row == 3, mid_ref[1:2], small)
    small = jnp.where(row == 4 + own_ref[1], cent_ref[0:1], small)
    out_ref[:, 3 * group :] = small.T
    for part in range(width // 256):
        piece = slice(part * 256, (part + 1) * 256)
        out_ref[piece, : 3 * group] = dot_tn(a_ref[:, piece], grad_ref[...])


def project_kernel(part_ref, w_ref, tok_ref, par_ref, table_ref, hidden_ref, packed_ref):
    hidden = tok_ref[...].astype(f32)
    for k in range(REPS):
        hidden = hidden + dot_nn(part_ref[k], w_ref[k])
    hidden_ref[...] = hidden
    normed, _ = stats_of(hidden)
    states = (normed * par_ref[1:2] + par_ref[3:4]).astype(bf16)
    packed_ref[...] = dot_nn(table_ref[...], states).astype(bf16)


def project_back_kernel(back_ref, w_ref, *refs):
    table_ref, hidden_ref, dy_ref, par_ref, dh_ref, dhb_ref, sum_ref, do_ref = refs
    grad = dot_nn(table_ref[...], back_ref[...])
    normed, inverse = stats_of(hidden_ref[...])
    sum_ref[...] = jnp.zeros_like(sum_ref)
    sum_ref[0:1] = jnp.sum(grad * normed, axis=0, keepdims=True)
    sum_ref[1:2] = jnp.sum(grad, axis=0, keepdims=True)
    dh = dy_ref[...].astype(f32) + norm_back(grad, normed, inverse, par_ref[1:2])
    dh_ref[...] = dh
    low = dh.astype(bf16)
    dhb_ref[...] = low
    for k in range(REPS):
        do_ref[k] = dot_nt(low, w_ref[k]).astype(bf16)


def proj_grad_kernel(part_ref, dhb_ref, out_ref):
    for k in range(REPS):
        out_ref[k] = dot_tn(part_ref[k], dhb_ref[...])


def tokens_grad_kernel(*refs):
    own_ref, from_x, from_y, upper, lower, tok_ref, par_ref, dh_ref, out_ref = refs
    half = upper.shape[0]
    parts = ((from_x, upper), (from_y, lower))
    for here, (direct, passed) in zip(halves(2 * half), parts):
        grad = own_ref[here] + direct[half:].astype(f32) + passed[...].astype(f32)
        normed, inverse = stats_of(tok_ref[here].astype(f32))
        back = norm_back(grad, normed, inverse, par_ref[0:1])
        out_ref[here] = (dh_ref[here] + back).astype(bf16)


def gelu_both(u):
    scale = (2.0 / jnp.pi) ** 0.5
    square = u * u
    half = 0.5 + 0.5 * jnp.tanh(u * (scale + scale * 0.044715 * square))
    active = u * half
    slope = half + (u - active) * half * (2.0 * scale + 2.0 * scale * 0.134145 * square)
    return active, slope


def fetch_slices(sources, in_buf, out_buf, sems):
    step = pl.program_id(0)

    @pl.when(step == 0)
    def _():
        for k, source_in, source_out in sources:
            pltpu.make_async_copy(source_in, in_buf.at[k], sems.at[0, k]).start()
            pltpu.make_async_copy(source_out, out_buf.at[k], sems.at[1, k]).start()

    _, source_in, source_out = sources[-1]
    pltpu.make_async_copy(source_in, in_buf.at[step], sems.at[0, step]).wait()
    pltpu.make_async_copy(source_out, out_buf.at[step], sems.at[1, step]).wait()


def gathered(ref):
    return [(k, ref.at[k, 0], ref.at[k, 1]) for k in range(REPS)]


def plane_slices(refs, rep):
    w_in, w_out, beside, above, diag_in, diag_out = refs
    return [
        (rep, w_in.at[0, 1], w_out.at[0, 1]),
        (rep ^ 1, beside.at[0], beside.at[1]),
        (rep ^ 2, above.at[0], above.at[1]),
        (rep ^ 3, diag_in, diag_out),
    ]


def halves(count):
    half = count // 2
    return [slice(0, half), slice(half, count)]


def expert_first_kernel(place_ref, par_ref, rows_a, rows_b, w_ref, gate_ref, *refs):
    act_ref, slope_ref, total_ref, low_a, low_b, rows_buf, in_buf, out_buf, sems = refs
    step = pl.program_id(0)
    count = rows_buf.shape[0]
    upper, lower = halves(count)

    @pl.when(step == 0)
    def _():
        rows_buf[upper] = rows_a[...]
        rows_buf[lower] = rows_b[...]
        total_ref[...] = jnp.zeros_like(total_ref)
        centroid = par_ref[pl.ds(4 + place_ref[1], 1)]
        weight = jnp.broadcast_to(centroid, (128, centroid.shape[1])).astype(bf16)
        for here in (upper, lower):
            gate_ref[here] = 1.0 / (1.0 + jnp.exp(-dot_nt(rows_buf[here], weight)))

    fetch_slices(gathered(w_ref), in_buf, out_buf, sems)
    active, slope = gelu_both(dot_nn(rows_buf[...], in_buf[step]))
    active = active.astype(bf16)
    act_ref[0] = active
    slope_ref[0] = slope.astype(bf16)
    total_ref[...] += dot_nt(active, out_buf[step])

    @pl.when(step == pl.num_programs(0) - 1)
    def _():
        low_a[...] = total_ref[upper].astype(bf16)
        low_b[...] = total_ref[lower].astype(bf16)


def expert_second_kernel(*refs):
    place_ref, rows_a, rows_b, first_ref, rec_a, rec_b, gate_ref, dy_a, dy_b, *refs = refs
    weights, refs = refs[:6], refs[6:]
    grads_ref, own_ref, z2_ref, dz_ref, low_a, low_b, *refs = refs
    zb_ref, db_ref, z2_acc, in_buf, out_buf, sems = refs
    step = pl.program_id(0)
    count = zb_ref.shape[0]
    upper, lower = halves(count)

    @pl.when(step == 0)
    def _():
        own = rows_a[...].astype(f32) + first_ref[upper] + rec_a[...].astype(f32)
        own_ref[...] = own
        zb_ref[upper] = own.astype(bf16)
        other = rows_b[...].astype(f32) + first_ref[lower] + rec_b[...].astype(f32)
        zb_ref[lower] = other.astype(bf16)
        db_ref[upper] = (gate_ref[upper, 0:1] * dy_a[...].astype(f32)).astype(bf16)
        db_ref[lower] = (gate_ref[lower, 0:1] * dy_b[...].astype(f32)).astype(bf16)
        z2_acc[...] = jnp.zeros_like(z2_acc)
        dz_ref[...] = jnp.zeros_like(dz_ref)

    fetch_slices(plane_slices(weights, place_ref[0]), in_buf, out_buf, sems)
    active, slope = gelu_both(dot_nn(zb_ref[...], in_buf[step]))
    active = active.astype(bf16)
    z2_acc[...] += dot_nt(active, out_buf[step])
    du = (slope * dot_nn(db_ref[...], out_buf[step])).astype(bf16)
    dz_ref[...] += dot_nt(du, in_buf[step])
    grads_ref[0, 0] = dot_tn(zb_ref[...], du).astype(bf16)
    grads_ref[0, 1] = dot_tn(db_ref[...], active).astype(bf16)

    @pl.when(step == REPS - 1)
    def _():
        own_ref[...] += z2_acc[upper]
        z2_ref[...] = z2_acc[lower].astype(bf16)
        low_a[...] = dz_ref[upper].astype(bf16)
        low_b[...] = dz_ref[lower].astype(bf16)


def expert_last_kernel(*refs):
    gate_ref, dy_a, dy_b, second_ref, rec_a, rec_b, slope_ref, act_ref, *refs = refs
    rows_a, rows_b, w_ref, grads_ref, own_ref, low_ref, *refs = refs
    rows_buf, db_ref, acc, in_buf, out_buf, sems = refs
    step = pl.program_id(0)
    count = db_ref.shape[0]
    upper, lower = halves(count)

    @pl.when(step == 0)
    def _():
        own = gate_ref[upper, 0:1] * dy_a[...].astype(f32) + second_ref[upper]
        own = own + rec_a[...].astype(f32)
        own_ref[...] = own
        db_ref[upper] = own.astype(bf16)
        other = gate_ref[lower, 0:1] * dy_b[...].astype(f32) + second_ref[lower]
        db_ref[lower] = (other + rec_b[...].astype(f32)).astype(bf16)
        rows_buf[upper] = rows_a[...]
        rows_buf[lower] = rows_b[...]
        acc[...] = jnp.zeros_like(acc)

    fetch_slices(gathered(w_ref), in_buf, out_buf, sems)
    du = (slope_ref[0].astype(f32) * dot_nn(db_ref[...], out_buf[step])).astype(bf16)
    acc[...] += dot_nt(du, in_buf[step])
    grads_ref[0, 0] = dot_tn(rows_buf[...], du).astype(bf16)
    grads_ref[0, 1] = dot_tn(db_ref[...], act_ref[0]).astype(bf16)

    @pl.when(step == REPS - 1)
    def _():
        own_ref[...] += acc[upper]
        low_ref[...] = acc[lower].astype(bf16)


def answer_kernel(final_ref, z2_ref, gate_ref, dy_ref, rows_ref, out_ref, score_ref, cent_ref):
    final = final_ref[...] + z2_ref[...].astype(f32)
    gate = gate_ref[...]
    out_ref[...] = (gate[:, 0:1] * final).astype(bf16)
    score = jnp.sum(dy_ref[...].astype(f32) * final, axis=1, keepdims=True)
    score = score * gate * (1.0 - gate)
    score_ref[...] = score
    cent_ref[...] = jnp.zeros_like(cent_ref)
    cent_ref[0:1] = jnp.sum(score[:, 0:1] * rows_ref[...].astype(f32), axis=0, keepdims=True)


def states_grad_kernel(place_ref, own_ref, low_ref, score_ref, par_ref, out_ref):
    centroid = par_ref[pl.ds(4 + place_ref[1], 1)]
    grad = own_ref[...] + low_ref[...].astype(f32) + score_ref[:, 0:1] * centroid
    out_ref[...] = grad.astype(bf16)


def layer_kernel(*refs):
    grads_ref, (in_ref, out_ref) = refs[0], refs[-2:]
    in_ref[0, 0] = grads_ref[0].astype(f32)
    out_ref[0, 0] = grads_ref[1].astype(f32)


def local(
    tokens,
    doc_ids,
    routes,
    norm_gains,
    norm_biases,
    w_qkv,
    w_proj,
    centroids,
    w_in,
    w_out,
    grad_out,
):
    rep = lax.axis_index("rep")
    parity = lax.axis_index("exp") % 2
    own_z = lax.axis_index("exp") // 2
    n_z = lax.axis_size("exp") // 2
    tok_rows = tokens.shape[1]
    width = tokens.shape[2]
    experts = centroids.shape[1]
    capacity = 2 * (5 * tok_rows // (8 * experts))
    group = width // REPS
    shard = w_qkv.shape[0]
    hidden_units = w_in.shape[3]
    seq_len = doc_ids.shape[1]
    half = tok_rows // 2
    place = jnp.stack([rep, own_z]).astype(jnp.int32)

    extra = 4 + experts
    pad = -extra % 128
    columns = 3 * group + extra + pad
    small = jnp.concatenate(
        [norm_gains, norm_biases, centroids, jnp.zeros((shard, pad), bf16)], axis=1
    )
    by_rep = w_qkv.reshape(shard, 3, REPS, group).transpose(2, 0, 1, 3)
    by_rep = by_rep.reshape(REPS, shard, 3 * group)
    small = jnp.concatenate([small, w_proj], axis=1)
    sends = jnp.concatenate(
        [by_rep, jnp.broadcast_to(small[None], (REPS,) + small.shape)], axis=2
    )
    got = exchange(sends, "rep")

    def assembled(blocks):
        blocks = both_cores(blocks, parity, 1).transpose(2, 0, 1, 3, 4)
        return blocks.reshape(width, blocks.shape[-1])

    own_tokens = tokens[0]
    tok_x, tok_y = over_x(own_tokens), over_y(own_tokens)
    along = gather_z(got[:, :, :columns])
    whole = assembled(along)
    proj_z = gather_z(after(got[:, :, columns:], along))
    params = whole[:, 3 * group :].T.astype(f32)

    seq = [own_tokens, tok_x, tok_y, over_y(tok_x[:half]), over_x(tok_y[half:])]

    own_in, own_out = after((w_in[0, 0], w_out[0, 0]), tok_x, tok_y, got)
    layer0 = lax.all_gather(jnp.stack([own_in, own_out]), "rep")
    expert = routes[0, :, 0]
    onehot = (expert[:, None] == jnp.arange(experts, dtype=jnp.int32)[None, :]).astype(jnp.int32)
    before = jnp.cumsum(onehot, axis=0) - onehot
    rank = jnp.sum(before * onehot, axis=1)
    slot = expert * capacity + rank % 2 * (capacity // 2) + rank // 2
    own_slots = experts * capacity
    slots = jnp.arange(own_slots, dtype=jnp.int32)
    table = (slots[:, None] == slot[None, :]).astype(bf16)
    table_t = (slots[None, :] == slot[:, None]).astype(bf16)
    spread = (2 * n_z, capacity // 2, width)

    def travel(rows):
        return exchange(rows.reshape(spread), "exp").reshape(own_slots, width)

    own_grad = grad_out[0]
    packed_grad = product(table, own_grad).astype(bf16)

    docs = doc_ids.reshape(1, seq_len)
    doc_col = doc_ids.reshape(seq_len, 1)
    attn_in, qkv, mixed_own, lse = call(
        functools.partial(attention_kernel, tok_rows, group),
        [
            ((seq_len, width), bf16),
            ((seq_len, 3 * group), bf16),
            ((seq_len, group), bf16),
            ((8, seq_len), f32),
        ],
        place,
        *seq,
        params,
        whole,
        doc_col,
        docs,
        specs={0: SMEM},
        scratch=[pltpu.VMEM((group, seq_len), bf16), pltpu.VMEM((group, tok_rows), f32)],
        cost=14,
    )
    mixed = exchange(mixed_own.reshape(REPS, tok_rows, group), "rep")
    proj_w = assembled(after(proj_z, lse)).reshape(REPS, group, width)
    own_second = after(jnp.stack([w_in[0, 1], w_out[0, 1]]), mixed)
    w1_x, w1_y = over_x(own_second), over_y(own_second)
    layer1 = [w_in, w_out, w1_x, w1_y, over_y(w1_x[0]), over_x(w1_y[1])]
    hidden, packed = call(
        project_kernel,
        [((tok_rows, width), f32), ((own_slots, width), bf16)],
        mixed,
        proj_w,
        own_tokens,
        params,
        table,
        cost=2,
    )

    all_slots = 2 * own_slots
    own_rows, all_rows = (own_slots, width), (all_slots, width)
    rows_a = travel(packed)
    rows_b = over_core(rows_a)
    dy_a = travel(after(packed_grad, rows_a))
    dy_b = over_core(dy_a)
    gate_shape = (all_slots, 128)
    by_slice = (REPS, all_slots, hidden_units)
    sliced = pl.BlockSpec((1, all_slots, hidden_units), lambda k: (k, 0, 0))
    slice_buf = pltpu.VMEM((REPS, width, hidden_units), bf16)
    slices = [slice_buf, slice_buf, pltpu.SemaphoreType.DMA((2, REPS))]
    gate, active0, slope0, first, low_a, low_b = call(
        expert_first_kernel,
        [
            (gate_shape, f32),
            (by_slice, bf16),
            (by_slice, bf16),
            (all_rows, f32),
            (own_rows, bf16),
            (own_rows, bf16),
        ],
        place,
        params,
        rows_a,
        rows_b,
        layer0,
        grid=(REPS,),
        specs={0: SMEM, 4: HBM},
        out_specs={1: sliced, 2: sliced},
        scratch=[pltpu.VMEM(all_rows, bf16)] + slices,
        limit=48,
        cost=14,
    )
    rec_a, rec_b = over_core(low_b), over_core(low_a)
    pair = (2, width, hidden_units)
    grads_shape = (REPS,) + pair
    grads_spec = pl.BlockSpec((1,) + pair, lambda k: (k, 0, 0, 0))
    weights1, own_final, z2_low, second, low_a, low_b = call(
        expert_second_kernel,
        [
            (grads_shape, bf16),
            (own_rows, f32),
            (own_rows, bf16),
            (all_rows, f32),
            (own_rows, bf16),
            (own_rows, bf16),
        ],
        place,
        rows_a,
        rows_b,
        first,
        rec_a,
        rec_b,
        gate,
        dy_a,
        dy_b,
        *layer1,
        grid=(REPS,),
        specs={0: SMEM, **{number: HBM for number in range(9, 15)}},
        out_specs={0: grads_spec},
        scratch=[pltpu.VMEM(all_rows, bf16)] * 2 + [pltpu.VMEM(all_rows, f32)] + slices,
        limit=60,
        cost=32,
    )
    grads1 = lax.psum_scatter(weights1, "rep", scatter_dimension=0)
    rec_a, rec_b = over_core(low_b), over_core(low_a)
    answer, score, grad_centroid = call(
        answer_kernel,
        [(own_rows, bf16), ((own_slots, 128), f32), ((8, width), f32)],
        own_final,
        over_core(z2_low),
        gate,
        dy_a,
        rows_a,
        specs={2: pl.BlockSpec((own_slots, 128), lambda _: (0, 0))},
        cost=2,
    )
    swapped = pl.BlockSpec((1,) + pair, lambda k: (k % 2 * 2 + k // 2, 0, 0, 0))
    weights0, own_first_grad, low = call(
        expert_last_kernel,
        [(grads_shape, bf16), (own_rows, f32), (own_rows, bf16)],
        gate,
        dy_a,
        dy_b,
        second,
        rec_a,
        rec_b,
        slope0,
        active0,
        rows_a,
        rows_b,
        layer0,
        grid=(REPS,),
        specs={6: sliced, 7: sliced, 10: HBM},
        out_specs={0: swapped},
        scratch=[pltpu.VMEM(all_rows, bf16)] * 2 + [pltpu.VMEM(all_rows, f32)] + slices,
        limit=60,
        cost=22,
    )
    grads0 = lax.psum_scatter(
        weights0, "rep", scatter_dimension=0, axis_index_groups=[[0, 2, 1, 3]]
    )
    (grad_inputs,) = call(
        states_grad_kernel,
        [(own_rows, bf16)],
        place,
        own_first_grad,
        over_core(low),
        score,
        params,
        specs={0: SMEM},
        cost=1,
    )
    grad_back = travel(grad_inputs)

    def layer_of(sub, grads, *held):
        shape = (1, 2, width, hidden_units)
        spec = pl.BlockSpec((1, 1, width, hidden_units), lambda _: (0, sub, 0, 0))
        return call(
            layer_kernel,
            [(shape, f32), (shape, f32)],
            grads,
            *held,
            specs={number: HBM for number in range(1, 1 + len(held))},
            out_specs={0: spec, 1: spec},
            alias={1: 0, 2: 1} if held else {},
            cost=2,
        )

    grad_hidden, grad_hidden_b, mid_sums, grad_mixed = call(
        project_back_kernel,
        [
            ((tok_rows, width), f32),
            ((tok_rows, width), bf16),
            ((8, width), f32),
            ((REPS, tok_rows, group), bf16),
        ],
        grad_back,
        proj_w,
        table_t,
        hidden,
        own_grad,
        params,
        cost=3,
    )
    grad_mixed = exchange(grad_mixed, "rep").reshape(seq_len, group)
    (proj_part,) = call(
        proj_grad_kernel, [((REPS, group, width), f32)], mixed, grad_hidden_b, cost=2
    )
    def own_parity(blocks):
        axis = blocks.ndim - 3
        sent = pick(blocks, 1 - parity, axis).astype(bf16)
        return pick(blocks, parity, axis) + over_core(sent).astype(f32)

    proj_part = own_parity(proj_part.reshape(REPS, n_z, 2, shard, width))
    proj_part = scatter_z(proj_part.transpose(1, 0, 2, 3)).astype(bf16)

    grad_qkv_b, first_sums, own_attn, to_x, to_y, left_y, left_x = call(
        functools.partial(attention_back_kernel, tok_rows, group),
        [
            ((seq_len, 3 * group), bf16),
            ((8, width), f32),
            ((tok_rows, width), f32),
            ((tok_rows, width), bf16),
            ((tok_rows, width), bf16),
            ((half, width), f32),
            ((half, width), f32),
        ],
        place,
        *seq,
        grad_mixed,
        whole,
        doc_col,
        docs,
        qkv,
        mixed_own,
        lse,
        specs={0: SMEM},
        scratch=[
            pltpu.VMEM((group, seq_len), bf16),
            pltpu.VMEM((group, tok_rows), f32),
            pltpu.VMEM((seq_len, group), f32),
            pltpu.VMEM((seq_len, group), f32),
            pltpu.VMEM((8, tok_rows), f32),
        ],
        limit=48,
        cost=17,
    )
    from_x, from_y = over_x(to_x), over_y(to_y)
    (qkv_part,) = call(
        functools.partial(qkv_grad_kernel, group, extra),
        [((width, columns), f32)],
        place,
        after(attn_in, proj_part),
        grad_qkv_b,
        first_sums,
        mid_sums,
        grad_centroid,
        specs={0: SMEM},
        cost=2,
    )
    qkv_part = own_parity(qkv_part.reshape(REPS, n_z, 2, shard, columns))
    qkv_part = scatter_z(qkv_part.transpose(1, 0, 2, 3)).astype(bf16)
    from_x, from_y = after((from_x, from_y), qkv_part)
    upper = over_y((left_y + from_x[:half].astype(f32)).astype(bf16))
    lower = over_x((left_x + from_y[:half].astype(f32)).astype(bf16))
    (grad_tokens,) = call(
        tokens_grad_kernel,
        [((tok_rows, width), bf16)],
        own_attn,
        from_x,
        from_y,
        upper,
        lower,
        own_tokens,
        params,
        grad_hidden,
        cost=2,
    )

    got = exchange(jnp.concatenate([qkv_part, proj_part], axis=2), "rep").astype(f32)
    returned = travel(after(answer, got))
    block_out = (hidden + product(table_t, returned)).astype(bf16)
    small_sum = jnp.sum(got[:, :, 3 * group : 3 * group + extra], axis=0)
    big = got[:, :, : 3 * group].reshape(REPS, shard, 3, group)
    grad_qkv = big.transpose(1, 2, 0, 3).reshape(shard, 3 * width)
    grad_proj = jnp.sum(got[:, :, columns:], axis=0)
    grad_w_in, grad_w_out = layer_of(0, grads0, *layer_of(1, grads1))
    return (
        block_out[None],
        grad_tokens[None],
        small_sum[:, 0:2],
        small_sum[:, 2:4],
        grad_qkv,
        grad_proj,
        small_sum[:, 4:],
        grad_w_in,
        grad_w_out,
    )


def solution(mesh):
    in_specs = (
        P("exp", "rep", None),
        P("exp", None),
        P("exp", "rep", None),
        P(("rep", "exp"), None),
        P(("rep", "exp"), None),
        P(("rep", "exp"), None),
        P(("rep", "exp"), None),
        P(("rep", "exp"), None),
        P("exp", None, None, "rep"),
        P("exp", None, None, "rep"),
        P("exp", "rep", None),
    )
    out_specs = (
        P("exp", "rep", None),
        P("exp", "rep", None),
        P(("rep", "exp"), None),
        P(("rep", "exp"), None),
        P(("rep", "exp"), None),
        P(("rep", "exp"), None),
        P(("rep", "exp"), None),
        P("exp", None, None, "rep"),
        P("exp", None, None, "rep"),
    )
    return jax.shard_map(local, mesh=mesh, in_specs=in_specs, out_specs=out_specs, check_vma=False)
```

```python
import functools

import jax
import jax.numpy as jnp
from jax import lax
from jax.experimental import pallas as pl
from jax.experimental.pallas import tpu as pltpu
from jax.sharding import PartitionSpec as P

HEAD_DIM = 64
REPS = 4
eps = 1e-05
neg_fill = -1e30
bf16 = jnp.bfloat16
f32 = jnp.float32


def flip(value, axis, mask):
    pairs = [(source, source ^ mask) for source in range(lax.axis_size(axis))]
    return lax.ppermute(value, axis, pairs)


def over_x(value):
    return flip(value, "rep", 1)


def over_y(value):
    return flip(value, "rep", 2)


def over_diag(value):
    return flip(value, "rep", 3)


def over_core(value):
    return flip(value, "exp", 1)


def shift_z(value, step):
    size = lax.axis_size("exp")
    if step % (size // 2) == 0:
        return value
    pairs = [(source, (source + 2 * step) % size) for source in range(size)]
    return lax.ppermute(value, "exp", pairs)


def pick(stacked, index, axis=0):
    return lax.dynamic_index_in_dim(stacked, index, axis=axis, keepdims=False)


def gather_z(block):
    n_z = lax.axis_size("exp") // 2
    own_z = lax.axis_index("exp") // 2
    out = jnp.zeros((n_z,) + block.shape, block.dtype)
    for step in range(n_z):
        out = lax.dynamic_update_index_in_dim(out, shift_z(block, step), (own_z - step) % n_z, 0)
    return out


def scatter_z(blocks):
    n_z = lax.axis_size("exp") // 2
    own_z = lax.axis_index("exp") // 2
    total = pick(blocks, own_z)
    for step in range(1, n_z):
        sent = pick(blocks, (own_z + step) % n_z).astype(bf16)
        total = total + shift_z(sent, step).astype(f32)
    return total


def both_cores(value, parity, axis):
    other = over_core(value)
    return jnp.stack(
        [jnp.where(parity == 0, value, other), jnp.where(parity == 0, other, value)], axis=axis
    )


def layer_norm(values, gain_vec, shift):
    average = jnp.mean(values, axis=-1, keepdims=True)
    centred = values - average
    inverse = lax.rsqrt(jnp.mean(centred * centred, axis=-1, keepdims=True) + eps)
    normed = centred * inverse
    return (normed * gain_vec + shift, normed, inverse)


def norm_back(gradient, normed, inverse, gain_vec):
    scaled = gradient * gain_vec
    bracket = (
        scaled
        - jnp.mean(scaled, axis=-1, keepdims=True)
        - normed * jnp.mean(scaled * normed, axis=-1, keepdims=True)
    )
    return inverse * bracket


def product(former, latter):
    return jnp.dot(former, latter, preferred_element_type=f32)


def after(values, *earlier):
    return lax.optimization_barrier((values, earlier))[0]


def exchange(blocks, axis):
    return lax.all_to_all(blocks, axis, split_axis=0, concat_axis=0, tiled=True)


MIB = 1 << 20


def whole_block(shape):
    return pl.BlockSpec(shape, lambda *_: (0,) * len(shape), pipeline_mode=pl.Buffered(1))


def call(
    body,
    outs,
    *operands,
    cost,
    grid=(1,),
    specs=None,
    out_specs=None,
    scratch=(),
    limit=40,
    alias=None,
    prefetch=0,
):
    shapes = [jax.ShapeDtypeStruct(shape, dtype) for shape, dtype in outs]
    in_specs = [whole_block(operand.shape) for operand in operands]
    for number, spec in (specs or {}).items():
        in_specs[number] = spec
    kinds = [whole_block(shape) for shape, _ in outs]
    for number, spec in (out_specs or {}).items():
        kinds[number] = spec
    return pl.pallas_call(
        body,
        out_shape=shapes,
        grid_spec=pltpu.PrefetchScalarGridSpec(
            num_scalar_prefetch=prefetch,
            grid=grid,
            in_specs=in_specs[prefetch:],
            out_specs=kinds,
            scratch_shapes=list(scratch),
        ),
        input_output_aliases=alias or {},
        compiler_params=pltpu.CompilerParams(vmem_limit_bytes=limit * MIB),
        cost_estimate=pl.CostEstimate(flops=cost * 1000**3, bytes_accessed=0, transcendentals=0),
    )(*operands)


SMEM = pl.BlockSpec(memory_space=pltpu.SMEM)
HBM = pl.BlockSpec(memory_space=pl.ANY)


def dot_nn(a, b):
    return lax.dot_general(a, b, (((1,), (0,)), ((), ())), preferred_element_type=f32)


def dot_nt(a, b):
    return lax.dot_general(a, b, (((1,), (1,)), ((), ())), preferred_element_type=f32)


def dot_tn(a, b):
    return lax.dot_general(a, b, (((0,), (0,)), ((), ())), preferred_element_type=f32)


def stats_of(values):
    average = jnp.mean(values, axis=-1, keepdims=True)
    centred = values - average
    inverse = lax.rsqrt(jnp.mean(centred * centred, axis=-1, keepdims=True) + eps)
    return centred * inverse, inverse


def head_lanes(values, head):
    lanes = lax.broadcasted_iota(jnp.int32, values.shape, 1)
    keep = (lanes >= head * HEAD_DIM) & (lanes < (head + 1) * HEAD_DIM)
    return jnp.where(keep, values, jnp.zeros_like(values))


def mask_of(doc_col, doc_row, index, rows):
    reach = (index + 1) * rows
    keys = lax.broadcasted_iota(jnp.int32, (reach, rows), 0)
    queries = lax.broadcasted_iota(jnp.int32, (reach, rows), 1) + index * rows
    same = doc_col[:reach] == doc_row[:, index * rows : reach]
    return jnp.where((keys <= queries) & same, 0.0, neg_fill)


def sequence_parts(refs, rows):
    own, beside, above, diag_a, diag_b = refs
    return [
        (own, 0, 0),
        (beside, 1, 0),
        (above, 2, 0),
        (diag_a, 3, 0),
        (diag_b, 3, rows // 2),
    ]


def sequence_parts(refs, rows):
    own, beside, above, diag_a, diag_b = refs
    return [
        (own, 0, 0),
        (beside, 1, 0),
        (above, 2, 0),
        (diag_a, 3, 0),
        (diag_b, 3, rows // 2),
    ]


def attention_kernel(rows, group, place_ref, *refs):
    toks, refs = refs[:5], refs[5:]
    par_ref, w_ref, col_ref, row_ref, a_ref, qkv_ref, o_ref, lse_ref, vt_ref, ot_ref = refs
    rep = place_ref[0]
    heads = group // HEAD_DIM
    gain, shift = par_ref[0:1], par_ref[2:3]
    for ref, k, first in sequence_parts(toks, rows):
        normed, _ = stats_of(ref[...].astype(f32))
        block = (normed * gain + shift).astype(bf16)
        count = ref.shape[0]
        here = pl.ds(pl.multiple_of((rep ^ k) * rows + first, count), count)
        a_ref[here] = block
        qkv_ref[here] = dot_nn(block, w_ref[:, : 3 * group]).astype(bf16)
    vt_ref[...] = qkv_ref[:, 2 * group :].T
    for index in range(REPS):
        reach = (index + 1) * rows
        here = pl.ds(index * rows, rows)
        bias = mask_of(col_ref[...], row_ref[...], index, rows)

        def one(head, carry):
            query = head_lanes(qkv_ref[here, :group] * jnp.asarray(HEAD_DIM**-0.5, bf16), head)
            score = dot_nt(qkv_ref[:reach, group : 2 * group], query) + bias
            top = jnp.max(score, axis=0, keepdims=True)
            weight = jnp.exp(score - top)
            total = jnp.sum(weight, axis=0, keepdims=True)
            lanes = pl.ds(pl.multiple_of(head * HEAD_DIM, HEAD_DIM), HEAD_DIM)
            ot_ref[lanes] = dot_nn(vt_ref[lanes, :reach], weight.astype(bf16)) / total
            lse_ref[pl.ds(head, 1), here] = top + jnp.log(total)
            return carry

        lax.fori_loop(0, heads, one, 0)
        o_ref[here] = ot_ref[...].T.astype(bf16)


def attention_back_kernel(rows, group, place_ref, *refs):
    toks, refs = refs[:5], refs[5:]
    do_ref, w_ref, col_ref, row_ref, qkv_ref, o_ref, lse_ref, *refs = refs
    grad_ref, sum_ref, own_ref, to_x, to_y, left_y, left_x, *refs = refs
    kt_ref, dq_ref, dk_ref, dv_ref, delta_ref = refs
    rep = place_ref[0]
    heads = group // HEAD_DIM
    half = rows // 2
    kt_ref[...] = qkv_ref[:, group : 2 * group].T
    dk_ref[...] = jnp.zeros_like(dk_ref)
    dv_ref[...] = jnp.zeros_like(dv_ref)
    for index in range(REPS):
        reach = (index + 1) * rows
        here = pl.ds(index * rows, rows)
        bias = mask_of(col_ref[...], row_ref[...], index, rows)
        both = (do_ref[here].astype(f32) * o_ref[here].astype(f32)).T
        for head in range(heads):
            delta_ref[head : head + 1] = jnp.sum(
                both[head * HEAD_DIM : (head + 1) * HEAD_DIM], axis=0, keepdims=True
            )

        def one(head, carry):
            query = head_lanes(qkv_ref[here, :group] * jnp.asarray(HEAD_DIM**-0.5, bf16), head)
            grad = head_lanes(do_ref[here], head)
            score = dot_nt(qkv_ref[:reach, group : 2 * group], query) + bias
            prob = jnp.exp(score - lse_ref[pl.ds(head, 1), here])
            dprob = dot_nt(qkv_ref[:reach, 2 * group :], grad)
            dscore = (prob * (dprob - delta_ref[pl.ds(head, 1)])).astype(bf16)
            dv_ref[:reach] += dot_nn(prob.astype(bf16), grad)
            dk_ref[:reach] += dot_nn(dscore, query)
            lanes = pl.ds(pl.multiple_of(head * HEAD_DIM, HEAD_DIM), HEAD_DIM)
            dq_ref[lanes] = dot_nn(kt_ref[lanes, :reach], dscore)
            return carry

        lax.fori_loop(0, heads, one, 0)
        grad_ref[here, :group] = (dq_ref[...].T * HEAD_DIM**-0.5).astype(bf16)
    grad_ref[:, group : 2 * group] = dk_ref[...].astype(bf16)
    grad_ref[:, 2 * group :] = dv_ref[...].astype(bf16)
    sum_ref[...] = jnp.zeros_like(sum_ref)
    for ref, k, first in sequence_parts(toks, rows):
        count = ref.shape[0]
        here = pl.ds(pl.multiple_of((rep ^ k) * rows + first, count), count)
        back = dot_nt(grad_ref[here], w_ref[:, : 3 * group])
        normed, _ = stats_of(ref[...].astype(f32))
        sum_ref[0:1] += jnp.sum(back * normed, axis=0, keepdims=True)
        sum_ref[1:2] += jnp.sum(back, axis=0, keepdims=True)
        if k == 0:
            own_ref[...] = back
        elif k == 1:
            to_x[half:] = back[:half].astype(bf16)
            left_x[...] = back[half:]
        elif k == 2:
            left_y[...] = back[:half]
            to_y[half:] = back[half:].astype(bf16)
        elif first == 0:
            to_x[:half] = back.astype(bf16)
        else:
            to_y[:half] = back.astype(bf16)


def qkv_grad_kernel(group, extra, own_ref, a_ref, grad_ref, first_ref, mid_ref, cent_ref, out_ref):
    width = a_ref.shape[1]
    pad = out_ref.shape[1] - 3 * group
    row = lax.broadcasted_iota(jnp.int32, (pad, width), 0)
    small = jnp.where(row == 0, first_ref[0:1], 0.0)
    small = jnp.where(row == 1, mid_ref[0:1], small)
    small = jnp.where(row == 2, first_ref[1:2], small)
    small = jnp.where(row == 3, mid_ref[1:2], small)
    small = jnp.where(row == 4 + own_ref[1], cent_ref[0:1], small)
    out_ref[:, 3 * group :] = small.T
    for part in range(width // 256):
        piece = slice(part * 256, (part + 1) * 256)
        out_ref[piece, : 3 * group] = dot_tn(a_ref[:, piece], grad_ref[...])


def project_kernel(part_ref, w_ref, tok_ref, par_ref, table_ref, hidden_ref, packed_ref):
    hidden = tok_ref[...].astype(f32)
    for k in range(REPS):
        hidden = hidden + dot_nn(part_ref[k], w_ref[k])
    hidden_ref[...] = hidden
    normed, _ = stats_of(hidden)
    states = (normed * par_ref[1:2] + par_ref[3:4]).astype(bf16)
    packed_ref[...] = dot_nn(table_ref[...], states).astype(bf16)


def project_back_kernel(back_ref, w_ref, *refs):
    table_ref, hidden_ref, dy_ref, par_ref, dh_ref, dhb_ref, sum_ref, do_ref = refs
    grad = dot_nn(table_ref[...], back_ref[...])
    normed, inverse = stats_of(hidden_ref[...])
    sum_ref[...] = jnp.zeros_like(sum_ref)
    sum_ref[0:1] = jnp.sum(grad * normed, axis=0, keepdims=True)
    sum_ref[1:2] = jnp.sum(grad, axis=0, keepdims=True)
    dh = dy_ref[...].astype(f32) + norm_back(grad, normed, inverse, par_ref[1:2])
    dh_ref[...] = dh
    low = dh.astype(bf16)
    dhb_ref[...] = low
    for k in range(REPS):
        do_ref[k] = dot_nt(low, w_ref[k]).astype(bf16)


def proj_grad_kernel(part_ref, dhb_ref, out_ref):
    for k in range(REPS):
        out_ref[k] = dot_tn(part_ref[k], dhb_ref[...])


def tokens_grad_kernel(*refs):
    own_ref, from_x, from_y, upper, lower, tok_ref, par_ref, dh_ref, out_ref = refs
    half = upper.shape[0]
    parts = ((from_x, upper), (from_y, lower))
    for here, (direct, passed) in zip(halves(2 * half), parts):
        grad = own_ref[here] + direct[half:].astype(f32) + passed[...].astype(f32)
        normed, inverse = stats_of(tok_ref[here].astype(f32))
        back = norm_back(grad, normed, inverse, par_ref[0:1])
        out_ref[here] = (dh_ref[here] + back).astype(bf16)


def gelu_both(u):
    scale = (2.0 / jnp.pi) ** 0.5
    square = u * u
    half = 0.5 + 0.5 * jnp.tanh(u * (scale + scale * 0.044715 * square))
    active = u * half
    slope = half + (u - active) * half * (2.0 * scale + 2.0 * scale * 0.134145 * square)
    return active, slope


def fetch_slices(sources, in_buf, out_buf, sems):
    step = pl.program_id(0)

    @pl.when(step == 0)
    def _():
        for k, source_in, source_out in sources:
            pltpu.make_async_copy(source_in, in_buf.at[k], sems.at[0, k]).start()
            pltpu.make_async_copy(source_out, out_buf.at[k], sems.at[1, k]).start()

    _, source_in, source_out = sources[-1]
    pltpu.make_async_copy(source_in, in_buf.at[step], sems.at[0, step]).wait()
    pltpu.make_async_copy(source_out, out_buf.at[step], sems.at[1, step]).wait()


def gathered(ref):
    return [(k, ref.at[k, 0], ref.at[k, 1]) for k in range(REPS)]


def near_slices(refs):
    w_in, w_out, beside, above = refs
    return [
        (0, w_in.at[0, 1], w_out.at[0, 1]),
        (1, beside.at[0], beside.at[1]),
        (2, above.at[0], above.at[1]),
    ]


def halves(count):
    half = count // 2
    return [slice(0, half), slice(half, count)]


def expert_first_kernel(place_ref, par_ref, rows_a, rows_b, w_ref, gate_ref, *refs):
    act_ref, slope_ref, total_ref, low_a, low_b, rows_buf, in_buf, out_buf, sems = refs
    step = pl.program_id(0)
    count = rows_buf.shape[0]
    upper, lower = halves(count)

    @pl.when(step == 0)
    def _():
        rows_buf[upper] = rows_a[...]
        rows_buf[lower] = rows_b[...]
        total_ref[...] = jnp.zeros_like(total_ref)
        centroid = par_ref[pl.ds(4 + place_ref[1], 1)]
        weight = jnp.broadcast_to(centroid, (128, centroid.shape[1])).astype(bf16)
        for here in (upper, lower):
            gate_ref[here] = 1.0 / (1.0 + jnp.exp(-dot_nt(rows_buf[here], weight)))

    fetch_slices(gathered(w_ref), in_buf, out_buf, sems)
    active, slope = gelu_both(dot_nn(rows_buf[...], in_buf[step]))
    active = active.astype(bf16)
    act_ref[0] = active
    slope_ref[0] = slope.astype(bf16)
    total_ref[...] += dot_nt(active, out_buf[step])

    @pl.when(step == pl.num_programs(0) - 1)
    def _():
        low_a[...] = total_ref[upper].astype(bf16)
        low_b[...] = total_ref[lower].astype(bf16)


def second_step(step, zb_ref, db_ref, bufs, grads_ref, z2_ref, dz_ref):
    in_buf, out_buf = bufs
    active, slope = gelu_both(dot_nn(zb_ref[...], in_buf[step]))
    active = active.astype(bf16)
    z2_ref[...] += dot_nt(active, out_buf[step])
    du = (slope * dot_nn(db_ref[...], out_buf[step])).astype(bf16)
    dz_ref[...] += dot_nt(du, in_buf[step])
    grads_ref[0, 0] = dot_tn(zb_ref[...], du).astype(bf16)
    grads_ref[0, 1] = dot_tn(db_ref[...], active).astype(bf16)


def expert_near_kernel(*refs):
    _, rows_a, rows_b, first_ref, rec_a, rec_b, gate_ref, dy_a, dy_b, *refs = refs
    weights, refs = refs[:4], refs[4:]
    grads_ref, own_ref, zb_ref, db_ref, z2_ref, dz_ref, in_buf, out_buf, sems = refs
    step = pl.program_id(0)
    upper, lower = halves(zb_ref.shape[0])

    @pl.when(step == 0)
    def _():
        own = rows_a[...].astype(f32) + first_ref[upper] + rec_a[...].astype(f32)
        own_ref[...] = own
        zb_ref[upper] = own.astype(bf16)
        other = rows_b[...].astype(f32) + first_ref[lower] + rec_b[...].astype(f32)
        zb_ref[lower] = other.astype(bf16)
        db_ref[upper] = (gate_ref[upper, 0:1] * dy_a[...].astype(f32)).astype(bf16)
        db_ref[lower] = (gate_ref[lower, 0:1] * dy_b[...].astype(f32)).astype(bf16)
        z2_ref[...] = jnp.zeros_like(z2_ref)
        dz_ref[...] = jnp.zeros_like(dz_ref)

    fetch_slices(near_slices(weights), in_buf, out_buf, sems)
    second_step(step, zb_ref, db_ref, (in_buf, out_buf), grads_ref, z2_ref, dz_ref)


def expert_far_kernel(*refs):
    _, zb_ref, db_ref, z2_in, dz_in, stream_ref, diag_in, diag_out, _, *refs = refs
    grads_ref, own_ref, z2_low, dz_ref, low_a, low_b, z2_ref, in_buf, out_buf, sems = refs
    upper, lower = halves(zb_ref.shape[0])
    z2_ref[...] = z2_in[...]
    dz_ref[...] = dz_in[...]
    fetch_slices([(0, diag_in, diag_out)], in_buf, out_buf, sems)
    second_step(0, zb_ref, db_ref, (in_buf, out_buf), grads_ref, z2_ref, dz_ref)
    own_ref[...] = stream_ref[...] + z2_ref[upper]
    z2_low[...] = z2_ref[lower].astype(bf16)
    low_a[...] = dz_ref[upper].astype(bf16)
    low_b[...] = dz_ref[lower].astype(bf16)


def expert_last_kernel(*refs):
    gate_ref, dy_a, dy_b, second_ref, rec_a, rec_b, slope_ref, act_ref, *refs = refs
    rows_a, rows_b, w_ref, grads_ref, own_ref, low_ref, *refs = refs
    rows_buf, db_ref, acc, in_buf, out_buf, sems = refs
    step = pl.program_id(0)
    count = db_ref.shape[0]
    upper, lower = halves(count)

    @pl.when(step == 0)
    def _():
        own = gate_ref[upper, 0:1] * dy_a[...].astype(f32) + second_ref[upper]
        own = own + rec_a[...].astype(f32)
        own_ref[...] = own
        db_ref[upper] = own.astype(bf16)
        other = gate_ref[lower, 0:1] * dy_b[...].astype(f32) + second_ref[lower]
        db_ref[lower] = (other + rec_b[...].astype(f32)).astype(bf16)
        rows_buf[upper] = rows_a[...]
        rows_buf[lower] = rows_b[...]
        acc[...] = jnp.zeros_like(acc)

    fetch_slices(gathered(w_ref), in_buf, out_buf, sems)
    du = (slope_ref[0].astype(f32) * dot_nn(db_ref[...], out_buf[step])).astype(bf16)
    acc[...] += dot_nt(du, in_buf[step])
    grads_ref[0, 0] = dot_tn(rows_buf[...], du).astype(bf16)
    grads_ref[0, 1] = dot_tn(db_ref[...], act_ref[0]).astype(bf16)

    @pl.when(step == REPS - 1)
    def _():
        own_ref[...] += acc[upper]
        low_ref[...] = acc[lower].astype(bf16)


def answer_kernel(final_ref, z2_ref, gate_ref, dy_ref, rows_ref, out_ref, score_ref, cent_ref):
    final = final_ref[...] + z2_ref[...].astype(f32)
    gate = gate_ref[...]
    out_ref[...] = (gate[:, 0:1] * final).astype(bf16)
    score = jnp.sum(dy_ref[...].astype(f32) * final, axis=1, keepdims=True)
    score = score * gate * (1.0 - gate)
    score_ref[...] = score
    cent_ref[...] = jnp.zeros_like(cent_ref)
    cent_ref[0:1] = jnp.sum(score[:, 0:1] * rows_ref[...].astype(f32), axis=0, keepdims=True)


def states_grad_kernel(place_ref, own_ref, low_ref, score_ref, par_ref, out_ref):
    centroid = par_ref[pl.ds(4 + place_ref[1], 1)]
    grad = own_ref[...] + low_ref[...].astype(f32) + score_ref[:, 0:1] * centroid
    out_ref[...] = grad.astype(bf16)


def layer_kernel(*refs):
    grads_ref, (in_ref, out_ref) = refs[0], refs[-2:]
    in_ref[0, 0] = grads_ref[0].astype(f32)
    out_ref[0, 0] = grads_ref[1].astype(f32)


def local(
    tokens,
    doc_ids,
    routes,
    norm_gains,
    norm_biases,
    w_qkv,
    w_proj,
    centroids,
    w_in,
    w_out,
    grad_out,
):
    rep = lax.axis_index("rep")
    parity = lax.axis_index("exp") % 2
    own_z = lax.axis_index("exp") // 2
    n_z = lax.axis_size("exp") // 2
    tok_rows = tokens.shape[1]
    width = tokens.shape[2]
    experts = centroids.shape[1]
    capacity = 2 * (5 * tok_rows // (8 * experts))
    group = width // REPS
    shard = w_qkv.shape[0]
    hidden_units = w_in.shape[3]
    seq_len = doc_ids.shape[1]
    half = tok_rows // 2
    place = jnp.stack([rep, own_z]).astype(jnp.int32)

    extra = 4 + experts
    pad = -extra % 128
    columns = 3 * group + extra + pad
    small = jnp.concatenate(
        [norm_gains, norm_biases, centroids, jnp.zeros((shard, pad), bf16)], axis=1
    )
    by_rep = w_qkv.reshape(shard, 3, REPS, group).transpose(2, 0, 1, 3)
    by_rep = by_rep.reshape(REPS, shard, 3 * group)
    small = jnp.concatenate([small, w_proj], axis=1)
    sends = jnp.concatenate(
        [by_rep, jnp.broadcast_to(small[None], (REPS,) + small.shape)], axis=2
    )
    got = exchange(sends, "rep")

    def assembled(blocks):
        blocks = both_cores(blocks, parity, 1).transpose(2, 0, 1, 3, 4)
        return blocks.reshape(width, blocks.shape[-1])

    own_tokens = tokens[0]
    tok_x, tok_y = over_x(own_tokens), over_y(own_tokens)
    along = gather_z(got[:, :, :columns])
    whole = assembled(along)
    proj_z = gather_z(after(got[:, :, columns:], along))
    params = whole[:, 3 * group :].T.astype(f32)

    seq = [own_tokens, tok_x, tok_y, over_y(tok_x[:half]), over_x(tok_y[half:])]

    own_in, own_out = after((w_in[0, 0], w_out[0, 0]), tok_x, tok_y, got)
    layer0 = lax.all_gather(jnp.stack([own_in, own_out]), "rep")
    expert = routes[0, :, 0]
    onehot = (expert[:, None] == jnp.arange(experts, dtype=jnp.int32)[None, :]).astype(jnp.int32)
    before = jnp.cumsum(onehot, axis=0) - onehot
    rank = jnp.sum(before * onehot, axis=1)
    slot = expert * capacity + rank % 2 * (capacity // 2) + rank // 2
    own_slots = experts * capacity
    slots = jnp.arange(own_slots, dtype=jnp.int32)
    table = (slots[:, None] == slot[None, :]).astype(bf16)
    table_t = (slots[None, :] == slot[:, None]).astype(bf16)
    spread = (2 * n_z, capacity // 2, width)

    def travel(rows):
        return exchange(rows.reshape(spread), "exp").reshape(own_slots, width)

    own_grad = grad_out[0]
    packed_grad = product(table, own_grad).astype(bf16)

    docs = doc_ids.reshape(1, seq_len)
    doc_col = doc_ids.reshape(seq_len, 1)
    attn_in, qkv, mixed_own, lse = call(
        functools.partial(attention_kernel, tok_rows, group),
        [
            ((seq_len, width), bf16),
            ((seq_len, 3 * group), bf16),
            ((seq_len, group), bf16),
            ((8, seq_len), f32),
        ],
        place,
        *seq,
        params,
        whole,
        doc_col,
        docs,
        specs={0: SMEM},
        scratch=[pltpu.VMEM((group, seq_len), bf16), pltpu.VMEM((group, tok_rows), f32)],
        cost=14,
    )
    mixed = exchange(mixed_own.reshape(REPS, tok_rows, group), "rep")
    proj_w = assembled(after(proj_z, lse)).reshape(REPS, group, width)
    own_second = after(jnp.stack([w_in[0, 1], w_out[0, 1]]), mixed)
    w1_x, w1_y = over_x(own_second), over_y(own_second)
    hidden, packed = call(
        project_kernel,
        [((tok_rows, width), f32), ((own_slots, width), bf16)],
        mixed,
        proj_w,
        own_tokens,
        params,
        table,
        cost=2,
    )

    all_slots = 2 * own_slots
    own_rows, all_rows = (own_slots, width), (all_slots, width)
    rows_a = travel(packed)
    rows_b = over_core(rows_a)
    dy_a = travel(after(packed_grad, rows_a))
    dy_b = over_core(dy_a)
    gate_shape = (all_slots, 128)
    by_slice = (REPS, all_slots, hidden_units)
    sliced = pl.BlockSpec((1, all_slots, hidden_units), lambda k: (k, 0, 0))
    slice_buf = pltpu.VMEM((REPS, width, hidden_units), bf16)
    slices = [slice_buf, slice_buf, pltpu.SemaphoreType.DMA((2, REPS))]
    gate, active0, slope0, first, low_a, low_b = call(
        expert_first_kernel,
        [
            (gate_shape, f32),
            (by_slice, bf16),
            (by_slice, bf16),
            (all_rows, f32),
            (own_rows, bf16),
            (own_rows, bf16),
        ],
        place,
        params,
        rows_a,
        rows_b,
        layer0,
        grid=(REPS,),
        specs={0: SMEM, 4: HBM},
        out_specs={1: sliced, 2: sliced},
        scratch=[pltpu.VMEM(all_rows, bf16)] + slices,
        limit=48,
        cost=1,
    )
    rec_a, rec_b = over_core(low_b), over_core(low_a)
    w1_x, w1_y = after((w1_x, w1_y), low_a)
    diag_in, diag_out = over_y(w1_x[0]), over_x(w1_y[1])
    pair = (2, width, hidden_units)
    grads_shape = (REPS,) + pair
    grads_spec = pl.BlockSpec((1,) + pair, lambda k: (k, 0, 0, 0))
    def by_place(first):
        return pl.BlockSpec((1,) + pair, lambda k, at: (at[0] ^ (first + k), 0, 0, 0))

    def some_slices(count):
        buf = pltpu.VMEM((count, width, hidden_units), bf16)
        return [buf, buf, pltpu.SemaphoreType.DMA((2, count))]

    weights1, z1_own, stream1, branch1, z2_sum, dz_sum = call(
        expert_near_kernel,
        [
            (grads_shape, bf16),
            (own_rows, f32),
            (all_rows, bf16),
            (all_rows, bf16),
            (all_rows, f32),
            (all_rows, f32),
        ],
        place,
        rows_a,
        rows_b,
        first,
        rec_a,
        rec_b,
        gate,
        dy_a,
        dy_b,
        w_in,
        w_out,
        w1_x,
        w1_y,
        grid=(3,),
        specs={number: HBM for number in range(9, 13)},
        out_specs={0: by_place(0)},
        scratch=some_slices(3),
        limit=56,
        cost=22,
        prefetch=1,
    )
    weights1, own_final, z2_low, second, low_a, low_b = call(
        expert_far_kernel,
        [
            (grads_shape, bf16),
            (own_rows, f32),
            (own_rows, bf16),
            (all_rows, f32),
            (own_rows, bf16),
            (own_rows, bf16),
        ],
        place,
        stream1,
        branch1,
        z2_sum,
        dz_sum,
        z1_own,
        diag_in,
        diag_out,
        weights1,
        specs={6: HBM, 7: HBM, 8: HBM},
        out_specs={0: by_place(3)},
        alias={8: 0},
        scratch=[pltpu.VMEM(all_rows, f32)] + some_slices(1),
        limit=56,
        cost=9,
        prefetch=1,
    )
    grads1 = lax.psum_scatter(weights1, "rep", scatter_dimension=0)
    rec_a, rec_b = over_core(low_b), over_core(low_a)
    answer, score, grad_centroid = call(
        answer_kernel,
        [(own_rows, bf16), ((own_slots, 128), f32), ((8, width), f32)],
        own_final,
        over_core(z2_low),
        gate,
        dy_a,
        rows_a,
        specs={2: pl.BlockSpec((own_slots, 128), lambda _: (0, 0))},
        cost=2,
    )
    swapped = pl.BlockSpec((1,) + pair, lambda k: (k % 2 * 2 + k // 2, 0, 0, 0))
    weights0, own_first_grad, low = call(
        expert_last_kernel,
        [(grads_shape, bf16), (own_rows, f32), (own_rows, bf16)],
        gate,
        dy_a,
        dy_b,
        second,
        rec_a,
        rec_b,
        slope0,
        active0,
        rows_a,
        rows_b,
        layer0,
        grid=(REPS,),
        specs={6: sliced, 7: sliced, 10: HBM},
        out_specs={0: swapped},
        scratch=[pltpu.VMEM(all_rows, bf16)] * 2 + [pltpu.VMEM(all_rows, f32)] + slices,
        limit=60,
        cost=22,
    )
    grads0 = lax.psum_scatter(
        weights0, "rep", scatter_dimension=0, axis_index_groups=[[0, 2, 1, 3]]
    )
    (grad_inputs,) = call(
        states_grad_kernel,
        [(own_rows, bf16)],
        place,
        own_first_grad,
        over_core(low),
        score,
        params,
        specs={0: SMEM},
        cost=1,
    )
    grad_back = travel(grad_inputs)

    def layer_of(sub, grads, *held):
        shape = (1, 2, width, hidden_units)
        spec = pl.BlockSpec((1, 1, width, hidden_units), lambda _: (0, sub, 0, 0))
        return call(
            layer_kernel,
            [(shape, f32), (shape, f32)],
            grads,
            *held,
            specs={number: HBM for number in range(1, 1 + len(held))},
            out_specs={0: spec, 1: spec},
            alias={1: 0, 2: 1} if held else {},
            cost=2,
        )

    grad_hidden, grad_hidden_b, mid_sums, grad_mixed = call(
        project_back_kernel,
        [
            ((tok_rows, width), f32),
            ((tok_rows, width), bf16),
            ((8, width), f32),
            ((REPS, tok_rows, group), bf16),
        ],
        grad_back,
        proj_w,
        table_t,
        hidden,
        own_grad,
        params,
        cost=3,
    )
    grad_mixed = exchange(grad_mixed, "rep").reshape(seq_len, group)
    (proj_part,) = call(
        proj_grad_kernel, [((REPS, group, width), f32)], mixed, grad_hidden_b, cost=2
    )
    def own_parity(blocks):
        axis = blocks.ndim - 3
        sent = pick(blocks, 1 - parity, axis).astype(bf16)
        return pick(blocks, parity, axis) + over_core(sent).astype(f32)

    proj_part = own_parity(proj_part.reshape(REPS, n_z, 2, shard, width))
    proj_part = scatter_z(proj_part.transpose(1, 0, 2, 3)).astype(bf16)

    grad_qkv_b, first_sums, own_attn, to_x, to_y, left_y, left_x = call(
        functools.partial(attention_back_kernel, tok_rows, group),
        [
            ((seq_len, 3 * group), bf16),
            ((8, width), f32),
            ((tok_rows, width), f32),
            ((tok_rows, width), bf16),
            ((tok_rows, width), bf16),
            ((half, width), f32),
            ((half, width), f32),
        ],
        place,
        *seq,
        grad_mixed,
        whole,
        doc_col,
        docs,
        qkv,
        mixed_own,
        lse,
        specs={0: SMEM},
        scratch=[
            pltpu.VMEM((group, seq_len), bf16),
            pltpu.VMEM((group, tok_rows), f32),
            pltpu.VMEM((seq_len, group), f32),
            pltpu.VMEM((seq_len, group), f32),
            pltpu.VMEM((8, tok_rows), f32),
        ],
        limit=48,
        cost=17,
    )
    from_x, from_y = over_x(to_x), over_y(to_y)
    (qkv_part,) = call(
        functools.partial(qkv_grad_kernel, group, extra),
        [((width, columns), f32)],
        place,
        after(attn_in, proj_part),
        grad_qkv_b,
        first_sums,
        mid_sums,
        grad_centroid,
        specs={0: SMEM},
        cost=2,
    )
    qkv_part = own_parity(qkv_part.reshape(REPS, n_z, 2, shard, columns))
    qkv_part = scatter_z(qkv_part.transpose(1, 0, 2, 3)).astype(bf16)
    from_x, from_y = after((from_x, from_y), qkv_part)
    upper = over_y((left_y + from_x[:half].astype(f32)).astype(bf16))
    lower = over_x((left_x + from_y[:half].astype(f32)).astype(bf16))
    (grad_tokens,) = call(
        tokens_grad_kernel,
        [((tok_rows, width), bf16)],
        own_attn,
        from_x,
        from_y,
        upper,
        lower,
        own_tokens,
        params,
        grad_hidden,
        cost=2,
    )

    got = exchange(jnp.concatenate([qkv_part, proj_part], axis=2), "rep").astype(f32)
    returned = travel(after(answer, got))
    block_out = (hidden + product(table_t, returned)).astype(bf16)
    small_sum = jnp.sum(got[:, :, 3 * group : 3 * group + extra], axis=0)
    big = got[:, :, : 3 * group].reshape(REPS, shard, 3, group)
    grad_qkv = big.transpose(1, 2, 0, 3).reshape(shard, 3 * width)
    grad_proj = jnp.sum(got[:, :, columns:], axis=0)
    grad_w_in, grad_w_out = layer_of(0, grads0, *layer_of(1, grads1))
    return (
        block_out[None],
        grad_tokens[None],
        small_sum[:, 0:2],
        small_sum[:, 2:4],
        grad_qkv,
        grad_proj,
        small_sum[:, 4:],
        grad_w_in,
        grad_w_out,
    )


def solution(mesh):
    in_specs = (
        P("exp", "rep", None),
        P("exp", None),
        P("exp", "rep", None),
        P(("rep", "exp"), None),
        P(("rep", "exp"), None),
        P(("rep", "exp"), None),
        P(("rep", "exp"), None),
        P(("rep", "exp"), None),
        P("exp", None, None, "rep"),
        P("exp", None, None, "rep"),
        P("exp", "rep", None),
    )
    out_specs = (
        P("exp", "rep", None),
        P("exp", "rep", None),
        P(("rep", "exp"), None),
        P(("rep", "exp"), None),
        P(("rep", "exp"), None),
        P(("rep", "exp"), None),
        P(("rep", "exp"), None),
        P("exp", None, None, "rep"),
        P("exp", None, None, "rep"),
    )
    return jax.shard_map(local, mesh=mesh, in_specs=in_specs, out_specs=out_specs, check_vma=False)
```

```python
import functools

import jax
import jax.numpy as jnp
from jax import lax
from jax.experimental import pallas as pl
from jax.experimental.pallas import tpu as pltpu
from jax.sharding import PartitionSpec as P

HEAD_DIM = 64
REPS = 4
eps = 1e-05
neg_fill = -1e30
bf16 = jnp.bfloat16
f32 = jnp.float32


def flip(value, axis, mask):
    pairs = [(source, source ^ mask) for source in range(lax.axis_size(axis))]
    return lax.ppermute(value, axis, pairs)


def over_x(value):
    return flip(value, "rep", 1)


def over_y(value):
    return flip(value, "rep", 2)


def over_diag(value):
    return flip(value, "rep", 3)


def over_core(value):
    return flip(value, "exp", 1)


def shift_z(value, step):
    size = lax.axis_size("exp")
    if step % (size // 2) == 0:
        return value
    pairs = [(source, (source + 2 * step) % size) for source in range(size)]
    return lax.ppermute(value, "exp", pairs)


def pick(stacked, index, axis=0):
    return lax.dynamic_index_in_dim(stacked, index, axis=axis, keepdims=False)


def gather_z(block):
    n_z = lax.axis_size("exp") // 2
    own_z = lax.axis_index("exp") // 2
    out = jnp.zeros((n_z,) + block.shape, block.dtype)
    for step in range(n_z):
        out = lax.dynamic_update_index_in_dim(out, shift_z(block, step), (own_z - step) % n_z, 0)
    return out


def scatter_z(blocks):
    n_z = lax.axis_size("exp") // 2
    own_z = lax.axis_index("exp") // 2
    total = pick(blocks, own_z)
    for step in range(1, n_z):
        sent = pick(blocks, (own_z + step) % n_z).astype(bf16)
        total = total + shift_z(sent, step).astype(f32)
    return total


def both_cores(value, parity, axis):
    other = over_core(value)
    return jnp.stack(
        [jnp.where(parity == 0, value, other), jnp.where(parity == 0, other, value)], axis=axis
    )


def layer_norm(values, gain_vec, shift):
    average = jnp.mean(values, axis=-1, keepdims=True)
    centred = values - average
    inverse = lax.rsqrt(jnp.mean(centred * centred, axis=-1, keepdims=True) + eps)
    normed = centred * inverse
    return (normed * gain_vec + shift, normed, inverse)


def norm_back(gradient, normed, inverse, gain_vec):
    scaled = gradient * gain_vec
    bracket = (
        scaled
        - jnp.mean(scaled, axis=-1, keepdims=True)
        - normed * jnp.mean(scaled * normed, axis=-1, keepdims=True)
    )
    return inverse * bracket


def product(former, latter):
    return jnp.dot(former, latter, preferred_element_type=f32)


def after(values, *earlier):
    return lax.optimization_barrier((values, earlier))[0]


def exchange(blocks, axis):
    return lax.all_to_all(blocks, axis, split_axis=0, concat_axis=0, tiled=True)


MIB = 1 << 20


def whole_block(shape):
    return pl.BlockSpec(shape, lambda *_: (0,) * len(shape), pipeline_mode=pl.Buffered(1))


def call(
    body,
    outs,
    *operands,
    cost,
    grid=(1,),
    specs=None,
    out_specs=None,
    scratch=(),
    limit=40,
    alias=None,
    prefetch=0,
):
    shapes = [jax.ShapeDtypeStruct(shape, dtype) for shape, dtype in outs]
    in_specs = [whole_block(operand.shape) for operand in operands]
    for number, spec in (specs or {}).items():
        in_specs[number] = spec
    kinds = [whole_block(shape) for shape, _ in outs]
    for number, spec in (out_specs or {}).items():
        kinds[number] = spec
    return pl.pallas_call(
        body,
        out_shape=shapes,
        grid_spec=pltpu.PrefetchScalarGridSpec(
            num_scalar_prefetch=prefetch,
            grid=grid,
            in_specs=in_specs[prefetch:],
            out_specs=kinds,
            scratch_shapes=list(scratch),
        ),
        input_output_aliases=alias or {},
        compiler_params=pltpu.CompilerParams(vmem_limit_bytes=limit * MIB),
        cost_estimate=pl.CostEstimate(flops=cost * 1000**3, bytes_accessed=0, transcendentals=0),
    )(*operands)


SMEM = pl.BlockSpec(memory_space=pltpu.SMEM)
HBM = pl.BlockSpec(memory_space=pl.ANY)


def dot_nn(a, b):
    return lax.dot_general(a, b, (((1,), (0,)), ((), ())), preferred_element_type=f32)


def dot_nt(a, b):
    return lax.dot_general(a, b, (((1,), (1,)), ((), ())), preferred_element_type=f32)


def dot_tn(a, b):
    return lax.dot_general(a, b, (((0,), (0,)), ((), ())), preferred_element_type=f32)


def stats_of(values):
    average = jnp.mean(values, axis=-1, keepdims=True)
    centred = values - average
    inverse = lax.rsqrt(jnp.mean(centred * centred, axis=-1, keepdims=True) + eps)
    return centred * inverse, inverse


def head_lanes(values, head):
    lanes = lax.broadcasted_iota(jnp.int32, values.shape, 1)
    keep = (lanes >= head * HEAD_DIM) & (lanes < (head + 1) * HEAD_DIM)
    return jnp.where(keep, values, jnp.zeros_like(values))


def mask_of(doc_col, doc_row, index, rows):
    reach = (index + 1) * rows
    keys = lax.broadcasted_iota(jnp.int32, (reach, rows), 0)
    queries = lax.broadcasted_iota(jnp.int32, (reach, rows), 1) + index * rows
    same = doc_col[:reach] == doc_row[:, index * rows : reach]
    return jnp.where((keys <= queries) & same, 0.0, neg_fill)


def sequence_parts(refs, rows):
    own, beside, above, diag_a, diag_b = refs
    return [
        (own, 0, 0),
        (beside, 1, 0),
        (above, 2, 0),
        (diag_a, 3, 0),
        (diag_b, 3, rows // 2),
    ]


def sequence_parts(refs, rows):
    own, beside, above, diag_a, diag_b = refs
    return [
        (own, 0, 0),
        (beside, 1, 0),
        (above, 2, 0),
        (diag_a, 3, 0),
        (diag_b, 3, rows // 2),
    ]


def sends_kernel(group, qkv_ref, gains_ref, biases_ref, cents_ref, proj_ref, out_ref):
    width = REPS * group
    shard = qkv_ref.shape[0]
    small = jnp.concatenate([gains_ref[...], biases_ref[...], cents_ref[...]], axis=1)
    pad = -small.shape[1] % 128
    small = jnp.concatenate([small, jnp.zeros((shard, pad), bf16)], axis=1)
    columns = 3 * group + small.shape[1]
    for r in range(REPS):
        for part in range(3):
            first = part * width + r * group
            out_ref[r, :, part * group : (part + 1) * group] = qkv_ref[:, first : first + group]
        out_ref[r, :, 3 * group : columns] = small
        out_ref[r, :, columns:] = proj_ref[...]


def stack_kernel(in_ref, out_ref, both_ref):
    both_ref[0] = in_ref[0, 0]
    both_ref[1] = out_ref[0, 0]


def attention_kernel(rows, group, place_ref, *refs):
    toks, refs = refs[:5], refs[5:]
    par_ref, w_ref, col_ref, row_ref, a_ref, qkv_ref, o_ref, lse_ref, vt_ref, ot_ref = refs
    rep = place_ref[0]
    heads = group // HEAD_DIM
    gain, shift = par_ref[0:1], par_ref[2:3]
    for ref, k, first in sequence_parts(toks, rows):
        normed, _ = stats_of(ref[...].astype(f32))
        block = (normed * gain + shift).astype(bf16)
        count = ref.shape[0]
        here = pl.ds(pl.multiple_of((rep ^ k) * rows + first, count), count)
        a_ref[here] = block
        qkv_ref[here] = dot_nn(block, w_ref[:, : 3 * group]).astype(bf16)
    vt_ref[...] = qkv_ref[:, 2 * group :].T
    for index in range(REPS):
        reach = (index + 1) * rows
        here = pl.ds(index * rows, rows)
        bias = mask_of(col_ref[...], row_ref[...], index, rows)

        def one(head, carry):
            query = head_lanes(qkv_ref[here, :group] * jnp.asarray(HEAD_DIM**-0.5, bf16), head)
            score = dot_nt(qkv_ref[:reach, group : 2 * group], query) + bias
            top = jnp.max(score, axis=0, keepdims=True)
            weight = jnp.exp(score - top)
            total = jnp.sum(weight, axis=0, keepdims=True)
            lanes = pl.ds(pl.multiple_of(head * HEAD_DIM, HEAD_DIM), HEAD_DIM)
            ot_ref[lanes] = dot_nn(vt_ref[lanes, :reach], weight.astype(bf16)) / total
            lse_ref[pl.ds(head, 1), here] = top + jnp.log(total)
            return carry

        lax.fori_loop(0, heads, one, 0)
        o_ref[here] = ot_ref[...].T.astype(bf16)


def attention_back_kernel(rows, group, place_ref, *refs):
    toks, refs = refs[:5], refs[5:]
    do_ref, w_ref, col_ref, row_ref, qkv_ref, o_ref, lse_ref, *refs = refs
    grad_ref, sum_ref, own_ref, to_x, to_y, left_y, left_x, *refs = refs
    kt_ref, dq_ref, dk_ref, dv_ref, delta_ref = refs
    rep = place_ref[0]
    heads = group // HEAD_DIM
    half = rows // 2
    kt_ref[...] = qkv_ref[:, group : 2 * group].T
    dk_ref[...] = jnp.zeros_like(dk_ref)
    dv_ref[...] = jnp.zeros_like(dv_ref)
    for index in range(REPS):
        reach = (index + 1) * rows
        here = pl.ds(index * rows, rows)
        bias = mask_of(col_ref[...], row_ref[...], index, rows)
        both = (do_ref[here].astype(f32) * o_ref[here].astype(f32)).T
        for head in range(heads):
            delta_ref[head : head + 1] = jnp.sum(
                both[head * HEAD_DIM : (head + 1) * HEAD_DIM], axis=0, keepdims=True
            )

        def one(head, carry):
            query = head_lanes(qkv_ref[here, :group] * jnp.asarray(HEAD_DIM**-0.5, bf16), head)
            grad = head_lanes(do_ref[here], head)
            score = dot_nt(qkv_ref[:reach, group : 2 * group], query) + bias
            prob = jnp.exp(score - lse_ref[pl.ds(head, 1), here])
            dprob = dot_nt(qkv_ref[:reach, 2 * group :], grad)
            dscore = (prob * (dprob - delta_ref[pl.ds(head, 1)])).astype(bf16)
            dv_ref[:reach] += dot_nn(prob.astype(bf16), grad)
            dk_ref[:reach] += dot_nn(dscore, query)
            lanes = pl.ds(pl.multiple_of(head * HEAD_DIM, HEAD_DIM), HEAD_DIM)
            dq_ref[lanes] = dot_nn(kt_ref[lanes, :reach], dscore)
            return carry

        lax.fori_loop(0, heads, one, 0)
        grad_ref[here, :group] = (dq_ref[...].T * HEAD_DIM**-0.5).astype(bf16)
    grad_ref[:, group : 2 * group] = dk_ref[...].astype(bf16)
    grad_ref[:, 2 * group :] = dv_ref[...].astype(bf16)
    sum_ref[...] = jnp.zeros_like(sum_ref)
    for ref, k, first in sequence_parts(toks, rows):
        count = ref.shape[0]
        here = pl.ds(pl.multiple_of((rep ^ k) * rows + first, count), count)
        back = dot_nt(grad_ref[here], w_ref[:, : 3 * group])
        normed, _ = stats_of(ref[...].astype(f32))
        sum_ref[0:1] += jnp.sum(back * normed, axis=0, keepdims=True)
        sum_ref[1:2] += jnp.sum(back, axis=0, keepdims=True)
        if k == 0:
            own_ref[...] = back
        elif k == 1:
            to_x[half:] = back[:half].astype(bf16)
            left_x[...] = back[half:]
        elif k == 2:
            left_y[...] = back[:half]
            to_y[half:] = back[half:].astype(bf16)
        elif first == 0:
            to_x[:half] = back.astype(bf16)
        else:
            to_y[:half] = back.astype(bf16)


def qkv_grad_kernel(group, extra, own_ref, a_ref, grad_ref, first_ref, mid_ref, cent_ref, out_ref):
    width = a_ref.shape[1]
    pad = out_ref.shape[1] - 3 * group
    row = lax.broadcasted_iota(jnp.int32, (pad, width), 0)
    small = jnp.where(row == 0, first_ref[0:1], 0.0)
    small = jnp.where(row == 1, mid_ref[0:1], small)
    small = jnp.where(row == 2, first_ref[1:2], small)
    small = jnp.where(row == 3, mid_ref[1:2], small)
    small = jnp.where(row == 4 + own_ref[1], cent_ref[0:1], small)
    out_ref[:, 3 * group :] = small.T
    for part in range(width // 256):
        piece = slice(part * 256, (part + 1) * 256)
        out_ref[piece, : 3 * group] = dot_tn(a_ref[:, piece], grad_ref[...])


def project_kernel(part_ref, w_ref, tok_ref, par_ref, table_ref, hidden_ref, packed_ref):
    hidden = tok_ref[...].astype(f32)
    for k in range(REPS):
        hidden = hidden + dot_nn(part_ref[k], w_ref[k])
    hidden_ref[...] = hidden
    normed, _ = stats_of(hidden)
    states = (normed * par_ref[1:2] + par_ref[3:4]).astype(bf16)
    packed_ref[...] = dot_nn(table_ref[...], states).astype(bf16)


def project_back_kernel(back_ref, w_ref, *refs):
    table_ref, hidden_ref, dy_ref, par_ref, dh_ref, dhb_ref, sum_ref, do_ref = refs
    grad = dot_nn(table_ref[...], back_ref[...])
    normed, inverse = stats_of(hidden_ref[...])
    sum_ref[...] = jnp.zeros_like(sum_ref)
    sum_ref[0:1] = jnp.sum(grad * normed, axis=0, keepdims=True)
    sum_ref[1:2] = jnp.sum(grad, axis=0, keepdims=True)
    dh = dy_ref[...].astype(f32) + norm_back(grad, normed, inverse, par_ref[1:2])
    dh_ref[...] = dh
    low = dh.astype(bf16)
    dhb_ref[...] = low
    for k in range(REPS):
        do_ref[k] = dot_nt(low, w_ref[k]).astype(bf16)


def proj_grad_kernel(part_ref, dhb_ref, out_ref):
    for k in range(REPS):
        out_ref[k] = dot_tn(part_ref[k], dhb_ref[...])


def tokens_grad_kernel(*refs):
    own_ref, from_x, from_y, upper, lower, tok_ref, par_ref, dh_ref, out_ref = refs
    half = upper.shape[0]
    parts = ((from_x, upper), (from_y, lower))
    for here, (direct, passed) in zip(halves(2 * half), parts):
        grad = own_ref[here] + direct[half:].astype(f32) + passed[...].astype(f32)
        normed, inverse = stats_of(tok_ref[here].astype(f32))
        back = norm_back(grad, normed, inverse, par_ref[0:1])
        out_ref[here] = (dh_ref[here] + back).astype(bf16)


def gelu_both(u):
    scale = (2.0 / jnp.pi) ** 0.5
    square = u * u
    half = 0.5 + 0.5 * jnp.tanh(u * (scale + scale * 0.044715 * square))
    active = u * half
    slope = half + (u - active) * half * (2.0 * scale + 2.0 * scale * 0.134145 * square)
    return active, slope


def fetch_slices(sources, in_buf, out_buf, sems):
    step = pl.program_id(0)

    @pl.when(step == 0)
    def _():
        for k, source_in, source_out in sources:
            pltpu.make_async_copy(source_in, in_buf.at[k], sems.at[0, k]).start()
            pltpu.make_async_copy(source_out, out_buf.at[k], sems.at[1, k]).start()

    _, source_in, source_out = sources[-1]
    pltpu.make_async_copy(source_in, in_buf.at[step], sems.at[0, step]).wait()
    pltpu.make_async_copy(source_out, out_buf.at[step], sems.at[1, step]).wait()


def gathered(ref):
    return [(k, ref.at[k, 0], ref.at[k, 1]) for k in range(REPS)]


def near_slices(refs):
    w_in, w_out, beside, above = refs
    return [
        (0, w_in.at[0, 1], w_out.at[0, 1]),
        (1, beside.at[0], beside.at[1]),
        (2, above.at[0], above.at[1]),
    ]


def halves(count):
    half = count // 2
    return [slice(0, half), slice(half, count)]


def expert_first_kernel(place_ref, par_ref, rows_a, rows_b, w_ref, gate_ref, *refs):
    act_ref, slope_ref, total_ref, low_a, low_b, rows_buf, in_buf, out_buf, sems = refs
    step = pl.program_id(0)
    count = rows_buf.shape[0]
    upper, lower = halves(count)

    @pl.when(step == 0)
    def _():
        rows_buf[upper] = rows_a[...]
        rows_buf[lower] = rows_b[...]
        total_ref[...] = jnp.zeros_like(total_ref)
        centroid = par_ref[pl.ds(4 + place_ref[1], 1)]
        weight = jnp.broadcast_to(centroid, (128, centroid.shape[1])).astype(bf16)
        for here in (upper, lower):
            gate_ref[here] = 1.0 / (1.0 + jnp.exp(-dot_nt(rows_buf[here], weight)))

    fetch_slices(gathered(w_ref), in_buf, out_buf, sems)
    active, slope = gelu_both(dot_nn(rows_buf[...], in_buf[step]))
    active = active.astype(bf16)
    act_ref[0] = active
    slope_ref[0] = slope.astype(bf16)
    total_ref[...] += dot_nt(active, out_buf[step])

    @pl.when(step == pl.num_programs(0) - 1)
    def _():
        low_a[...] = total_ref[upper].astype(bf16)
        low_b[...] = total_ref[lower].astype(bf16)


def second_step(step, zb_ref, db_ref, bufs, grads_ref, z2_ref, dz_ref):
    in_buf, out_buf = bufs
    active, slope = gelu_both(dot_nn(zb_ref[...], in_buf[step]))
    active = active.astype(bf16)
    z2_ref[...] += dot_nt(active, out_buf[step])
    du = (slope * dot_nn(db_ref[...], out_buf[step])).astype(bf16)
    dz_ref[...] += dot_nt(du, in_buf[step])
    grads_ref[0, 0] = dot_tn(zb_ref[...], du).astype(bf16)
    grads_ref[0, 1] = dot_tn(db_ref[...], active).astype(bf16)


def expert_near_kernel(*refs):
    _, rows_a, rows_b, first_ref, rec_a, rec_b, gate_ref, dy_a, dy_b, *refs = refs
    weights, refs = refs[:4], refs[4:]
    grads_ref, own_ref, zb_ref, db_ref, z2_ref, dz_ref, in_buf, out_buf, sems = refs
    step = pl.program_id(0)
    upper, lower = halves(zb_ref.shape[0])

    @pl.when(step == 0)
    def _():
        own = rows_a[...].astype(f32) + first_ref[upper] + rec_a[...].astype(f32)
        own_ref[...] = own
        zb_ref[upper] = own.astype(bf16)
        other = rows_b[...].astype(f32) + first_ref[lower] + rec_b[...].astype(f32)
        zb_ref[lower] = other.astype(bf16)
        db_ref[upper] = (gate_ref[upper, 0:1] * dy_a[...].astype(f32)).astype(bf16)
        db_ref[lower] = (gate_ref[lower, 0:1] * dy_b[...].astype(f32)).astype(bf16)
        z2_ref[...] = jnp.zeros_like(z2_ref)
        dz_ref[...] = jnp.zeros_like(dz_ref)

    fetch_slices(near_slices(weights), in_buf, out_buf, sems)
    second_step(step, zb_ref, db_ref, (in_buf, out_buf), grads_ref, z2_ref, dz_ref)


def expert_far_kernel(*refs):
    _, zb_ref, db_ref, z2_in, dz_in, stream_ref, diag_in, diag_out, _, *refs = refs
    grads_ref, own_ref, z2_low, dz_ref, low_a, low_b, z2_ref, in_buf, out_buf, sems = refs
    upper, lower = halves(zb_ref.shape[0])
    z2_ref[...] = z2_in[...]
    dz_ref[...] = dz_in[...]
    fetch_slices([(0, diag_in, diag_out)], in_buf, out_buf, sems)
    second_step(0, zb_ref, db_ref, (in_buf, out_buf), grads_ref, z2_ref, dz_ref)
    own_ref[...] = stream_ref[...] + z2_ref[upper]
    z2_low[...] = z2_ref[lower].astype(bf16)
    low_a[...] = dz_ref[upper].astype(bf16)
    low_b[...] = dz_ref[lower].astype(bf16)


def expert_last_kernel(*refs):
    gate_ref, dy_a, dy_b, second_ref, rec_a, rec_b, slope_ref, act_ref, *refs = refs
    rows_a, rows_b, w_ref, grads_ref, own_ref, low_ref, *refs = refs
    rows_buf, db_ref, acc, in_buf, out_buf, sems = refs
    step = pl.program_id(0)
    count = db_ref.shape[0]
    upper, lower = halves(count)

    @pl.when(step == 0)
    def _():
        own = gate_ref[upper, 0:1] * dy_a[...].astype(f32) + second_ref[upper]
        own = own + rec_a[...].astype(f32)
        own_ref[...] = own
        db_ref[upper] = own.astype(bf16)
        other = gate_ref[lower, 0:1] * dy_b[...].astype(f32) + second_ref[lower]
        db_ref[lower] = (other + rec_b[...].astype(f32)).astype(bf16)
        rows_buf[upper] = rows_a[...]
        rows_buf[lower] = rows_b[...]
        acc[...] = jnp.zeros_like(acc)

    fetch_slices(gathered(w_ref), in_buf, out_buf, sems)
    du = (slope_ref[0].astype(f32) * dot_nn(db_ref[...], out_buf[step])).astype(bf16)
    acc[...] += dot_nt(du, in_buf[step])
    grads_ref[0, 0] = dot_tn(rows_buf[...], du).astype(bf16)
    grads_ref[0, 1] = dot_tn(db_ref[...], act_ref[0]).astype(bf16)

    @pl.when(step == REPS - 1)
    def _():
        own_ref[...] += acc[upper]
        low_ref[...] = acc[lower].astype(bf16)


def answer_kernel(final_ref, z2_ref, gate_ref, dy_ref, rows_ref, out_ref, score_ref, cent_ref):
    final = final_ref[...] + z2_ref[...].astype(f32)
    gate = gate_ref[...]
    out_ref[...] = (gate[:, 0:1] * final).astype(bf16)
    score = jnp.sum(dy_ref[...].astype(f32) * final, axis=1, keepdims=True)
    score = score * gate * (1.0 - gate)
    score_ref[...] = score
    cent_ref[...] = jnp.zeros_like(cent_ref)
    cent_ref[0:1] = jnp.sum(score[:, 0:1] * rows_ref[...].astype(f32), axis=0, keepdims=True)


def states_grad_kernel(place_ref, own_ref, low_ref, score_ref, par_ref, out_ref):
    centroid = par_ref[pl.ds(4 + place_ref[1], 1)]
    grad = own_ref[...] + low_ref[...].astype(f32) + score_ref[:, 0:1] * centroid
    out_ref[...] = grad.astype(bf16)


def layer_kernel(*refs):
    grads_ref, (in_ref, out_ref) = refs[0], refs[-2:]
    in_ref[0, 0] = grads_ref[0].astype(f32)
    out_ref[0, 0] = grads_ref[1].astype(f32)


def local(
    tokens,
    doc_ids,
    routes,
    norm_gains,
    norm_biases,
    w_qkv,
    w_proj,
    centroids,
    w_in,
    w_out,
    grad_out,
):
    rep = lax.axis_index("rep")
    parity = lax.axis_index("exp") % 2
    own_z = lax.axis_index("exp") // 2
    n_z = lax.axis_size("exp") // 2
    tok_rows = tokens.shape[1]
    width = tokens.shape[2]
    experts = centroids.shape[1]
    capacity = 2 * (5 * tok_rows // (8 * experts))
    group = width // REPS
    shard = w_qkv.shape[0]
    hidden_units = w_in.shape[3]
    seq_len = doc_ids.shape[1]
    half = tok_rows // 2
    place = jnp.stack([rep, own_z]).astype(jnp.int32)

    extra = 4 + experts
    pad = -extra % 128
    columns = 3 * group + extra + pad
    (sends,) = call(
        functools.partial(sends_kernel, group),
        [((REPS, shard, columns + width), bf16)],
        w_qkv,
        norm_gains,
        norm_biases,
        centroids,
        w_proj,
        cost=1,
    )
    got = exchange(sends, "rep")

    def assembled(blocks):
        blocks = both_cores(blocks, parity, 1).transpose(2, 0, 1, 3, 4)
        return blocks.reshape(width, blocks.shape[-1])

    own_tokens = tokens[0]
    tok_x, tok_y = over_x(own_tokens), over_y(own_tokens)
    along = gather_z(got[:, :, :columns])
    whole = assembled(along)
    proj_z = gather_z(after(got[:, :, columns:], along))
    params = whole[:, 3 * group :].T.astype(f32)

    seq = [own_tokens, tok_x, tok_y, over_y(tok_x[:half]), over_x(tok_y[half:])]

    one = (1, 1, width, hidden_units)

    def stacked(sub, *earlier):
        spec = pl.BlockSpec(one, lambda _: (0, sub, 0, 0))
        (both,) = call(
            stack_kernel,
            [((2, width, hidden_units), bf16)],
            *after((w_in, w_out), *earlier),
            specs={0: spec, 1: spec},
            cost=1,
        )
        return both

    layer0 = lax.all_gather(stacked(0, tok_x, tok_y, got), "rep")
    own_second = stacked(1, along)
    expert = routes[0, :, 0]
    onehot = (expert[:, None] == jnp.arange(experts, dtype=jnp.int32)[None, :]).astype(jnp.int32)
    before = jnp.cumsum(onehot, axis=0) - onehot
    rank = jnp.sum(before * onehot, axis=1)
    slot = expert * capacity + rank % 2 * (capacity // 2) + rank // 2
    own_slots = experts * capacity
    slots = jnp.arange(own_slots, dtype=jnp.int32)
    table = (slots[:, None] == slot[None, :]).astype(bf16)
    table_t = (slots[None, :] == slot[:, None]).astype(bf16)
    spread = (2 * n_z, capacity // 2, width)

    def travel(rows):
        return exchange(rows.reshape(spread), "exp").reshape(own_slots, width)

    own_grad = grad_out[0]
    packed_grad = product(table, own_grad).astype(bf16)

    docs = doc_ids.reshape(1, seq_len)
    doc_col = doc_ids.reshape(seq_len, 1)
    seq[0] = after(seq[0], own_second)
    attn_in, qkv, mixed_own, lse = call(
        functools.partial(attention_kernel, tok_rows, group),
        [
            ((seq_len, width), bf16),
            ((seq_len, 3 * group), bf16),
            ((seq_len, group), bf16),
            ((8, seq_len), f32),
        ],
        place,
        *seq,
        params,
        whole,
        doc_col,
        docs,
        specs={0: SMEM},
        scratch=[pltpu.VMEM((group, seq_len), bf16), pltpu.VMEM((group, tok_rows), f32)],
        cost=14,
    )
    mixed = exchange(mixed_own.reshape(REPS, tok_rows, group), "rep")
    proj_w = assembled(after(proj_z, lse)).reshape(REPS, group, width)
    own_second = after(own_second, mixed)
    w1_x, w1_y = over_x(own_second), over_y(own_second)
    hidden, packed = call(
        project_kernel,
        [((tok_rows, width), f32), ((own_slots, width), bf16)],
        mixed,
        proj_w,
        own_tokens,
        params,
        table,
        cost=0,
    )

    all_slots = 2 * own_slots
    own_rows, all_rows = (own_slots, width), (all_slots, width)
    rows_a = travel(packed)
    rows_b = over_core(rows_a)
    dy_a = travel(after(packed_grad, rows_a))
    gate_shape = (all_slots, 128)
    by_slice = (REPS, all_slots, hidden_units)
    sliced = pl.BlockSpec((1, all_slots, hidden_units), lambda k: (k, 0, 0))
    slice_buf = pltpu.VMEM((REPS, width, hidden_units), bf16)
    slices = [slice_buf, slice_buf, pltpu.SemaphoreType.DMA((2, REPS))]
    gate, active0, slope0, first, low_a, low_b = call(
        expert_first_kernel,
        [
            (gate_shape, f32),
            (by_slice, bf16),
            (by_slice, bf16),
            (all_rows, f32),
            (own_rows, bf16),
            (own_rows, bf16),
        ],
        place,
        params,
        rows_a,
        rows_b,
        layer0,
        grid=(REPS,),
        specs={0: SMEM, 4: HBM},
        out_specs={1: sliced, 2: sliced},
        scratch=[pltpu.VMEM(all_rows, bf16)] + slices,
        limit=48,
        cost=0,
    )
    dy_a, w1_x, w1_y, low_a = lax.optimization_barrier((dy_a, w1_x, w1_y, low_a))
    dy_b = over_core(dy_a)
    rec_a, rec_b = over_core(low_b), over_core(low_a)
    diag_in, diag_out = over_y(w1_x[0]), over_x(w1_y[1])
    pair = (2, width, hidden_units)
    grads_shape = (REPS,) + pair
    grads_spec = pl.BlockSpec((1,) + pair, lambda k: (k, 0, 0, 0))
    def by_place(first):
        return pl.BlockSpec((1,) + pair, lambda k, at: (at[0] ^ (first + k), 0, 0, 0))

    def some_slices(count):
        buf = pltpu.VMEM((count, width, hidden_units), bf16)
        return [buf, buf, pltpu.SemaphoreType.DMA((2, count))]

    weights1, z1_own, stream1, branch1, z2_sum, dz_sum = call(
        expert_near_kernel,
        [
            (grads_shape, bf16),
            (own_rows, f32),
            (all_rows, bf16),
            (all_rows, bf16),
            (all_rows, f32),
            (all_rows, f32),
        ],
        place,
        rows_a,
        rows_b,
        first,
        rec_a,
        rec_b,
        gate,
        dy_a,
        dy_b,
        w_in,
        w_out,
        w1_x,
        w1_y,
        grid=(3,),
        specs={number: HBM for number in range(9, 13)},
        out_specs={0: by_place(0)},
        scratch=some_slices(3),
        limit=56,
        cost=22,
        prefetch=1,
    )
    weights1, own_final, z2_low, second, low_a, low_b = call(
        expert_far_kernel,
        [
            (grads_shape, bf16),
            (own_rows, f32),
            (own_rows, bf16),
            (all_rows, f32),
            (own_rows, bf16),
            (own_rows, bf16),
        ],
        place,
        stream1,
        branch1,
        z2_sum,
        dz_sum,
        z1_own,
        diag_in,
        diag_out,
        weights1,
        specs={6: HBM, 7: HBM, 8: HBM},
        out_specs={0: by_place(3)},
        alias={8: 0},
        scratch=[pltpu.VMEM(all_rows, f32)] + some_slices(1),
        limit=56,
        cost=9,
        prefetch=1,
    )
    grads1 = lax.psum_scatter(weights1, "rep", scatter_dimension=0)
    rec_a, rec_b = over_core(low_b), over_core(low_a)
    answer, score, grad_centroid = call(
        answer_kernel,
        [(own_rows, bf16), ((own_slots, 128), f32), ((8, width), f32)],
        own_final,
        over_core(z2_low),
        gate,
        dy_a,
        rows_a,
        specs={2: pl.BlockSpec((own_slots, 128), lambda _: (0, 0))},
        cost=2,
    )
    swapped = pl.BlockSpec((1,) + pair, lambda k: (k % 2 * 2 + k // 2, 0, 0, 0))
    weights0, own_first_grad, low = call(
        expert_last_kernel,
        [(grads_shape, bf16), (own_rows, f32), (own_rows, bf16)],
        gate,
        dy_a,
        dy_b,
        second,
        rec_a,
        rec_b,
        slope0,
        active0,
        rows_a,
        rows_b,
        layer0,
        grid=(REPS,),
        specs={6: sliced, 7: sliced, 10: HBM},
        out_specs={0: swapped},
        scratch=[pltpu.VMEM(all_rows, bf16)] * 2 + [pltpu.VMEM(all_rows, f32)] + slices,
        limit=60,
        cost=22,
    )
    grads0 = lax.psum_scatter(
        weights0, "rep", scatter_dimension=0, axis_index_groups=[[0, 2, 1, 3]]
    )
    (grad_inputs,) = call(
        states_grad_kernel,
        [(own_rows, bf16)],
        place,
        own_first_grad,
        over_core(low),
        score,
        params,
        specs={0: SMEM},
        cost=1,
    )
    grad_back = travel(grad_inputs)

    def layer_of(sub, grads, *held):
        shape = (1, 2, width, hidden_units)
        spec = pl.BlockSpec((1, 1, width, hidden_units), lambda _: (0, sub, 0, 0))
        return call(
            layer_kernel,
            [(shape, f32), (shape, f32)],
            grads,
            *held,
            specs={number: HBM for number in range(1, 1 + len(held))},
            out_specs={0: spec, 1: spec},
            alias={1: 0, 2: 1} if held else {},
            cost=2,
        )

    grad_hidden, grad_hidden_b, mid_sums, grad_mixed = call(
        project_back_kernel,
        [
            ((tok_rows, width), f32),
            ((tok_rows, width), bf16),
            ((8, width), f32),
            ((REPS, tok_rows, group), bf16),
        ],
        grad_back,
        proj_w,
        table_t,
        hidden,
        own_grad,
        params,
        cost=3,
    )
    grad_mixed = exchange(grad_mixed, "rep").reshape(seq_len, group)
    (proj_part,) = call(
        proj_grad_kernel, [((REPS, group, width), f32)], mixed, grad_hidden_b, cost=2
    )
    def own_parity(blocks):
        axis = blocks.ndim - 3
        sent = pick(blocks, 1 - parity, axis).astype(bf16)
        return pick(blocks, parity, axis) + over_core(sent).astype(f32)

    proj_part = own_parity(proj_part.reshape(REPS, n_z, 2, shard, width))
    proj_part = scatter_z(proj_part.transpose(1, 0, 2, 3)).astype(bf16)

    grad_qkv_b, first_sums, own_attn, to_x, to_y, left_y, left_x = call(
        functools.partial(attention_back_kernel, tok_rows, group),
        [
            ((seq_len, 3 * group), bf16),
            ((8, width), f32),
            ((tok_rows, width), f32),
            ((tok_rows, width), bf16),
            ((tok_rows, width), bf16),
            ((half, width), f32),
            ((half, width), f32),
        ],
        place,
        *seq,
        grad_mixed,
        whole,
        doc_col,
        docs,
        qkv,
        mixed_own,
        lse,
        specs={0: SMEM},
        scratch=[
            pltpu.VMEM((group, seq_len), bf16),
            pltpu.VMEM((group, tok_rows), f32),
            pltpu.VMEM((seq_len, group), f32),
            pltpu.VMEM((seq_len, group), f32),
            pltpu.VMEM((8, tok_rows), f32),
        ],
        limit=48,
        cost=17,
    )
    from_x, from_y = over_x(to_x), over_y(to_y)
    (qkv_part,) = call(
        functools.partial(qkv_grad_kernel, group, extra),
        [((width, columns), f32)],
        place,
        after(attn_in, proj_part),
        grad_qkv_b,
        first_sums,
        mid_sums,
        grad_centroid,
        specs={0: SMEM},
        cost=2,
    )
    qkv_part = own_parity(qkv_part.reshape(REPS, n_z, 2, shard, columns))
    qkv_part = scatter_z(qkv_part.transpose(1, 0, 2, 3)).astype(bf16)
    from_x, from_y = after((from_x, from_y), qkv_part)
    upper = over_y((left_y + from_x[:half].astype(f32)).astype(bf16))
    lower = over_x((left_x + from_y[:half].astype(f32)).astype(bf16))
    (grad_tokens,) = call(
        tokens_grad_kernel,
        [((tok_rows, width), bf16)],
        own_attn,
        from_x,
        from_y,
        upper,
        lower,
        own_tokens,
        params,
        grad_hidden,
        cost=2,
    )

    got = exchange(jnp.concatenate([qkv_part, proj_part], axis=2), "rep").astype(f32)
    returned = travel(after(answer, got))
    block_out = (hidden + product(table_t, returned)).astype(bf16)
    small_sum = jnp.sum(got[:, :, 3 * group : 3 * group + extra], axis=0)
    big = got[:, :, : 3 * group].reshape(REPS, shard, 3, group)
    grad_qkv = big.transpose(1, 2, 0, 3).reshape(shard, 3 * width)
    grad_proj = jnp.sum(got[:, :, columns:], axis=0)
    grad_w_in, grad_w_out = layer_of(0, grads0, *layer_of(1, grads1))
    return (
        block_out[None],
        grad_tokens[None],
        small_sum[:, 0:2],
        small_sum[:, 2:4],
        grad_qkv,
        grad_proj,
        small_sum[:, 4:],
        grad_w_in,
        grad_w_out,
    )


def solution(mesh):
    in_specs = (
        P("exp", "rep", None),
        P("exp", None),
        P("exp", "rep", None),
        P(("rep", "exp"), None),
        P(("rep", "exp"), None),
        P(("rep", "exp"), None),
        P(("rep", "exp"), None),
        P(("rep", "exp"), None),
        P("exp", None, None, "rep"),
        P("exp", None, None, "rep"),
        P("exp", "rep", None),
    )
    out_specs = (
        P("exp", "rep", None),
        P("exp", "rep", None),
        P(("rep", "exp"), None),
        P(("rep", "exp"), None),
        P(("rep", "exp"), None),
        P(("rep", "exp"), None),
        P(("rep", "exp"), None),
        P("exp", None, None, "rep"),
        P("exp", None, None, "rep"),
    )
    return jax.shard_map(local, mesh=mesh, in_specs=in_specs, out_specs=out_specs, check_vma=False)
```

```python
import functools

import jax
import jax.numpy as jnp
from jax import lax
from jax.experimental import pallas as pl
from jax.experimental.pallas import tpu as pltpu
from jax.sharding import PartitionSpec as P

HEAD_DIM = 64
REPS = 4
eps = 1e-05
neg_fill = -1e30
bf16 = jnp.bfloat16
f32 = jnp.float32


def flip(value, axis, mask):
    pairs = [(source, source ^ mask) for source in range(lax.axis_size(axis))]
    return lax.ppermute(value, axis, pairs)


def over_x(value):
    return flip(value, "rep", 1)


def over_y(value):
    return flip(value, "rep", 2)


def over_diag(value):
    return flip(value, "rep", 3)


def over_core(value):
    return flip(value, "exp", 1)


def shift_z(value, step):
    size = lax.axis_size("exp")
    if step % (size // 2) == 0:
        return value
    pairs = [(source, (source + 2 * step) % size) for source in range(size)]
    return lax.ppermute(value, "exp", pairs)


def pick(stacked, index, axis=0):
    return lax.dynamic_index_in_dim(stacked, index, axis=axis, keepdims=False)


def gather_z(block):
    n_z = lax.axis_size("exp") // 2
    own_z = lax.axis_index("exp") // 2
    out = jnp.zeros((n_z,) + block.shape, block.dtype)
    for step in range(n_z):
        out = lax.dynamic_update_index_in_dim(out, shift_z(block, step), (own_z - step) % n_z, 0)
    return out


def scatter_z(blocks):
    n_z = lax.axis_size("exp") // 2
    own_z = lax.axis_index("exp") // 2
    total = pick(blocks, own_z)
    for step in range(1, n_z):
        sent = pick(blocks, (own_z + step) % n_z).astype(bf16)
        total = total + shift_z(sent, step).astype(f32)
    return total


def both_cores(value, parity, axis):
    other = over_core(value)
    return jnp.stack(
        [jnp.where(parity == 0, value, other), jnp.where(parity == 0, other, value)], axis=axis
    )


def layer_norm(values, gain_vec, shift):
    average = jnp.mean(values, axis=-1, keepdims=True)
    centred = values - average
    inverse = lax.rsqrt(jnp.mean(centred * centred, axis=-1, keepdims=True) + eps)
    normed = centred * inverse
    return (normed * gain_vec + shift, normed, inverse)


def norm_back(gradient, normed, inverse, gain_vec):
    scaled = gradient * gain_vec
    bracket = (
        scaled
        - jnp.mean(scaled, axis=-1, keepdims=True)
        - normed * jnp.mean(scaled * normed, axis=-1, keepdims=True)
    )
    return inverse * bracket


def product(former, latter):
    return jnp.dot(former, latter, preferred_element_type=f32)


def after(values, *earlier):
    return lax.optimization_barrier((values, earlier))[0]


def exchange(blocks, axis):
    return lax.all_to_all(blocks, axis, split_axis=0, concat_axis=0, tiled=True)


MIB = 1 << 20


def whole_block(shape):
    return pl.BlockSpec(shape, lambda *_: (0,) * len(shape), pipeline_mode=pl.Buffered(1))


def call(
    body,
    outs,
    *operands,
    cost,
    grid=(1,),
    specs=None,
    out_specs=None,
    scratch=(),
    limit=40,
    alias=None,
    prefetch=0,
):
    shapes = [jax.ShapeDtypeStruct(shape, dtype) for shape, dtype in outs]
    in_specs = [whole_block(operand.shape) for operand in operands]
    for number, spec in (specs or {}).items():
        in_specs[number] = spec
    kinds = [whole_block(shape) for shape, _ in outs]
    for number, spec in (out_specs or {}).items():
        kinds[number] = spec
    return pl.pallas_call(
        body,
        out_shape=shapes,
        grid_spec=pltpu.PrefetchScalarGridSpec(
            num_scalar_prefetch=prefetch,
            grid=grid,
            in_specs=in_specs[prefetch:],
            out_specs=kinds,
            scratch_shapes=list(scratch),
        ),
        input_output_aliases=alias or {},
        compiler_params=pltpu.CompilerParams(vmem_limit_bytes=limit * MIB),
        cost_estimate=pl.CostEstimate(flops=cost * 1000**3, bytes_accessed=0, transcendentals=0),
    )(*operands)


SMEM = pl.BlockSpec(memory_space=pltpu.SMEM)
HBM = pl.BlockSpec(memory_space=pl.ANY)


def dot_nn(a, b):
    return lax.dot_general(a, b, (((1,), (0,)), ((), ())), preferred_element_type=f32)


def dot_nt(a, b):
    return lax.dot_general(a, b, (((1,), (1,)), ((), ())), preferred_element_type=f32)


def dot_tn(a, b):
    return lax.dot_general(a, b, (((0,), (0,)), ((), ())), preferred_element_type=f32)


def stats_of(values):
    average = jnp.mean(values, axis=-1, keepdims=True)
    centred = values - average
    inverse = lax.rsqrt(jnp.mean(centred * centred, axis=-1, keepdims=True) + eps)
    return centred * inverse, inverse


def head_lanes(values, head):
    lanes = lax.broadcasted_iota(jnp.int32, values.shape, 1)
    keep = (lanes >= head * HEAD_DIM) & (lanes < (head + 1) * HEAD_DIM)
    return jnp.where(keep, values, jnp.zeros_like(values))


def mask_of(doc_col, doc_row, index, rows):
    reach = (index + 1) * rows
    keys = lax.broadcasted_iota(jnp.int32, (reach, rows), 0)
    queries = lax.broadcasted_iota(jnp.int32, (reach, rows), 1) + index * rows
    same = doc_col[:reach] == doc_row[:, index * rows : reach]
    return jnp.where((keys <= queries) & same, 0.0, neg_fill)


def sequence_parts(refs, rows):
    own, beside, above, diag_a, diag_b = refs
    return [
        (own, 0, 0),
        (beside, 1, 0),
        (above, 2, 0),
        (diag_a, 3, 0),
        (diag_b, 3, rows // 2),
    ]


def sequence_parts(refs, rows):
    own, beside, above, diag_a, diag_b = refs
    return [
        (own, 0, 0),
        (beside, 1, 0),
        (above, 2, 0),
        (diag_a, 3, 0),
        (diag_b, 3, rows // 2),
    ]


def sends_kernel(group, qkv_ref, gains_ref, biases_ref, cents_ref, proj_ref, out_ref):
    width = REPS * group
    shard = qkv_ref.shape[0]
    small = jnp.concatenate([gains_ref[...], biases_ref[...], cents_ref[...]], axis=1)
    pad = -small.shape[1] % 128
    small = jnp.concatenate([small, jnp.zeros((shard, pad), bf16)], axis=1)
    columns = 3 * group + small.shape[1]
    for r in range(REPS):
        for part in range(3):
            first = part * width + r * group
            out_ref[r, :, part * group : (part + 1) * group] = qkv_ref[:, first : first + group]
        out_ref[r, :, 3 * group : columns] = small
        out_ref[r, :, columns:] = proj_ref[...]


def stack_kernel(in_ref, out_ref, both_ref):
    both_ref[0] = in_ref[0, 0]
    both_ref[1] = out_ref[0, 0]


def attention_kernel(rows, group, place_ref, *refs):
    toks, refs = refs[:5], refs[5:]
    par_ref, w_ref, col_ref, row_ref, a_ref, qkv_ref, o_ref, lse_ref, vt_ref, ot_ref = refs
    rep = place_ref[0]
    heads = group // HEAD_DIM
    gain, shift = par_ref[0:1], par_ref[2:3]
    for ref, k, first in sequence_parts(toks, rows):
        normed, _ = stats_of(ref[...].astype(f32))
        block = (normed * gain + shift).astype(bf16)
        count = ref.shape[0]
        here = pl.ds(pl.multiple_of((rep ^ k) * rows + first, count), count)
        a_ref[here] = block
        qkv_ref[here] = dot_nn(block, w_ref[:, : 3 * group]).astype(bf16)
    vt_ref[...] = qkv_ref[:, 2 * group :].T
    for index in range(REPS):
        reach = (index + 1) * rows
        here = pl.ds(index * rows, rows)
        bias = mask_of(col_ref[...], row_ref[...], index, rows)

        def one(head, carry):
            query = head_lanes(qkv_ref[here, :group] * jnp.asarray(HEAD_DIM**-0.5, bf16), head)
            score = dot_nt(qkv_ref[:reach, group : 2 * group], query) + bias
            top = jnp.max(score, axis=0, keepdims=True)
            weight = jnp.exp(score - top)
            total = jnp.sum(weight, axis=0, keepdims=True)
            lanes = pl.ds(pl.multiple_of(head * HEAD_DIM, HEAD_DIM), HEAD_DIM)
            ot_ref[lanes] = dot_nn(vt_ref[lanes, :reach], weight.astype(bf16)) / total
            lse_ref[pl.ds(head, 1), here] = top + jnp.log(total)
            return carry

        lax.fori_loop(0, heads, one, 0, unroll=True)
        o_ref[here] = ot_ref[...].T.astype(bf16)


def attention_back_kernel(rows, group, place_ref, *refs):
    toks, refs = refs[:5], refs[5:]
    do_ref, w_ref, col_ref, row_ref, qkv_ref, o_ref, lse_ref, *refs = refs
    grad_ref, sum_ref, own_ref, to_x, to_y, left_y, left_x, *refs = refs
    kt_ref, dq_ref, dk_ref, dv_ref, delta_ref = refs
    rep = place_ref[0]
    heads = group // HEAD_DIM
    half = rows // 2
    kt_ref[...] = qkv_ref[:, group : 2 * group].T
    dk_ref[...] = jnp.zeros_like(dk_ref)
    dv_ref[...] = jnp.zeros_like(dv_ref)
    for index in range(REPS):
        reach = (index + 1) * rows
        here = pl.ds(index * rows, rows)
        bias = mask_of(col_ref[...], row_ref[...], index, rows)
        both = (do_ref[here].astype(f32) * o_ref[here].astype(f32)).T
        for head in range(heads):
            delta_ref[head : head + 1] = jnp.sum(
                both[head * HEAD_DIM : (head + 1) * HEAD_DIM], axis=0, keepdims=True
            )

        def one(head, carry):
            query = head_lanes(qkv_ref[here, :group] * jnp.asarray(HEAD_DIM**-0.5, bf16), head)
            grad = head_lanes(do_ref[here], head)
            score = dot_nt(qkv_ref[:reach, group : 2 * group], query) + bias
            prob = jnp.exp(score - lse_ref[pl.ds(head, 1), here])
            dprob = dot_nt(qkv_ref[:reach, 2 * group :], grad)
            dscore = (prob * (dprob - delta_ref[pl.ds(head, 1)])).astype(bf16)
            dv_ref[:reach] += dot_nn(prob.astype(bf16), grad)
            dk_ref[:reach] += dot_nn(dscore, query)
            lanes = pl.ds(pl.multiple_of(head * HEAD_DIM, HEAD_DIM), HEAD_DIM)
            dq_ref[lanes] = dot_nn(kt_ref[lanes, :reach], dscore)
            return carry

        lax.fori_loop(0, heads, one, 0)
        grad_ref[here, :group] = (dq_ref[...].T * HEAD_DIM**-0.5).astype(bf16)
    grad_ref[:, group : 2 * group] = dk_ref[...].astype(bf16)
    grad_ref[:, 2 * group :] = dv_ref[...].astype(bf16)
    sum_ref[...] = jnp.zeros_like(sum_ref)
    for ref, k, first in sequence_parts(toks, rows):
        count = ref.shape[0]
        here = pl.ds(pl.multiple_of((rep ^ k) * rows + first, count), count)
        back = dot_nt(grad_ref[here], w_ref[:, : 3 * group])
        normed, _ = stats_of(ref[...].astype(f32))
        sum_ref[0:1] += jnp.sum(back * normed, axis=0, keepdims=True)
        sum_ref[1:2] += jnp.sum(back, axis=0, keepdims=True)
        if k == 0:
            own_ref[...] = back
        elif k == 1:
            to_x[half:] = back[:half].astype(bf16)
            left_x[...] = back[half:]
        elif k == 2:
            left_y[...] = back[:half]
            to_y[half:] = back[half:].astype(bf16)
        elif first == 0:
            to_x[:half] = back.astype(bf16)
        else:
            to_y[:half] = back.astype(bf16)


def qkv_grad_kernel(group, extra, own_ref, a_ref, grad_ref, first_ref, mid_ref, cent_ref, out_ref):
    width = a_ref.shape[1]
    pad = out_ref.shape[1] - 3 * group
    row = lax.broadcasted_iota(jnp.int32, (pad, width), 0)
    small = jnp.where(row == 0, first_ref[0:1], 0.0)
    small = jnp.where(row == 1, mid_ref[0:1], small)
    small = jnp.where(row == 2, first_ref[1:2], small)
    small = jnp.where(row == 3, mid_ref[1:2], small)
    small = jnp.where(row == 4 + own_ref[1], cent_ref[0:1], small)
    out_ref[:, 3 * group :] = small.T
    for part in range(width // 256):
        piece = slice(part * 256, (part + 1) * 256)
        out_ref[piece, : 3 * group] = dot_tn(a_ref[:, piece], grad_ref[...])


def project_kernel(part_ref, w_ref, tok_ref, par_ref, table_ref, hidden_ref, packed_ref):
    hidden = tok_ref[...].astype(f32)
    for k in range(REPS):
        hidden = hidden + dot_nn(part_ref[k], w_ref[k])
    hidden_ref[...] = hidden
    normed, _ = stats_of(hidden)
    states = (normed * par_ref[1:2] + par_ref[3:4]).astype(bf16)
    packed_ref[...] = dot_nn(table_ref[...], states).astype(bf16)


def project_back_kernel(back_ref, w_ref, *refs):
    table_ref, hidden_ref, dy_ref, par_ref, dh_ref, dhb_ref, sum_ref, do_ref = refs
    grad = dot_nn(table_ref[...], back_ref[...])
    normed, inverse = stats_of(hidden_ref[...])
    sum_ref[...] = jnp.zeros_like(sum_ref)
    sum_ref[0:1] = jnp.sum(grad * normed, axis=0, keepdims=True)
    sum_ref[1:2] = jnp.sum(grad, axis=0, keepdims=True)
    dh = dy_ref[...].astype(f32) + norm_back(grad, normed, inverse, par_ref[1:2])
    dh_ref[...] = dh
    low = dh.astype(bf16)
    dhb_ref[...] = low
    for k in range(REPS):
        do_ref[k] = dot_nt(low, w_ref[k]).astype(bf16)


def proj_grad_kernel(part_ref, dhb_ref, out_ref):
    for k in range(REPS):
        out_ref[k] = dot_tn(part_ref[k], dhb_ref[...])


def tokens_grad_kernel(*refs):
    own_ref, from_x, from_y, upper, lower, tok_ref, par_ref, dh_ref, out_ref = refs
    half = upper.shape[0]
    parts = ((from_x, upper), (from_y, lower))
    for here, (direct, passed) in zip(halves(2 * half), parts):
        grad = own_ref[here] + direct[half:].astype(f32) + passed[...].astype(f32)
        normed, inverse = stats_of(tok_ref[here].astype(f32))
        back = norm_back(grad, normed, inverse, par_ref[0:1])
        out_ref[here] = (dh_ref[here] + back).astype(bf16)


def gelu_both(u):
    scale = (2.0 / jnp.pi) ** 0.5
    square = u * u
    half = 0.5 + 0.5 * jnp.tanh(u * (scale + scale * 0.044715 * square))
    active = u * half
    slope = half + (u - active) * half * (2.0 * scale + 2.0 * scale * 0.134145 * square)
    return active, slope


def fetch_slices(sources, in_buf, out_buf, sems):
    step = pl.program_id(0)

    @pl.when(step == 0)
    def _():
        for k, source_in, source_out in sources:
            pltpu.make_async_copy(source_in, in_buf.at[k], sems.at[0, k]).start()
            pltpu.make_async_copy(source_out, out_buf.at[k], sems.at[1, k]).start()

    _, source_in, source_out = sources[-1]
    pltpu.make_async_copy(source_in, in_buf.at[step], sems.at[0, step]).wait()
    pltpu.make_async_copy(source_out, out_buf.at[step], sems.at[1, step]).wait()


def gathered(ref):
    return [(k, ref.at[k, 0], ref.at[k, 1]) for k in range(REPS)]


def near_slices(refs):
    w_in, w_out, beside, above = refs
    return [
        (0, w_in.at[0, 1], w_out.at[0, 1]),
        (1, beside.at[0], beside.at[1]),
        (2, above.at[0], above.at[1]),
    ]


def halves(count):
    half = count // 2
    return [slice(0, half), slice(half, count)]


def expert_first_kernel(place_ref, par_ref, rows_a, rows_b, w_ref, gate_ref, *refs):
    act_ref, slope_ref, total_ref, low_a, low_b, rows_buf, in_buf, out_buf, sems = refs
    step = pl.program_id(0)
    count = rows_buf.shape[0]
    upper, lower = halves(count)

    @pl.when(step == 0)
    def _():
        rows_buf[upper] = rows_a[...]
        rows_buf[lower] = rows_b[...]
        total_ref[...] = jnp.zeros_like(total_ref)
        centroid = par_ref[pl.ds(4 + place_ref[1], 1)]
        weight = jnp.broadcast_to(centroid, (128, centroid.shape[1])).astype(bf16)
        for here in (upper, lower):
            gate_ref[here] = 1.0 / (1.0 + jnp.exp(-dot_nt(rows_buf[here], weight)))

    fetch_slices(gathered(w_ref), in_buf, out_buf, sems)
    active, slope = gelu_both(dot_nn(rows_buf[...], in_buf[step]))
    active = active.astype(bf16)
    act_ref[0] = active
    slope_ref[0] = slope.astype(bf16)
    total_ref[...] += dot_nt(active, out_buf[step])

    @pl.when(step == pl.num_programs(0) - 1)
    def _():
        low_a[...] = total_ref[upper].astype(bf16)
        low_b[...] = total_ref[lower].astype(bf16)


def second_step(step, zb_ref, db_ref, bufs, grads_ref, z2_ref, dz_ref):
    in_buf, out_buf = bufs
    active, slope = gelu_both(dot_nn(zb_ref[...], in_buf[step]))
    active = active.astype(bf16)
    z2_ref[...] += dot_nt(active, out_buf[step])
    du = (slope * dot_nn(db_ref[...], out_buf[step])).astype(bf16)
    dz_ref[...] += dot_nt(du, in_buf[step])
    grads_ref[0, 0] = dot_tn(zb_ref[...], du).astype(bf16)
    grads_ref[0, 1] = dot_tn(db_ref[...], active).astype(bf16)


def expert_near_kernel(*refs):
    _, rows_a, rows_b, first_ref, rec_a, rec_b, gate_ref, dy_a, dy_b, *refs = refs
    weights, refs = refs[:4], refs[4:]
    grads_ref, own_ref, zb_ref, db_ref, z2_ref, dz_ref, in_buf, out_buf, sems = refs
    step = pl.program_id(0)
    upper, lower = halves(zb_ref.shape[0])

    @pl.when(step == 0)
    def _():
        own = rows_a[...].astype(f32) + first_ref[upper] + rec_a[...].astype(f32)
        own_ref[...] = own
        zb_ref[upper] = own.astype(bf16)
        other = rows_b[...].astype(f32) + first_ref[lower] + rec_b[...].astype(f32)
        zb_ref[lower] = other.astype(bf16)
        db_ref[upper] = (gate_ref[upper, 0:1] * dy_a[...].astype(f32)).astype(bf16)
        db_ref[lower] = (gate_ref[lower, 0:1] * dy_b[...].astype(f32)).astype(bf16)
        z2_ref[...] = jnp.zeros_like(z2_ref)
        dz_ref[...] = jnp.zeros_like(dz_ref)

    fetch_slices(near_slices(weights), in_buf, out_buf, sems)
    second_step(step, zb_ref, db_ref, (in_buf, out_buf), grads_ref, z2_ref, dz_ref)


def expert_far_kernel(*refs):
    _, zb_ref, db_ref, z2_in, dz_in, stream_ref, diag_in, diag_out, _, *refs = refs
    grads_ref, own_ref, z2_low, dz_ref, low_a, low_b, z2_ref, in_buf, out_buf, sems = refs
    upper, lower = halves(zb_ref.shape[0])
    fetch_slices([(0, diag_in, diag_out)], in_buf, out_buf, sems)
    active, slope = gelu_both(dot_nn(zb_ref[...], in_buf[0]))
    active = active.astype(bf16)
    du = (slope * dot_nn(db_ref[...], out_buf[0])).astype(bf16)
    dz_ref[...] = dz_in[...] + dot_nt(du, in_buf[0])
    z2_ref[...] = z2_in[...] + dot_nt(active, out_buf[0])
    grads_ref[0, 0] = dot_tn(zb_ref[...], du).astype(bf16)
    grads_ref[0, 1] = dot_tn(db_ref[...], active).astype(bf16)
    own_ref[...] = stream_ref[...] + z2_ref[upper]
    z2_low[...] = z2_ref[lower].astype(bf16)
    low_a[...] = dz_ref[upper].astype(bf16)
    low_b[...] = dz_ref[lower].astype(bf16)


def expert_last_kernel(*refs):
    gate_ref, dy_a, dy_b, second_ref, rec_a, rec_b, slope_ref, act_ref, *refs = refs
    rows_a, rows_b, w_ref, grads_ref, own_ref, low_ref, *refs = refs
    rows_buf, db_ref, acc, in_buf, out_buf, sems = refs
    step = pl.program_id(0)
    count = db_ref.shape[0]
    upper, lower = halves(count)

    @pl.when(step == 0)
    def _():
        own = gate_ref[upper, 0:1] * dy_a[...].astype(f32) + second_ref[upper]
        own = own + rec_a[...].astype(f32)
        own_ref[...] = own
        db_ref[upper] = own.astype(bf16)
        other = gate_ref[lower, 0:1] * dy_b[...].astype(f32) + second_ref[lower]
        db_ref[lower] = (other + rec_b[...].astype(f32)).astype(bf16)
        rows_buf[upper] = rows_a[...]
        rows_buf[lower] = rows_b[...]
        acc[...] = jnp.zeros_like(acc)

    fetch_slices(gathered(w_ref), in_buf, out_buf, sems)
    du = (slope_ref[0].astype(f32) * dot_nn(db_ref[...], out_buf[step])).astype(bf16)
    acc[...] += dot_nt(du, in_buf[step])
    grads_ref[0, 0] = dot_tn(rows_buf[...], du).astype(bf16)
    grads_ref[0, 1] = dot_tn(db_ref[...], act_ref[0]).astype(bf16)

    @pl.when(step == REPS - 1)
    def _():
        own_ref[...] += acc[upper]
        low_ref[...] = acc[lower].astype(bf16)


def answer_kernel(final_ref, z2_ref, gate_ref, dy_ref, rows_ref, out_ref, score_ref, cent_ref):
    final = final_ref[...] + z2_ref[...].astype(f32)
    gate = gate_ref[...]
    out_ref[...] = (gate[:, 0:1] * final).astype(bf16)
    score = jnp.sum(dy_ref[...].astype(f32) * final, axis=1, keepdims=True)
    score = score * gate * (1.0 - gate)
    score_ref[...] = score
    cent_ref[...] = jnp.zeros_like(cent_ref)
    cent_ref[0:1] = jnp.sum(score[:, 0:1] * rows_ref[...].astype(f32), axis=0, keepdims=True)


def states_grad_kernel(place_ref, own_ref, low_ref, score_ref, par_ref, out_ref):
    centroid = par_ref[pl.ds(4 + place_ref[1], 1)]
    grad = own_ref[...] + low_ref[...].astype(f32) + score_ref[:, 0:1] * centroid
    out_ref[...] = grad.astype(bf16)


def layer_kernel(*refs):
    grads_ref, (in_ref, out_ref) = refs[0], refs[-2:]
    in_ref[0, 0] = grads_ref[0].astype(f32)
    out_ref[0, 0] = grads_ref[1].astype(f32)


def local(
    tokens,
    doc_ids,
    routes,
    norm_gains,
    norm_biases,
    w_qkv,
    w_proj,
    centroids,
    w_in,
    w_out,
    grad_out,
):
    rep = lax.axis_index("rep")
    parity = lax.axis_index("exp") % 2
    own_z = lax.axis_index("exp") // 2
    n_z = lax.axis_size("exp") // 2
    tok_rows = tokens.shape[1]
    width = tokens.shape[2]
    experts = centroids.shape[1]
    capacity = 2 * (5 * tok_rows // (8 * experts))
    group = width // REPS
    shard = w_qkv.shape[0]
    hidden_units = w_in.shape[3]
    seq_len = doc_ids.shape[1]
    half = tok_rows // 2
    place = jnp.stack([rep, own_z]).astype(jnp.int32)

    extra = 4 + experts
    pad = -extra % 128
    columns = 3 * group + extra + pad
    (sends,) = call(
        functools.partial(sends_kernel, group),
        [((REPS, shard, columns + width), bf16)],
        w_qkv,
        norm_gains,
        norm_biases,
        centroids,
        w_proj,
        cost=1,
    )
    got = exchange(sends, "rep")

    def assembled(blocks):
        blocks = both_cores(blocks, parity, 1).transpose(2, 0, 1, 3, 4)
        return blocks.reshape(width, blocks.shape[-1])

    own_tokens = tokens[0]
    tok_x, tok_y = over_x(own_tokens), over_y(own_tokens)
    along = gather_z(got[:, :, :columns])
    whole = assembled(along)
    proj_z = gather_z(after(got[:, :, columns:], along))
    params = whole[:, 3 * group :].T.astype(f32)

    seq = [own_tokens, tok_x, tok_y, over_y(tok_x[:half]), over_x(tok_y[half:])]

    one = (1, 1, width, hidden_units)

    def stacked(sub, *earlier):
        spec = pl.BlockSpec(one, lambda _: (0, sub, 0, 0))
        (both,) = call(
            stack_kernel,
            [((2, width, hidden_units), bf16)],
            *after((w_in, w_out), *earlier),
            specs={0: spec, 1: spec},
            cost=1,
        )
        return both

    layer0 = lax.all_gather(stacked(0, tok_x, tok_y, got), "rep")
    own_second = stacked(1, along)
    expert = routes[0, :, 0]
    onehot = (expert[:, None] == jnp.arange(experts, dtype=jnp.int32)[None, :]).astype(jnp.int32)
    before = jnp.cumsum(onehot, axis=0) - onehot
    rank = jnp.sum(before * onehot, axis=1)
    slot = expert * capacity + rank % 2 * (capacity // 2) + rank // 2
    own_slots = experts * capacity
    slots = jnp.arange(own_slots, dtype=jnp.int32)
    table = (slots[:, None] == slot[None, :]).astype(bf16)
    table_t = (slots[None, :] == slot[:, None]).astype(bf16)
    spread = (2 * n_z, capacity // 2, width)

    def travel(rows):
        return exchange(rows.reshape(spread), "exp").reshape(own_slots, width)

    own_grad = grad_out[0]
    packed_grad = product(table, own_grad).astype(bf16)

    docs = doc_ids.reshape(1, seq_len)
    doc_col = doc_ids.reshape(seq_len, 1)
    seq[0] = after(seq[0], own_second)
    attn_in, qkv, mixed_own, lse = call(
        functools.partial(attention_kernel, tok_rows, group),
        [
            ((seq_len, width), bf16),
            ((seq_len, 3 * group), bf16),
            ((seq_len, group), bf16),
            ((8, seq_len), f32),
        ],
        place,
        *seq,
        params,
        whole,
        doc_col,
        docs,
        specs={0: SMEM},
        scratch=[pltpu.VMEM((group, seq_len), bf16), pltpu.VMEM((group, tok_rows), f32)],
        cost=14,
    )
    mixed = exchange(mixed_own.reshape(REPS, tok_rows, group), "rep")
    proj_w = assembled(after(proj_z, lse)).reshape(REPS, group, width)
    own_second = after(own_second, mixed)
    w1_x, w1_y = over_x(own_second), over_y(own_second)
    hidden, packed = call(
        project_kernel,
        [((tok_rows, width), f32), ((own_slots, width), bf16)],
        mixed,
        proj_w,
        own_tokens,
        params,
        table,
        cost=0,
    )

    all_slots = 2 * own_slots
    own_rows, all_rows = (own_slots, width), (all_slots, width)
    rows_a = travel(packed)
    rows_b = over_core(rows_a)
    dy_a = travel(after(packed_grad, rows_a))
    gate_shape = (all_slots, 128)
    by_slice = (REPS, all_slots, hidden_units)
    sliced = pl.BlockSpec((1, all_slots, hidden_units), lambda k: (k, 0, 0))
    slice_buf = pltpu.VMEM((REPS, width, hidden_units), bf16)
    slices = [slice_buf, slice_buf, pltpu.SemaphoreType.DMA((2, REPS))]
    gate, active0, slope0, first, low_a, low_b = call(
        expert_first_kernel,
        [
            (gate_shape, f32),
            (by_slice, bf16),
            (by_slice, bf16),
            (all_rows, f32),
            (own_rows, bf16),
            (own_rows, bf16),
        ],
        place,
        params,
        rows_a,
        rows_b,
        layer0,
        grid=(REPS,),
        specs={0: SMEM, 4: HBM},
        out_specs={1: sliced, 2: sliced},
        scratch=[pltpu.VMEM(all_rows, bf16)] + slices,
        limit=48,
        cost=0,
    )
    dy_a, w1_x, w1_y, low_a = lax.optimization_barrier((dy_a, w1_x, w1_y, low_a))
    dy_b = over_core(dy_a)
    rec_a, rec_b = over_core(low_b), over_core(low_a)
    diag_in, diag_out, w1_x, w1_y = lax.optimization_barrier((w1_x[0], w1_y[1], w1_x, w1_y))
    diag_in, diag_out = over_y(diag_in), over_x(diag_out)
    pair = (2, width, hidden_units)
    grads_shape = (REPS,) + pair
    grads_spec = pl.BlockSpec((1,) + pair, lambda k: (k, 0, 0, 0))
    def by_place(first):
        return pl.BlockSpec((1,) + pair, lambda k, at: (at[0] ^ (first + k), 0, 0, 0))

    def some_slices(count):
        buf = pltpu.VMEM((count, width, hidden_units), bf16)
        return [buf, buf, pltpu.SemaphoreType.DMA((2, count))]

    weights1, z1_own, stream1, branch1, z2_sum, dz_sum = call(
        expert_near_kernel,
        [
            (grads_shape, bf16),
            (own_rows, f32),
            (all_rows, bf16),
            (all_rows, bf16),
            (all_rows, f32),
            (all_rows, f32),
        ],
        place,
        rows_a,
        rows_b,
        first,
        rec_a,
        rec_b,
        gate,
        dy_a,
        dy_b,
        w_in,
        w_out,
        w1_x,
        w1_y,
        grid=(3,),
        specs={number: HBM for number in range(9, 13)},
        out_specs={0: by_place(0)},
        scratch=some_slices(3),
        limit=56,
        cost=22,
        prefetch=1,
    )
    weights1, own_final, z2_low, second, low_a, low_b = call(
        expert_far_kernel,
        [
            (grads_shape, bf16),
            (own_rows, f32),
            (own_rows, bf16),
            (all_rows, f32),
            (own_rows, bf16),
            (own_rows, bf16),
        ],
        place,
        stream1,
        branch1,
        z2_sum,
        dz_sum,
        z1_own,
        diag_in,
        diag_out,
        weights1,
        specs={6: HBM, 7: HBM, 8: HBM},
        out_specs={0: by_place(3)},
        alias={8: 0},
        scratch=[pltpu.VMEM(all_rows, f32)] + some_slices(1),
        limit=56,
        cost=9,
        prefetch=1,
    )
    grads1 = lax.psum_scatter(weights1, "rep", scatter_dimension=0)
    rec_a, rec_b = over_core(low_b), over_core(low_a)
    answer, score, grad_centroid = call(
        answer_kernel,
        [(own_rows, bf16), ((own_slots, 128), f32), ((8, width), f32)],
        own_final,
        over_core(z2_low),
        gate,
        dy_a,
        rows_a,
        specs={2: pl.BlockSpec((own_slots, 128), lambda _: (0, 0))},
        cost=2,
    )
    swapped = pl.BlockSpec((1,) + pair, lambda k: (k % 2 * 2 + k // 2, 0, 0, 0))
    weights0, own_first_grad, low = call(
        expert_last_kernel,
        [(grads_shape, bf16), (own_rows, f32), (own_rows, bf16)],
        gate,
        dy_a,
        dy_b,
        second,
        rec_a,
        rec_b,
        slope0,
        active0,
        rows_a,
        rows_b,
        layer0,
        grid=(REPS,),
        specs={6: sliced, 7: sliced, 10: HBM},
        out_specs={0: swapped},
        scratch=[pltpu.VMEM(all_rows, bf16)] * 2 + [pltpu.VMEM(all_rows, f32)] + slices,
        limit=60,
        cost=22,
    )
    grads0 = lax.psum_scatter(
        weights0, "rep", scatter_dimension=0, axis_index_groups=[[0, 2, 1, 3]]
    )
    (grad_inputs,) = call(
        states_grad_kernel,
        [(own_rows, bf16)],
        place,
        own_first_grad,
        over_core(low),
        score,
        params,
        specs={0: SMEM},
        cost=1,
    )
    grad_back = travel(grad_inputs)

    def layer_of(sub, grads, *held):
        shape = (1, 2, width, hidden_units)
        spec = pl.BlockSpec((1, 1, width, hidden_units), lambda _: (0, sub, 0, 0))
        return call(
            layer_kernel,
            [(shape, f32), (shape, f32)],
            grads,
            *held,
            specs={number: HBM for number in range(1, 1 + len(held))},
            out_specs={0: spec, 1: spec},
            alias={1: 0, 2: 1} if held else {},
            cost=2,
        )

    grad_hidden, grad_hidden_b, mid_sums, grad_mixed = call(
        project_back_kernel,
        [
            ((tok_rows, width), f32),
            ((tok_rows, width), bf16),
            ((8, width), f32),
            ((REPS, tok_rows, group), bf16),
        ],
        grad_back,
        proj_w,
        table_t,
        hidden,
        own_grad,
        params,
        cost=3,
    )
    grad_mixed = exchange(grad_mixed, "rep").reshape(seq_len, group)
    (proj_part,) = call(
        proj_grad_kernel, [((REPS, group, width), f32)], mixed, grad_hidden_b, cost=2
    )
    def own_parity(blocks):
        axis = blocks.ndim - 3
        sent = pick(blocks, 1 - parity, axis).astype(bf16)
        return pick(blocks, parity, axis) + over_core(sent).astype(f32)

    proj_part = own_parity(proj_part.reshape(REPS, n_z, 2, shard, width))
    proj_part = scatter_z(proj_part.transpose(1, 0, 2, 3)).astype(bf16)

    grad_qkv_b, first_sums, own_attn, to_x, to_y, left_y, left_x = call(
        functools.partial(attention_back_kernel, tok_rows, group),
        [
            ((seq_len, 3 * group), bf16),
            ((8, width), f32),
            ((tok_rows, width), f32),
            ((tok_rows, width), bf16),
            ((tok_rows, width), bf16),
            ((half, width), f32),
            ((half, width), f32),
        ],
        place,
        *seq,
        grad_mixed,
        whole,
        doc_col,
        docs,
        qkv,
        mixed_own,
        lse,
        specs={0: SMEM},
        scratch=[
            pltpu.VMEM((group, seq_len), bf16),
            pltpu.VMEM((group, tok_rows), f32),
            pltpu.VMEM((seq_len, group), f32),
            pltpu.VMEM((seq_len, group), f32),
            pltpu.VMEM((8, tok_rows), f32),
        ],
        limit=48,
        cost=17,
    )
    from_x, from_y = over_x(to_x), over_y(to_y)
    (qkv_part,) = call(
        functools.partial(qkv_grad_kernel, group, extra),
        [((width, columns), f32)],
        place,
        after(attn_in, proj_part),
        grad_qkv_b,
        first_sums,
        mid_sums,
        grad_centroid,
        specs={0: SMEM},
        cost=2,
    )
    qkv_part = own_parity(qkv_part.reshape(REPS, n_z, 2, shard, columns))
    qkv_part = scatter_z(qkv_part.transpose(1, 0, 2, 3)).astype(bf16)
    from_x, from_y = after((from_x, from_y), qkv_part)
    upper = over_y((left_y + from_x[:half].astype(f32)).astype(bf16))
    lower = over_x((left_x + from_y[:half].astype(f32)).astype(bf16))
    (grad_tokens,) = call(
        tokens_grad_kernel,
        [((tok_rows, width), bf16)],
        own_attn,
        from_x,
        from_y,
        upper,
        lower,
        own_tokens,
        params,
        grad_hidden,
        cost=2,
    )

    got = exchange(jnp.concatenate([qkv_part, proj_part], axis=2), "rep").astype(f32)
    returned = travel(after(answer, got))
    block_out = (hidden + product(table_t, returned)).astype(bf16)
    small_sum = jnp.sum(got[:, :, 3 * group : 3 * group + extra], axis=0)
    big = got[:, :, : 3 * group].reshape(REPS, shard, 3, group)
    grad_qkv = big.transpose(1, 2, 0, 3).reshape(shard, 3 * width)
    grad_proj = jnp.sum(got[:, :, columns:], axis=0)
    grad_w_in, grad_w_out = layer_of(0, grads0, *layer_of(1, grads1))
    return (
        block_out[None],
        grad_tokens[None],
        small_sum[:, 0:2],
        small_sum[:, 2:4],
        grad_qkv,
        grad_proj,
        small_sum[:, 4:],
        grad_w_in,
        grad_w_out,
    )


def solution(mesh):
    in_specs = (
        P("exp", "rep", None),
        P("exp", None),
        P("exp", "rep", None),
        P(("rep", "exp"), None),
        P(("rep", "exp"), None),
        P(("rep", "exp"), None),
        P(("rep", "exp"), None),
        P(("rep", "exp"), None),
        P("exp", None, None, "rep"),
        P("exp", None, None, "rep"),
        P("exp", "rep", None),
    )
    out_specs = (
        P("exp", "rep", None),
        P("exp", "rep", None),
        P(("rep", "exp"), None),
        P(("rep", "exp"), None),
        P(("rep", "exp"), None),
        P(("rep", "exp"), None),
        P(("rep", "exp"), None),
        P("exp", None, None, "rep"),
        P("exp", None, None, "rep"),
    )
    return jax.shard_map(local, mesh=mesh, in_specs=in_specs, out_specs=out_specs, check_vma=False)
```
